256 devices in a mesh: grp: 2 (over z_lo), gx: 32 (over x, y, core), gy: 4 (over z_hi).
Axes of the slice: x: 4, y: 4, z: 8 (z_hi: 4, z_lo: 2; z = z_hi * 2 + z_lo), core: 2. Of those that a mesh axis runs over, the one named last changes fastest.
Arguments:
- velocity: float32 [3, 256, 128, 256], P(None, 'gx', 'gy', 'grp'), may hold values from -6 to 6
- viscosity: float32 [256, 128, 256], P('gx', 'gy', 'grp'), may hold values from 0.02 to 0.15
- selection: int32 [2, 32, 4, 96], P('grp', 'gx', 'gy'), may hold values from 0 to 255
- w_in: bfloat16 [384, 1024], replicated, may hold values from -0.3125 to 0.3125
- w_up: bfloat16 [1024, 4096], P(None, 'gy'), may hold values from -0.1875 to 0.1875
- w_down: bfloat16 [4096, 1024], P('gy'), may hold values from -0.09375 to 0.09375
- w_out: bfloat16 [1024, 384], replicated, may hold values from -0.1875 to 0.1875
Outputs:
- velocity_next: float32 [3, 256, 128, 256], P(None, 'gx', 'gy', 'grp')
- pressure: float32 [256, 128, 256], P('gx', 'gy', 'grp')
- grad_in: float32 [384, 1024], P(None, ('grp', 'gx', 'gy'))
- grad_up: float32 [1024, 4096], P(('grp', 'gx'), 'gy')
- grad_down: float32 [4096, 1024], P('gy', ('grp', 'gx'))
- grad_out: float32 [1024, 384], P(('grp', 'gx', 'gy'))
The draws below stay inside these ranges and needn't reach their ends.
Inputs may be any that keep to these rules, and one draw needn't show every extreme that they name: `selection`: each entry numbers a patch of the device's own block.
All inputs are finite; a program needn't handle non-finite values.
Results may differ from the reference program's by a relative error of at most 0.0055.
Values may be sent and summed in bfloat16 or wider, within the bound.
A program may use at most 128 MiB of HBM per device.

```python
import math
import jax
import jax.numpy as jnp
from jax import lax

CX = 8
CY = 32
CZ = 128
PX = 4
PY = 4
PZ = 8
ITERS = 6
TSEL = 96
D = 1024
FF = 4096
F = 384
PATCHES = 256
NX = 256
NY = 128
NZ = 256
ALL_ROWS = 24576
N_GRP = 2
N_GX = 32
N_GY = 4


def set_ends(array, own_key, least, largest):
    longest = array.shape.index(max(array.shape))
    spots = []
    for shift in (0, 1):
        where = [jax.random.randint(jax.random.fold_in(own_key, axis), (), 0, length) for axis, length in enumerate(array.shape)]
        where[longest] = (where[longest] + shift) % array.shape[longest]
        spots.append(tuple(where))
    return array.at[spots[0]].set(least).at[spots[1]].set(largest)


def block_levels(stream_key, dims, shards, least, largest):
    loudness = 1.0
    for axis_at, parts in shards:
        draws = jax.random.uniform(jax.random.fold_in(jax.random.fold_in(stream_key, 6), axis_at), (parts,), jnp.float32, least / len(shards), largest / len(shards))
        loudness = loudness * jnp.repeat(jnp.exp(draws), dims[axis_at] // parts).reshape((-1,) + (1,) * (len(dims) - 1 - axis_at))
    return loudness


def noise(key, extent, scale, limit, cuts=(), dtype=jnp.bfloat16):
    level = block_levels(key, extent, cuts, -0.22, 0.18) if cuts else 1.0
    drawn = jax.random.normal(key, extent, jnp.float32) * scale * level
    return jnp.minimum(jnp.maximum(drawn, -limit), limit).astype(dtype)


def setup_inputs(seed: int = 0) -> dict:
    keys = jax.random.split(jax.random.key(seed), 8)
    return {
        "velocity": noise(keys[0], (3, NX, NY, NZ), 1.0, 6.0, ((1, 32), (2, 4), (3, 2)), jnp.float32),
        "viscosity": jnp.clip(jnp.exp(math.log(0.15) - 2.014903 * jax.random.uniform(keys[1], (NX, NY, NZ), jnp.float32) ** block_levels(keys[1], (NX, NY, NZ), ((0, 32), (1, 4), (2, 2)), -0.2, 0.2)), 0.02, 0.15),
        "selection": set_ends(jax.random.randint(keys[2], (N_GRP, N_GX, N_GY, TSEL), 0, PATCHES), jax.random.fold_in(keys[2], 1), 0, PATCHES - 1).astype(jnp.int32),
        "w_in": noise(keys[3], (F, D), F ** -0.5, 0.3125),
        "w_up": noise(keys[4], (D, FF), D ** -0.5, 0.1875, ((1, 4),)),
        "w_down": noise(keys[5], (FF, D), FF ** -0.5, 0.09375, ((0, 4),)),
        "w_out": noise(keys[6], (D, F), D ** -0.5, 0.1875),
    }


def widen(field_in):
    return jnp.pad(field_in, ((0, 0), (1, 1), (1, 1), (1, 1)))


def beside_all(padded):
    total = padded[:, 2:, 1:-1, 1:-1] + padded[:, :-2, 1:-1, 1:-1]
    total = total + padded[:, 1:-1, 2:, 1:-1] + padded[:, 1:-1, :-2, 1:-1]
    return total + padded[:, 1:-1, 1:-1, 2:] + padded[:, 1:-1, 1:-1, :-2]


def divergence(padded):
    along_x = padded[0, 2:, 1:-1, 1:-1] - padded[0, :-2, 1:-1, 1:-1]
    along_y = padded[1, 1:-1, 2:, 1:-1] - padded[1, 1:-1, :-2, 1:-1]
    along_z = padded[2, 1:-1, 1:-1, 2:] - padded[2, 1:-1, 1:-1, :-2]
    return (0.5 * (along_x + along_y + along_z))[None]


def slopes(padded):
    along_x = padded[0, 2:, 1:-1, 1:-1] - padded[0, :-2, 1:-1, 1:-1]
    along_y = padded[0, 1:-1, 2:, 1:-1] - padded[0, 1:-1, :-2, 1:-1]
    along_z = padded[0, 1:-1, 1:-1, 2:] - padded[0, 1:-1, 1:-1, :-2]
    return 0.5 * jnp.stack([along_x, along_y, along_z])


def silu_slope(raised):
    sigmoid_raised = jax.nn.sigmoid(raised)
    return sigmoid_raised * (1.0 + raised * (1.0 - sigmoid_raised))


def all_patches(field_in):
    reshaped = field_in.reshape(3, N_GX, CX // PX, PX, N_GY, CY // PY, PY, N_GRP, CZ // PZ, PZ)
    reordered = reshaped.transpose(7, 1, 4, 2, 5, 8, 0, 3, 6, 9)
    return reordered.reshape(N_GRP, N_GX, N_GY, PATCHES, F)


def train_terms(rows_pair, w_in, w_up, w_down, w_out, loss_scale):
    inputs, targets = rows_pair
    lifted = jnp.dot(inputs, w_in, preferred_element_type=jnp.float32)
    lifted_b = lifted.astype(jnp.bfloat16)
    raised = jnp.dot(lifted_b, w_up, preferred_element_type=jnp.float32)
    active = jax.nn.silu(raised).astype(jnp.bfloat16)
    mixed_sum = lifted + jnp.dot(active, w_down, preferred_element_type=jnp.float32)
    mixed_b = mixed_sum.astype(jnp.bfloat16)
    predicted = jnp.dot(mixed_b, w_out, preferred_element_type=jnp.float32)
    residual_error = ((predicted - targets.astype(jnp.float32)) * loss_scale).astype(jnp.bfloat16)
    back_mixed = jnp.dot(residual_error, w_out.T, preferred_element_type=jnp.float32)
    back_b = back_mixed.astype(jnp.bfloat16)
    back_active = jnp.dot(back_b, w_down.T, preferred_element_type=jnp.float32)
    back_raised = (back_active * silu_slope(raised)).astype(jnp.bfloat16)
    back_lift = back_mixed + jnp.dot(back_raised, w_up.T, preferred_element_type=jnp.float32)
    back_lift_b = back_lift.astype(jnp.bfloat16)
    return (jnp.dot(inputs.T, back_lift_b, preferred_element_type=jnp.float32),
            jnp.dot(lifted_b.T, back_raised, preferred_element_type=jnp.float32),
            jnp.dot(active.T, back_b, preferred_element_type=jnp.float32),
            jnp.dot(mixed_b.T, residual_error, preferred_element_type=jnp.float32))


def reference(velocity, viscosity, selection, w_in, w_up, w_down, w_out):
    provisional = velocity + viscosity[None] * (beside_all(widen(velocity)) - 6.0 * velocity)
    source = divergence(widen(provisional))
    pressure = jnp.zeros(source.shape, jnp.float32)
    for repeat in range(ITERS):
        pressure = (beside_all(widen(pressure)) - source) / 6.0
    velocity_next = provisional - slopes(widen(pressure))
    chosen = jnp.broadcast_to(selection[..., None], (N_GRP, N_GX, N_GY, TSEL, F))
    inputs = jnp.take_along_axis(all_patches(velocity), chosen, axis=3).astype(jnp.bfloat16)
    targets = jnp.take_along_axis(all_patches(velocity_next), chosen, axis=3).astype(jnp.bfloat16)
    inputs = inputs.reshape(N_GRP * N_GX, N_GY * TSEL, F)
    targets = targets.reshape(N_GRP * N_GX, N_GY * TSEL, F)
    loss_scale = float(ALL_ROWS) ** -0.5

    def group_step(totals, rows_pair):
        terms = train_terms(rows_pair, w_in, w_up, w_down, w_out, loss_scale)
        return tuple(a + b for a, b in zip(totals, terms)), None

    initial = (jnp.zeros((F, D), jnp.float32), jnp.zeros((D, FF), jnp.float32),
               jnp.zeros((FF, D), jnp.float32), jnp.zeros((D, F), jnp.float32))
    gradients, unused = lax.scan(group_step, initial, (inputs, targets))
    return (velocity_next, pressure[0], gradients[0], gradients[1], gradients[2], gradients[3])
```

```python
import jax
import jax.numpy as jnp
from jax import lax
from jax.experimental import pallas as pl
from jax.experimental.pallas import tpu as pltpu
from jax.sharding import PartitionSpec as P

F32 = jnp.float32
BF16 = jnp.bfloat16
MESH = pl.DeviceIdType.MESH
MIB = 1 << 20

FACES = [(1, 0), (-1, 0), (0, 1), (0, -1)]
DIAGONALS = [(1, 1), (1, -1), (-1, 1), (-1, -1)]
PLANE = FACES + DIAGONALS
CROSS_ONE = [(0, 0)] + FACES
CROSS_TWO = [(0, 0)] + PLANE


def place():
    return lax.axis_index("grp"), lax.axis_index("gx"), lax.axis_index("gy")


def push(src, dst, sems, slot, target):
    return pltpu.make_async_remote_copy(
        src_ref=src,
        dst_ref=dst,
        send_sem=sems.at[0, slot],
        recv_sem=sems.at[1, slot],
        device_id=target,
        device_id_type=MESH,
    )


def greet(targets):
    barrier = pltpu.get_barrier_semaphore()
    for target in targets:
        pl.semaphore_signal(barrier, inc=1, device_id=target, device_id_type=MESH)
    pl.semaphore_wait(barrier, len(targets))


def matmul(a, b):
    return jnp.dot(a, b, preferred_element_type=F32)


def matmul_nt(a, b):
    return lax.dot_general(a, b, (((1,), (1,)), ((), ())), preferred_element_type=F32)


def matmul_tn(a, b):
    return lax.dot_general(a, b, (((0,), (0,)), ((), ())), preferred_element_type=F32)


def iota(shape, dim):
    return lax.broadcasted_iota(jnp.int32, shape, dim)


def offset(here, dx, dy, flip):
    g, i, k = here
    return (1 - g if flip else g, lax.rem(i + dx + 32, 32), lax.rem(k + dy + 4, 4))


def stencil_targets(here):
    return [offset(here, dx, dy, False) for dx, dy in PLANE] + [
        offset(here, dx, dy, True) for dx, dy in CROSS_TWO
    ]


def pack_edge(g, group):
    lane = iota((16, 128), 1) // 8
    packed = jnp.zeros((16, 128), F32)
    for part in range(16):
        rows = group(part)
        rows = jnp.where(g == 0, pltpu.roll(rows, 8, 1), rows)
        moved = rows if part == 0 else pltpu.roll(rows, 8 * part, 1)
        packed = jnp.where(lane == part, moved, packed)
    return packed


def unpack_edge(g, packed, part):
    lane = iota((16, 128), 1)
    rows = packed if part == 0 else pltpu.roll(packed, 128 - 8 * part, 1)
    rows = jnp.where(lane < 8, rows, 0.0)
    return jnp.where(g == 0, rows, pltpu.roll(rows, 120, 1))


def unpack_block(g, packed, dx, dy, deep, store):
    planes = range(8) if dx == 0 else (range(8 - deep, 8) if dx < 0 else range(deep))
    for x in planes:
        to = deep + x if dx == 0 else (x - (8 - deep) if dx < 0 else deep + 8 + x)
        if dy == 0:
            store(to, 8, unpack_edge(g, packed, 2 * x))
            store(to, 24, unpack_edge(g, packed, 2 * x + 1))
        elif dy < 0:
            store(to, 0, unpack_edge(g, packed, 2 * x + 1)[8:16])
        else:
            store(to, 40, unpack_edge(g, packed, 2 * x)[0:8])


def along_z(low, high):
    lane = iota(low.shape, 1)
    low_r, high_r = pltpu.roll(low, 127, 1), pltpu.roll(high, 127, 1)
    low_l, high_l = pltpu.roll(low, 1, 1), pltpu.roll(high, 1, 1)
    right = (jnp.where(lane == 127, high_r, low_r), jnp.where(lane == 127, 0.0, high_r))
    left = (jnp.where(lane == 0, 0.0, low_l), jnp.where(lane == 0, low_l, high_l))
    return right, left


def own_slices(dx, dy, deep, rows):
    xs = slice(0, 8) if dx == 0 else (slice(8 - deep, 8) if dx > 0 else slice(0, deep))
    ys = slice(0, 32) if dy == 0 else (slice(32 - rows, 32) if dy > 0 else slice(0, rows))
    return xs, ys


class Stencil:
    scratch = [
        pltpu.VMEM((4, 8, 32, 128), F32),
        pltpu.VMEM((2, 4, 8, 2, 128), F32),
        pltpu.VMEM((2, 4, 8, 2, 128), F32),
        pltpu.VMEM((4, 4, 2, 2, 128), F32),
        pltpu.VMEM((4, 16, 128), F32),
        pltpu.VMEM((5, 4, 16, 128), F32),
        pltpu.VMEM((4, 2, 12, 48, 128), F32),
        pltpu.VMEM((3, 2, 12, 48, 128), F32),
        pltpu.VMEM((8, 32, 128), F32),
        pltpu.VMEM((16, 128), F32),
        pltpu.VMEM((9, 16, 128), F32),
        pltpu.VMEM((2, 20, 48, 128), F32),
        pltpu.VMEM((2, 20, 48, 128), F32),
        pltpu.VMEM((2, 20, 48, 128), F32),
        pltpu.SemaphoreType.DMA((2, 13)),
        pltpu.SemaphoreType.DMA((2, 17)),
    ]

    def __init__(self, here, velocity, viscosity, velocity_next, pressure, refs):
        self.here = here
        self.velocity, self.viscosity = velocity, viscosity
        self.velocity_next, self.pressure = velocity_next, pressure
        (
            self.fields, self.y_send, self.y_recv, self.d_recv, self.z_send, self.z_recv,
            self.wide, self.prov, self.source, self.sz_send, self.sz_recv, self.swide,
            self.p_a, self.p_b, self.sems_one, self.sems_two,
        ) = refs

    def prepare(self):
        g = self.here[0]
        self.fields[0:3] = self.velocity[...]
        self.fields[3] = self.viscosity[...]
        self.y_send[0] = self.fields[:, :, 30:32, :]
        self.y_send[1] = self.fields[:, :, 0:2, :]
        for f in range(4):
            self.z_send[f] = pack_edge(
                g, lambda part: self.fields[f, part // 2, 16 * (part % 2) : 16 * (part % 2) + 16, :]
            )

    def send_one(self):
        g = self.here[0]
        copies = []
        for dx, dy in PLANE:
            slot = len(copies)
            target = offset(self.here, dx, dy, False)
            xs, _ = own_slices(dx, dy, 2, 2)
            if dy == 0:
                x_to = 0 if dx > 0 else 10
                src = self.fields.at[:, xs]
                dst = self.wide.at[:, g, x_to : x_to + 2, 8:40, :]
            elif dx == 0:
                edge = 0 if dy > 0 else 1
                src, dst = self.y_send.at[edge], self.y_recv.at[edge]
            else:
                edge = 0 if dy > 0 else 1
                src, dst = self.y_send.at[edge, :, xs], self.d_recv.at[slot - 4]
            copies.append(push(src, dst, self.sems_one, slot, target))
        for n, (dx, dy) in enumerate(CROSS_ONE):
            target = offset(self.here, dx, dy, True)
            copies.append(push(self.z_send, self.z_recv.at[n], self.sems_one, len(copies), target))
        for copy in copies:
            copy.start()
        self.copies_one = copies

    def make_source(self):
        g, i, k = self.here
        wide = self.wide
        wide[:, g, 2:10, 8:40, :] = self.fields[...]
        for copy in self.copies_one:
            copy.wait_recv()
        wide[:, g, 2:10, 6:8, :] = self.y_recv[0]
        wide[:, g, 2:10, 40:42, :] = self.y_recv[1]
        for n, (dx, dy) in enumerate(DIAGONALS):
            x_to, y_to = (0 if dx > 0 else 10), (6 if dy > 0 else 40)
            wide[:, g, x_to : x_to + 2, y_to : y_to + 2, :] = self.d_recv[n]
        for n, (dx, dy) in enumerate(CROSS_ONE):
            for f in range(4):

                def store(to, row, rows, f=f):
                    wide[f, 1 - g, to, row : row + rows.shape[0], :] = rows

                unpack_block(g, self.z_recv[n, f], -dx, -dy, 2, store)

        @pl.when(i == 0)
        def _():
            wide[:, :, 0:2] = jnp.zeros((4, 2, 2, 48, 128), F32)

        @pl.when(i == 31)
        def _():
            wide[:, :, 10:12] = jnp.zeros((4, 2, 2, 48, 128), F32)

        @pl.when(k == 0)
        def _():
            wide[:, :, :, 0:8, :] = jnp.zeros((4, 2, 12, 8, 128), F32)

        @pl.when(k == 3)
        def _():
            wide[:, :, :, 40:48, :] = jnp.zeros((4, 2, 12, 8, 128), F32)

        def provisional(x, carry):
            for c in range(3):
                mid = (wide[c, 0, x], wide[c, 1, x])
                right, left = along_z(*mid)
                for t in range(2):
                    total = wide[c, t, x + 1] + wide[c, t, x - 1]
                    total = total + pltpu.roll(mid[t], 47, 0) + pltpu.roll(mid[t], 1, 0)
                    total = total + right[t] + left[t]
                    self.prov[c, t, x] = mid[t] + wide[3, t, x] * (total - 6.0 * mid[t])
            return carry

        lax.fori_loop(1, 11, provisional, 0)
        prov = self.prov

        def source(x, carry):
            right, left = along_z(prov[2, 0, x, 8:40, :], prov[2, 1, x, 8:40, :])
            slope = jnp.where(g == 0, right[0] - left[0], right[1] - left[1])
            slope = slope + prov[0, g, x + 1, 8:40, :] - prov[0, g, x - 1, 8:40, :]
            slope = slope + prov[1, g, x, 9:41, :] - prov[1, g, x, 7:39, :]
            self.source[x - 2] = 0.5 * slope
            return carry

        lax.fori_loop(2, 10, source, 0)
        self.sz_send[...] = pack_edge(
            g, lambda part: self.source[part // 2, 16 * (part % 2) : 16 * (part % 2) + 16, :]
        )

    def send_two(self):
        g = self.here[0]
        copies = []
        for dx, dy in PLANE:
            target = offset(self.here, dx, dy, False)
            xs, ys = own_slices(dx, dy, 6, 8)
            x_to = 6 if dx == 0 else (0 if dx > 0 else 14)
            y_to = 8 if dy == 0 else (0 if dy > 0 else 40)
            dst = self.swide.at[
                g, x_to : x_to + xs.stop - xs.start, y_to : y_to + ys.stop - ys.start, :
            ]
            copies.append(push(self.source.at[xs, ys, :], dst, self.sems_two, len(copies), target))
        for n, (dx, dy) in enumerate(CROSS_TWO):
            target = offset(self.here, dx, dy, True)
            copies.append(push(self.sz_send, self.sz_recv.at[n], self.sems_two, len(copies), target))
        for copy in copies:
            copy.start()
        self.copies_two = copies

    def solve(self):
        g, i, k = self.here
        swide = self.swide
        swide[g, 6:14, 8:40, :] = self.source[...]
        for copy in self.copies_two:
            copy.wait_recv()
        for n, (dx, dy) in enumerate(CROSS_TWO):

            def store(to, row, rows):
                swide[1 - g, to, row : row + rows.shape[0], :] = rows

            unpack_block(g, self.sz_recv[n], -dx, -dy, 6, store)
        row = iota((48, 128), 0)
        outside = ((k == 0) & (row < 8)) | ((k == 3) & (row >= 40))
        sixth = jnp.where(outside, 0.0, 1.0 / 6.0).astype(F32)

        def inside(x):
            out = ((i == 0) & (x < 6)) | ((i == 31) & (x >= 14))
            return sixth * jnp.where(out, 0.0, 1.0).astype(F32)

        def first(x, carry):
            scale = inside(x)
            for t in range(2):
                self.p_a[t, x] = -swide[t, x] * scale
            return carry

        lax.fori_loop(0, 20, first, 0)
        old, new = self.p_a, self.p_b
        for sweep in range(1, 6):

            def relax(x, carry, old=old, new=new):
                scale = inside(x)
                mid = (old[0, x], old[1, x])
                right, left = along_z(*mid)
                for t in range(2):
                    total = old[t, x + 1] + old[t, x - 1]
                    total = total + pltpu.roll(mid[t], 47, 0) + pltpu.roll(mid[t], 1, 0)
                    total = total + right[t] + left[t]
                    new[t, x] = (total - swide[t, x]) * scale
                return carry

            lax.fori_loop(sweep, 20 - sweep, relax, 0)
            old, new = new, old
        p, prov = old, self.prov

        def project(x, carry):
            at = x + 6
            right, left = along_z(p[0, at, 8:40, :], p[1, at, 8:40, :])
            slope_z = jnp.where(g == 0, right[0] - left[0], right[1] - left[1])
            slope_x = p[g, at + 1, 8:40, :] - p[g, at - 1, 8:40, :]
            slope_y = p[g, at, 9:41, :] - p[g, at, 7:39, :]
            for c, slope in enumerate((slope_x, slope_y, slope_z)):
                self.velocity_next[c, x] = prov[c, g, x + 2, 8:40, :] - 0.5 * slope
            self.pressure[x] = p[g, at, 8:40, :]
            return carry

        lax.fori_loop(0, 8, project, 0)

    def finish(self):
        for copy in self.copies_one + self.copies_two:
            copy.wait_send()


PATCH_SCRATCH = [pltpu.VMEM((16, 6144), F32), pltpu.VMEM((2048, 128), BF16)]


def make_fold(fold):
    row, col = iota((2048, 128), 0), iota((2048, 128), 1)
    hit = (row // 128 == col // 8) & (row % 8 == col % 8)
    fold[...] = hit.astype(F32).astype(BF16)


def pick_patches(field, selection, lines, fold, out):
    for c in range(3):
        for x in range(8):
            for py in range(4):
                combo = (c * 4 + x % 4) * 4 + py
                row = 8 * (x // 4)
                lines[row : row + 8, 128 * combo : 128 * combo + 128] = field[
                    c, x, pl.ds(py, 8, stride=4), :
                ]
    chosen = selection[...]
    line = (jnp.broadcast_to(chosen >> 4, (96, 16)) == iota((96, 16), 1)).astype(F32).astype(BF16)
    lane = (iota((96, 2048), 1) & 127) >> 3
    here = lane == jnp.broadcast_to(chosen & 15, (96, 2048))
    for part in range(3):
        source = lines[:, 2048 * part : 2048 * part + 2048].astype(BF16)
        rows = jnp.where(here, matmul(line, source), 0.0).astype(BF16)
        out[:, 128 * part : 128 * part + 128] = matmul(rows, fold[...]).astype(BF16)


def stencil_kernel(velocity, viscosity, selection, velocity_next, pressure, inputs, targets, *refs):
    here = place()
    lines, fold = refs[:2]
    step = Stencil(here, velocity, viscosity, velocity_next, pressure, refs[2:])
    step.prepare()
    greet(stencil_targets(here))
    step.send_one()
    make_fold(fold)
    pick_patches(velocity, selection, lines, fold, inputs)
    step.make_source()
    step.send_two()
    step.solve()
    pick_patches(velocity_next, selection, lines, fold, targets)
    step.finish()


def trainer_targets(here):
    g, i, k = here
    x, y, c = lax.div(i, 8), lax.rem(lax.div(i, 2), 4), lax.rem(i, 2)
    out = [(g, i, lax.rem(k + d, 4)) for d in (1, 2, 3)]
    out += [(g, lax.rem(x + d, 4) * 8 + y * 2 + c, k) for d in (1, 2, 3)]
    out += [(g, x * 8 + lax.rem(y + d, 4) * 2 + c, k) for d in (1, 2, 3)]
    return out + [(g, x * 8 + y * 2 + 1 - c, k), (1 - g, i, k)]


class Scatter:
    @staticmethod
    def scratch(rows, width, wire):
        return [
            pltpu.VMEM((2, 4, 4, 2, rows, width), F32),
            pltpu.VMEM((2, 4, 4, rows, width), F32),
            pltpu.VMEM((4, 2, 4, rows, width), wire),
            pltpu.VMEM((4, 2, 4, rows, width), wire),
            pltpu.VMEM((2, 4, rows, width), F32),
            pltpu.VMEM((4, 2, rows, width), F32),
            pltpu.VMEM((2, rows, width), F32),
            pltpu.VMEM((rows, width), F32),
            pltpu.SemaphoreType.DMA((2, 8)),
            pltpu.SemaphoreType.DMA((2, 4)),
            pltpu.SemaphoreType.DMA((2, 4)),
            pltpu.SemaphoreType.DMA((2, 1)),
        ]

    def __init__(self, here, refs, wire, x_first):
        g, i, k = here
        self.here, self.wire, self.x_first = here, wire, x_first
        self.x, self.y, self.c = lax.div(i, 8), lax.rem(lax.div(i, 2), 4), lax.rem(i, 2)
        (
            self.parts, self.core_recv, self.one_send, self.one_recv, self.one_sum,
            self.two_recv, self.two_sum, self.three_recv,
            self.core_sems, self.one_sems, self.two_sems, self.three_sems,
        ) = refs

    def along(self, on_x, d):
        g, i, k = self.here
        x, y = self.x, self.y
        if on_x:
            x = lax.rem(x + d, 4)
        else:
            y = lax.rem(y + d, 4)
        return (g, x * 8 + y * 2 + self.c, k)

    def core_copy(self, chunk):
        g, i, k = self.here
        half, x = lax.div(chunk, 4), lax.rem(chunk, 4)
        return push(
            self.parts.at[half, x, :, 1 - self.c],
            self.core_recv.at[half, x],
            self.core_sems,
            chunk,
            (g, self.x * 8 + self.y * 2 + 1 - self.c, k),
        )

    def start_core(self, chunk):
        self.core_copy(jnp.int32(chunk)).start()

    def wait_core(self):
        for chunk in range(8):
            self.core_copy(jnp.int32(chunk)).wait_recv()

    def first(self):
        mine = self.x if self.x_first else self.y
        self.one = []
        for d in (2, 1, 3, 0):
            to = lax.rem(mine + d, 4)
            if self.x_first:
                total = self.parts[:, to, :, self.c] + self.core_recv[:, to]
            else:
                total = self.parts[:, :, to, self.c] + self.core_recv[:, :, to]
            if d == 0:
                self.one_sum[...] = total
            else:
                self.one_send[d] = total.astype(self.wire)
                copy = push(
                    self.one_send.at[d], self.one_recv.at[d], self.one_sems, d,
                    self.along(self.x_first, d),
                )
                copy.start()
                self.one.append(copy)

    def second(self):
        for copy in self.one:
            copy.wait_recv()
        total = self.one_sum[...]
        for d in (1, 2, 3):
            total = total + self.one_recv[d].astype(F32)
        self.one_sum[...] = total
        mine = self.y if self.x_first else self.x
        self.two = []
        for d in (2, 1, 3):
            copy = push(
                self.one_sum.at[:, lax.rem(mine + d, 4)], self.two_recv.at[d], self.two_sems, d,
                self.along(not self.x_first, d),
            )
            copy.start()
            self.two.append(copy)

    def third(self):
        g, i, k = self.here
        mine = self.y if self.x_first else self.x
        for copy in self.two:
            copy.wait_recv()
        self.two_sum[...] = (
            self.one_sum[:, mine] + self.two_recv[1] + self.two_recv[2] + self.two_recv[3]
        )
        self.three = push(
            self.two_sum.at[1 - g], self.three_recv, self.three_sems, 0, (1 - g, i, k)
        )
        self.three.start()

    def result(self):
        self.three.wait_recv()
        return self.two_sum[self.here[0]] + self.three_recv[...]

    def finish(self):
        for chunk in range(8):
            self.core_copy(jnp.int32(chunk)).wait_send()
        for copy in self.one + self.two + [self.three]:
            copy.wait_send()


N_SCATTER = 12
TRAINER_SCRATCH = [
    pltpu.VMEM((4, 96, 384), BF16),
    pltpu.VMEM((4, 96, 384), BF16),
    pltpu.VMEM((384, 1024), BF16),
    pltpu.VMEM((384, 1024), F32),
    pltpu.VMEM((384, 1024), BF16),
    pltpu.VMEM((4, 96, 1024), BF16),
    pltpu.VMEM((4, 96, 1024), BF16),
    pltpu.VMEM((384, 1024), BF16),
    pltpu.VMEM((384, 1024), BF16),
    pltpu.VMEM((4, 1024, 256), BF16),
    pltpu.VMEM((4, 96, 256), BF16),
    pltpu.VMEM((4, 96, 256), BF16),
    pltpu.VMEM((4, 384, 256), BF16),
    pltpu.VMEM((4, 384, 256), BF16),
    pltpu.VMEM((4, 256, 1024), BF16),
    pltpu.SemaphoreType.DMA((2, 4)),
    pltpu.SemaphoreType.DMA((2, 4)),
    pltpu.SemaphoreType.DMA((2, 4)),
    pltpu.SemaphoreType.DMA((2, 4)),
    pltpu.SemaphoreType.DMA((2, 4)),
]
TRAINER_SCRATCH += Scatter.scratch(16, 1024, BF16) + Scatter.scratch(16, 1024, BF16)
TRAINER_SCRATCH += Scatter.scratch(8, 384, F32)


def columns(n):
    return pl.ds(pl.multiple_of(n * 256, 256), 256)


def trainer_kernel(
    inputs, targets, w_in, w_up, w_down, w_out, out_up, out_down, out_small, *refs
):
    here = place()
    g, i, k = here
    (
        in_all, err_all, lifted_b, slope, active, down_send, down_recv, back_b, back_raised,
        order, mix_send, mix_recv, lift_send, lift_recv, up_order,
        in_sems, down_sems, err_sems, mix_sems, lift_sems,
    ) = refs[:20]
    rest = refs[20:]
    up = Scatter(here, rest[:N_SCATTER], BF16, True)
    down = Scatter(here, rest[N_SCATTER : 2 * N_SCATTER], BF16, False)
    small = Scatter(here, rest[2 * N_SCATTER :], F32, True)
    sent = []

    def peer(d):
        return (g, i, lax.rem(k + d, 4))

    def start(copies):
        for copy in copies:
            copy.start()
        sent.extend(copies)
        return copies

    in_all[k] = inputs[...]
    greet(trainer_targets(here))
    in_copies = start(
        [push(in_all.at[k], in_all.at[k], in_sems, d, peer(d)) for d in (2, 1, 3)]
    )
    row, col = iota((1024, 256), 0), iota((1024, 256), 1)
    for j in range(4):
        wanted = (col >> 2) * 16 + j * 4 + (col & 3)
        order[j] = (row == wanted).astype(F32).astype(BF16)
        up_order[j] = matmul_tn(order[j], w_up[...]).astype(BF16)
    w_out_k = matmul_tn(order[k], w_out[...]).astype(BF16)
    own_lift = matmul(inputs[...], w_in[...])
    for copy in in_copies:
        copy.wait_recv()

    rows_in = in_all[...].reshape(384, 384)

    def lift(n, carry):
        at = columns(n)
        lifted_b[:, at] = matmul(rows_in, w_in[:, at]).astype(BF16)
        return carry

    lax.fori_loop(0, 4, lift, 0)

    def raise_(n, carry):
        at = columns(n)
        raised = matmul(lifted_b[...], w_up[:, at])
        sigmoid = jax.nn.sigmoid(raised)
        active[:, at] = (raised * sigmoid).astype(BF16)
        slope[:, at] = sigmoid * (1.0 + raised * (1.0 - sigmoid))
        return carry

    lax.fori_loop(0, 4, raise_, 0)
    down_copies = []
    for d in (2, 1, 3):
        to = lax.rem(k + d, 4)
        rows = active[pl.ds(pl.multiple_of(to * 96, 32), 96), :]
        down_send[d] = matmul(rows, w_down[...]).astype(BF16)
        down_copies += start([push(down_send.at[d], down_recv.at[d], down_sems, d, peer(d))])
    mixed = own_lift + matmul(active[pl.ds(pl.multiple_of(k * 96, 32), 96), :], w_down[...])
    for copy in down_copies:
        copy.wait_recv()
    for d in (1, 2, 3):
        mixed = mixed + down_recv[d].astype(F32)
    mixed_b = mixed.astype(BF16)
    predicted = matmul(mixed_b, w_out[...])
    scale = float(24576) ** (-0.5)
    err_all[k] = ((predicted - targets[...].astype(F32)) * scale).astype(BF16)
    err_copies = start(
        [push(err_all.at[k], err_all.at[k], err_sems, d, peer(d)) for d in (2, 1, 3)]
    )
    mix_copies = []
    for d in (2, 1, 3, 0):
        part = matmul(mixed_b, order[lax.rem(k + d, 4)]).astype(BF16)
        if d:
            mix_send[d] = part
            mix_copies += start([push(mix_send.at[d], mix_recv.at[k], mix_sems, d, peer(d))])
        else:
            mix_recv[k] = part
    for copy in err_copies:
        copy.wait_recv()
    errors = err_all[...].reshape(384, 384)

    def back(n, carry):
        at = columns(n)
        back_b[:, at] = matmul_nt(errors, w_out[at, :]).astype(BF16)
        return carry

    lax.fori_loop(0, 4, back, 0)

    def back_up(n, carry):
        at = columns(n)
        back_raised[:, at] = (matmul_nt(back_b[...], w_down[at, :]) * slope[:, at]).astype(BF16)
        return carry

    lax.fori_loop(0, 4, back_up, 0)
    lift_copies = []
    for d in (2, 1, 3, 0):
        part = matmul_nt(back_raised[...], up_order[lax.rem(k + d, 4)])
        if d:
            lift_send[d] = part.astype(BF16)
            lift_copies += start([push(lift_send.at[d], lift_recv.at[d], lift_sems, d, peer(d))])
        else:
            lift_sum = part + matmul_nt(errors, w_out_k)

    def grad_down(n, carry):
        at = pl.ds(pl.multiple_of(n * 128, 128), 128)
        block = matmul_tn(back_b[:, at], active[...])
        down.parts[lax.div(n, 4), lax.rem(n, 4)] = block.reshape(4, 2, 16, 1024)
        down.start_core(n)
        return carry

    lax.fori_loop(0, 8, grad_down, 0)

    def grad_up(n, carry):
        at = pl.ds(pl.multiple_of(n * 128, 128), 128)
        block = matmul_tn(lifted_b[:, at], back_raised[...])
        up.parts[lax.div(n, 4), lax.rem(n, 4)] = block.reshape(4, 2, 16, 1024)
        up.start_core(n)
        return carry

    lax.fori_loop(0, 8, grad_up, 0)
    down.wait_core()
    down.first()
    up.wait_core()
    up.first()
    for copy in mix_copies + lift_copies:
        copy.wait_recv()
    row, col = iota((256, 512), 0), iota((256, 512), 1)
    spread = (row >> 2) * 8 + (row & 3)
    spread_in = (col == spread).astype(F32).astype(BF16)
    spread_out = (col == spread + 4).astype(F32).astype(BF16)
    for d in (1, 2, 3):
        lift_sum = lift_sum + lift_recv[d].astype(F32)
    lift_wide = matmul(lift_sum.astype(BF16), spread_in).astype(BF16)
    mix_wide = matmul(mix_recv[...].reshape(384, 256), spread_out).astype(BF16)
    both = matmul_tn(lift_wide, rows_in) + matmul_tn(mix_wide, errors)
    small.parts[...] = both.reshape(2, 4, 4, 2, 8, 384)
    for chunk in range(8):
        small.start_core(chunk)
    down.second()
    up.second()
    small.wait_core()
    small.first()
    down.third()
    up.third()
    small.second()
    out_down[...] = down.result()
    out_up[...] = up.result()
    small.third()
    out_small[...] = small.result()
    for copy in sent:
        copy.wait_send()
    for scatter in (down, up, small):
        scatter.finish()


def whole(count):
    return [pl.BlockSpec(memory_space=pltpu.VMEM)] * count


def on_device(velocity, viscosity, selection, w_in, w_up, w_down, w_out):
    shape = jax.ShapeDtypeStruct
    velocity_next, pressure, inputs, targets = pl.pallas_call(
        stencil_kernel,
        out_shape=[
            shape((3, 8, 32, 128), F32),
            shape((8, 32, 128), F32),
            shape((96, 384), BF16),
            shape((96, 384), BF16),
        ],
        in_specs=whole(3),
        out_specs=whole(4),
        scratch_shapes=PATCH_SCRATCH + Stencil.scratch,
        compiler_params=pltpu.CompilerParams(
            collective_id=0, has_side_effects=True, vmem_limit_bytes=48 * MIB
        ),
        name="stencil",
    )(velocity, viscosity, selection.reshape(96, 1))
    grad_up, grad_down, small = pl.pallas_call(
        trainer_kernel,
        out_shape=[shape((16, 1024), F32), shape((16, 1024), F32), shape((8, 384), F32)],
        in_specs=whole(6),
        out_specs=whole(3),
        scratch_shapes=TRAINER_SCRATCH,
        compiler_params=pltpu.CompilerParams(
            collective_id=1, has_side_effects=True, vmem_limit_bytes=56 * MIB
        ),
        name="trainer",
    )(inputs, targets, w_in, w_up, w_down, w_out)
    return (velocity_next, pressure, small[:4].T, grad_up, grad_down.T, small[4:])


def solution(mesh):
    placed = (
        P(None, "gx", "gy", "grp"),
        P("gx", "gy", "grp"),
        P("grp", "gx", "gy", None),
        P(),
        P(None, "gy"),
        P("gy", None),
        P(),
    )
    return jax.shard_map(
        on_device,
        mesh=mesh,
        in_specs=placed,
        out_specs=(
            P(None, "gx", "gy", "grp"),
            P("gx", "gy", "grp"),
            P(None, ("grp", "gx", "gy")),
            P(("grp", "gx"), "gy"),
            P("gy", ("grp", "gx")),
            P(("grp", "gx", "gy"), None),
        ),
        check_vma=False,
    )
```

```python
import jax
import jax.numpy as jnp
from jax import lax
from jax.experimental import pallas as pl
from jax.experimental.pallas import tpu as pltpu
from jax.sharding import PartitionSpec as P

F32 = jnp.float32
BF16 = jnp.bfloat16
MESH = pl.DeviceIdType.MESH
MIB = 1 << 20

FACES = [(1, 0), (-1, 0), (0, 1), (0, -1)]
DIAGONALS = [(1, 1), (1, -1), (-1, 1), (-1, -1)]
PLANE = FACES + DIAGONALS
CROSS_ONE = [(0, 0)] + FACES
CROSS_TWO = [(0, 0)] + PLANE


def place():
    return lax.axis_index("grp"), lax.axis_index("gx"), lax.axis_index("gy")


def push(src, dst, sems, slot, target):
    return pltpu.make_async_remote_copy(
        src_ref=src,
        dst_ref=dst,
        send_sem=sems.at[0, slot],
        recv_sem=sems.at[1, slot],
        device_id=target,
        device_id_type=MESH,
    )


def greet(targets):
    barrier = pltpu.get_barrier_semaphore()
    for target in targets:
        pl.semaphore_signal(barrier, inc=1, device_id=target, device_id_type=MESH)


def greeted(targets):
    pl.semaphore_wait(pltpu.get_barrier_semaphore(), len(targets))


def matmul(a, b):
    return jnp.dot(a, b, preferred_element_type=F32)


def matmul_nt(a, b):
    return lax.dot_general(a, b, (((1,), (1,)), ((), ())), preferred_element_type=F32)


def matmul_tn(a, b):
    return lax.dot_general(a, b, (((0,), (0,)), ((), ())), preferred_element_type=F32)


def iota(shape, dim):
    return lax.broadcasted_iota(jnp.int32, shape, dim)


def offset(here, dx, dy, flip):
    g, i, k = here
    return (1 - g if flip else g, lax.rem(i + dx + 32, 32), lax.rem(k + dy + 4, 4))


def stencil_targets(here):
    return [offset(here, dx, dy, False) for dx, dy in PLANE] + [
        offset(here, dx, dy, True) for dx, dy in CROSS_TWO
    ]


def pack_edge(g, group):
    lane = iota((16, 128), 1) // 8
    packed = jnp.zeros((16, 128), F32)
    for part in range(16):
        moved = pltpu.roll(group(part), lax.rem(8 * part + 8 * (1 - g), 128), 1)
        packed = jnp.where(lane == part, moved, packed)
    return packed


def unpack_edge(g, packed, part):
    lane = iota((16, 128), 1)
    rows = pltpu.roll(packed, lax.rem(128 - 8 * part + 120 * g, 128), 1)
    return jnp.where((lane - 120 * g) >> 3 == 0, rows, 0.0)


def unpack_block(g, packed, dx, dy, deep, store):
    planes = range(8) if dx == 0 else (range(8 - deep, 8) if dx < 0 else range(deep))
    for x in planes:
        to = deep + x if dx == 0 else (x - (8 - deep) if dx < 0 else deep + 8 + x)
        if dy == 0:
            store(to, 8, unpack_edge(g, packed, 2 * x))
            store(to, 24, unpack_edge(g, packed, 2 * x + 1))
        elif dy < 0:
            store(to, 0, unpack_edge(g, packed, 2 * x + 1)[8:16])
        else:
            store(to, 40, unpack_edge(g, packed, 2 * x)[0:8])


def along_z(own, other):
    lane = iota(own.shape, 1)
    own_r, other_r = pltpu.roll(own, 127, 1), pltpu.roll(other, 127, 1)
    own_l, other_l = pltpu.roll(own, 1, 1), pltpu.roll(other, 1, 1)
    last, first = lane == 127, lane == 0
    right = (jnp.where(last, other_r, own_r), jnp.where(last, own_r, other_r))
    left = (jnp.where(first, other_l, own_l), jnp.where(first, own_l, other_l))
    return right, left


def own_slices(dx, dy, deep, rows):
    xs = slice(0, 8) if dx == 0 else (slice(8 - deep, 8) if dx > 0 else slice(0, deep))
    ys = slice(0, 32) if dy == 0 else (slice(32 - rows, 32) if dy > 0 else slice(0, rows))
    return xs, ys


class Stencil:
    scratch = [
        pltpu.VMEM((4, 8, 32, 128), F32),
        pltpu.VMEM((2, 4, 8, 2, 128), F32),
        pltpu.VMEM((2, 4, 8, 2, 128), F32),
        pltpu.VMEM((4, 4, 2, 2, 128), F32),
        pltpu.VMEM((4, 16, 128), F32),
        pltpu.VMEM((5, 4, 16, 128), F32),
        pltpu.VMEM((4, 2, 12, 48, 128), F32),
        pltpu.VMEM((3, 2, 12, 48, 128), F32),
        pltpu.VMEM((8, 32, 128), F32),
        pltpu.VMEM((16, 128), F32),
        pltpu.VMEM((9, 16, 128), F32),
        pltpu.VMEM((2, 20, 48, 128), F32),
        pltpu.VMEM((2, 20, 64, 128), F32),
        pltpu.VMEM((2, 20, 64, 128), F32),
        pltpu.SemaphoreType.DMA((2, 13)),
        pltpu.SemaphoreType.DMA((2, 17)),
    ]

    def __init__(self, here, velocity_next, pressure, refs):
        self.here = here
        self.velocity_next, self.pressure = velocity_next, pressure
        (
            self.fields, self.y_send, self.y_recv, self.d_recv, self.z_send, self.z_recv,
            self.wide, self.prov, self.source, self.sz_send, self.sz_recv, self.swide,
            self.p_a, self.p_b, self.sems_one, self.sems_two,
        ) = refs

    def prepare(self):
        g = self.here[0]
        self.y_send[0] = self.fields[:, :, 30:32, :]
        self.y_send[1] = self.fields[:, :, 0:2, :]
        for f in range(4):
            self.z_send[f] = pack_edge(
                g, lambda part: self.fields[f, part // 2, 16 * (part % 2) : 16 * (part % 2) + 16, :]
            )

    def send_one(self):
        g = self.here[0]
        copies = []
        for dx, dy in PLANE:
            slot = len(copies)
            target = offset(self.here, dx, dy, False)
            xs, _ = own_slices(dx, dy, 2, 2)
            if dy == 0:
                x_to = 0 if dx > 0 else 10
                src = self.fields.at[:, xs]
                dst = self.wide.at[:, 0, x_to : x_to + 2, 8:40, :]
            elif dx == 0:
                edge = 0 if dy > 0 else 1
                src, dst = self.y_send.at[edge], self.y_recv.at[edge]
            else:
                edge = 0 if dy > 0 else 1
                src, dst = self.y_send.at[edge, :, xs], self.d_recv.at[slot - 4]
            copies.append(push(src, dst, self.sems_one, slot, target))
        for n, (dx, dy) in enumerate(CROSS_ONE):
            target = offset(self.here, dx, dy, True)
            copies.append(push(self.z_send, self.z_recv.at[n], self.sems_one, len(copies), target))
        for copy in copies:
            copy.start()
        self.copies_one = copies

    def make_source(self):
        g, i, k = self.here
        wide = self.wide
        wide[:, 0, 2:10, 8:40, :] = self.fields[...]
        for copy in self.copies_one:
            copy.wait_recv()
        wide[:, 0, 2:10, 6:8, :] = self.y_recv[0]
        wide[:, 0, 2:10, 40:42, :] = self.y_recv[1]
        for n, (dx, dy) in enumerate(DIAGONALS):
            x_to, y_to = (0 if dx > 0 else 10), (6 if dy > 0 else 40)
            wide[:, 0, x_to : x_to + 2, y_to : y_to + 2, :] = self.d_recv[n]
        for n, (dx, dy) in enumerate(CROSS_ONE):
            for f in (0, 1, 2, 3) if n == 0 else ((0, 2) if dx else (1, 2)):

                def store(to, row, rows, f=f):
                    wide[f, 1, to, row : row + rows.shape[0], :] = rows

                unpack_block(g, self.z_recv[n, f], -dx, -dy, 2, store)

        @pl.when(i == 0)
        def _():
            wide[:, :, 0:2] = jnp.zeros((4, 2, 2, 48, 128), F32)

        @pl.when(i == 31)
        def _():
            wide[:, :, 10:12] = jnp.zeros((4, 2, 2, 48, 128), F32)

        @pl.when(k == 0)
        def _():
            wide[:, :, :, 0:8, :] = jnp.zeros((4, 2, 12, 8, 128), F32)

        @pl.when(k == 3)
        def _():
            wide[:, :, :, 40:48, :] = jnp.zeros((4, 2, 12, 8, 128), F32)

        def advance(c, x, top, bottom, tiles):
            mid = [wide[c, t, x, top:bottom, :] for t in range(2)]
            right, left = along_z(*mid)
            for t in tiles:
                total = wide[c, t, x + 1, top:bottom, :] + wide[c, t, x - 1, top:bottom, :]
                total = total + wide[c, t, x, top + 1 : bottom + 1, :]
                total = total + wide[c, t, x, top - 1 : bottom - 1, :]
                total = total + right[t] + left[t]
                after = mid[t] + wide[3, t, x, top:bottom, :] * (total - 6.0 * mid[t])
                self.prov[c, t, x, top:bottom, :] = after

        def provisional(x, carry):
            advance(0, x, 8, 40, (0,))
            advance(1, x, 7, 41, (0,))
            advance(2, x, 8, 40, (0, 1))
            return carry

        advance(0, 1, 8, 40, (0,))
        advance(0, 10, 8, 40, (0,))
        lax.fori_loop(2, 10, provisional, 0)
        prov = self.prov

        def source(x, carry):
            right, left = along_z(prov[2, 0, x, 8:40, :], prov[2, 1, x, 8:40, :])
            slope = right[0] - left[0]
            slope = slope + prov[0, 0, x + 1, 8:40, :] - prov[0, 0, x - 1, 8:40, :]
            slope = slope + prov[1, 0, x, 9:41, :] - prov[1, 0, x, 7:39, :]
            self.source[x - 2] = 0.5 * slope
            return carry

        lax.fori_loop(2, 10, source, 0)
        self.sz_send[...] = pack_edge(
            g, lambda part: self.source[part // 2, 16 * (part % 2) : 16 * (part % 2) + 16, :]
        )

    def send_two(self):
        g = self.here[0]
        copies = []
        for dx, dy in PLANE:
            target = offset(self.here, dx, dy, False)
            xs, ys = own_slices(dx, dy, 6, 8)
            x_to = 6 if dx == 0 else (0 if dx > 0 else 14)
            y_to = 8 if dy == 0 else (0 if dy > 0 else 40)
            dst = self.swide.at[
                0, x_to : x_to + xs.stop - xs.start, y_to : y_to + ys.stop - ys.start, :
            ]
            copies.append(push(self.source.at[xs, ys, :], dst, self.sems_two, len(copies), target))
        for n, (dx, dy) in enumerate(CROSS_TWO):
            target = offset(self.here, dx, dy, True)
            copies.append(push(self.sz_send, self.sz_recv.at[n], self.sems_two, len(copies), target))
        for copy in copies:
            copy.start()
        self.copies_two = copies

    def solve(self):
        g, i, k = self.here
        swide = self.swide
        swide[0, 6:14, 8:40, :] = self.source[...]
        for copy in self.copies_two:
            copy.wait_recv()
        for n, (dx, dy) in enumerate(CROSS_TWO):

            def store(to, row, rows):
                swide[1, to, row : row + rows.shape[0], :] = rows

            unpack_block(g, self.sz_recv[n], -dx, -dy, 6, store)
        row, lane = iota((48, 128), 0), iota((48, 128), 1)
        outside = ((k == 0) & (row < 8)) | ((k == 3) & (row >= 40))
        sixth = jnp.where(outside, 0.0, 1.0 / 6.0).astype(F32)
        sixths = (sixth, jnp.where((lane - 120 * g) >> 3 == 0, sixth, 0.0))

        def inside(x):
            out = ((i == 0) & (x < 6)) | ((i == 31) & (x >= 14))
            scale = jnp.where(out, 0.0, 1.0).astype(F32)
            return [one * scale for one in sixths]

        def first(x, carry):
            scale = inside(x)
            for t in range(2):
                self.p_a[t, x, 8:56, :] = -swide[t, x] * scale[t]
            return carry

        lax.fori_loop(0, 20, first, 0)
        old, new = self.p_a, self.p_b
        for sweep in range(1, 6):

            def relax(x, carry, old=old, new=new):
                scale = inside(x)
                right, left = along_z(old[0, x, 8:56, :], old[1, x, 8:56, :])
                for t in range(2):
                    total = old[t, x + 1, 8:56, :] + old[t, x - 1, 8:56, :]
                    total = total + old[t, x, 9:57, :] + old[t, x, 7:55, :]
                    total = total + right[t] + left[t]
                    new[t, x, 8:56, :] = (total - swide[t, x]) * scale[t]
                return carry

            lax.fori_loop(sweep, 20 - sweep, relax, 0)
            old, new = new, old
        p, prov = old, self.prov

        def project(x, carry):
            at = x + 6
            right, left = along_z(p[0, at, 16:48, :], p[1, at, 16:48, :])
            slope_z = right[0] - left[0]
            slope_x = p[0, at + 1, 16:48, :] - p[0, at - 1, 16:48, :]
            slope_y = p[0, at, 17:49, :] - p[0, at, 15:47, :]
            for c, slope in enumerate((slope_x, slope_y, slope_z)):
                self.velocity_next[c, x] = prov[c, 0, x + 2, 8:40, :] - 0.5 * slope
            self.pressure[x] = p[0, at, 16:48, :]
            return carry

        lax.fori_loop(0, 8, project, 0)

    def finish(self):
        for copy in self.copies_one + self.copies_two:
            copy.wait_send()


PATCH_SCRATCH = [pltpu.VMEM((16, 6144), F32), pltpu.VMEM((2048, 128), BF16)]


def make_fold(fold):
    row, col = iota((2048, 128), 0), iota((2048, 128), 1)
    hit = (row // 128 == col // 8) & (row % 8 == col % 8)
    fold[...] = hit.astype(F32).astype(BF16)


def pick_patches(field, selection, lines, fold, out):
    for c in range(3):
        for x in range(8):
            for py in range(4):
                combo = (c * 4 + x % 4) * 4 + py
                row = 8 * (x // 4)
                lines[row : row + 8, 128 * combo : 128 * combo + 128] = field[
                    c, x, pl.ds(py, 8, stride=4), :
                ]
    chosen = jnp.broadcast_to(selection[...], (16, 96))
    line = (chosen >> 4 == iota((16, 96), 0)).astype(F32).astype(BF16)
    cell = (chosen & 15 == iota((16, 96), 0)).astype(F32).astype(BF16)
    spread = ((iota((16, 2048), 1) & 127) >> 3 == iota((16, 2048), 0)).astype(F32).astype(BF16)
    here = matmul_tn(cell, spread)
    for part in range(3):
        source = lines[:, 2048 * part : 2048 * part + 2048].astype(BF16)
        rows = (matmul_tn(line, source) * here).astype(BF16)
        out[:, 128 * part : 128 * part + 128] = matmul(rows, fold[...]).astype(BF16)


def trainer_targets(here):
    g, i, k = here
    x, y, c = lax.div(i, 8), lax.rem(lax.div(i, 2), 4), lax.rem(i, 2)
    out = [(g, i, lax.rem(k + d, 4)) for d in (1, 2, 3)]
    out += [(g, lax.rem(x + d, 4) * 8 + y * 2 + c, k) for d in (1, 2, 3)]
    out += [(g, x * 8 + lax.rem(y + d, 4) * 2 + c, k) for d in (1, 2, 3)]
    return out + [(g, x * 8 + y * 2 + 1 - c, k), (1 - g, i, k)]


class Scatter:
    @staticmethod
    def scratch(rows, width, wire):
        return [
            pltpu.VMEM((2, 4, 4, 2, rows, width), F32),
            pltpu.VMEM((2, 4, 4, rows, width), F32),
            pltpu.VMEM((4, 2, 4, rows, width), wire),
            pltpu.VMEM((4, 2, 4, rows, width), wire),
            pltpu.VMEM((2, 4, rows, width), F32),
            pltpu.VMEM((4, 2, rows, width), F32),
            pltpu.VMEM((2, rows, width), F32),
            pltpu.VMEM((rows, width), F32),
            pltpu.SemaphoreType.DMA((2, 8)),
            pltpu.SemaphoreType.DMA((2, 4)),
            pltpu.SemaphoreType.DMA((2, 4)),
            pltpu.SemaphoreType.DMA((2, 1)),
        ]

    def __init__(self, here, refs, wire, x_first):
        g, i, k = here
        self.here, self.wire, self.x_first = here, wire, x_first
        self.x, self.y, self.c = lax.div(i, 8), lax.rem(lax.div(i, 2), 4), lax.rem(i, 2)
        (
            self.parts, self.core_recv, self.one_send, self.one_recv, self.one_sum,
            self.two_recv, self.two_sum, self.three_recv,
            self.core_sems, self.one_sems, self.two_sems, self.three_sems,
        ) = refs

    def along(self, on_x, d):
        g, i, k = self.here
        x, y = self.x, self.y
        if on_x:
            x = lax.rem(x + d, 4)
        else:
            y = lax.rem(y + d, 4)
        return (g, x * 8 + y * 2 + self.c, k)

    def core_copy(self, chunk):
        g, i, k = self.here
        half, x = lax.div(chunk, 4), lax.rem(chunk, 4)
        return push(
            self.parts.at[half, x, :, 1 - self.c],
            self.core_recv.at[half, x],
            self.core_sems,
            chunk,
            (g, self.x * 8 + self.y * 2 + 1 - self.c, k),
        )

    def start_core(self, chunk):
        self.core_copy(jnp.int32(chunk)).start()

    def wait_core(self):
        for chunk in range(8):
            self.core_copy(jnp.int32(chunk)).wait_recv()

    def first(self):
        mine = self.x if self.x_first else self.y
        self.one = []
        for d in (2, 1, 3, 0):
            to = lax.rem(mine + d, 4)
            if self.x_first:
                total = self.parts[:, to, :, self.c] + self.core_recv[:, to]
            else:
                total = self.parts[:, :, to, self.c] + self.core_recv[:, :, to]
            if d == 0:
                self.one_sum[...] = total
            else:
                self.one_send[d] = total.astype(self.wire)
                copy = push(
                    self.one_send.at[d], self.one_recv.at[d], self.one_sems, d,
                    self.along(self.x_first, d),
                )
                copy.start()
                self.one.append(copy)

    def second(self):
        for copy in self.one:
            copy.wait_recv()
        total = self.one_sum[...]
        for d in (1, 2, 3):
            total = total + self.one_recv[d].astype(F32)
        self.one_sum[...] = total
        mine = self.y if self.x_first else self.x
        self.two = []
        for d in (2, 1, 3):
            copy = push(
                self.one_sum.at[:, lax.rem(mine + d, 4)], self.two_recv.at[d], self.two_sems, d,
                self.along(not self.x_first, d),
            )
            copy.start()
            self.two.append(copy)

    def third(self):
        g, i, k = self.here
        mine = self.y if self.x_first else self.x
        for copy in self.two:
            copy.wait_recv()
        self.two_sum[...] = (
            self.one_sum[:, mine] + self.two_recv[1] + self.two_recv[2] + self.two_recv[3]
        )
        self.three = push(
            self.two_sum.at[1 - g], self.three_recv, self.three_sems, 0, (1 - g, i, k)
        )
        self.three.start()

    def result(self):
        self.three.wait_recv()
        return self.two_sum[self.here[0]] + self.three_recv[...]

    def finish(self):
        for chunk in range(8):
            self.core_copy(jnp.int32(chunk)).wait_send()
        for copy in self.one + self.two + [self.three]:
            copy.wait_send()


N_SCATTER = 12
TRAINER_SCRATCH = [
    pltpu.VMEM((384, 1024), BF16),
    pltpu.VMEM((1024, 1024), BF16),
    pltpu.VMEM((1024, 1024), BF16),
    pltpu.VMEM((1024, 384), BF16),
    pltpu.VMEM((96, 384), BF16),
    pltpu.VMEM((4, 96, 384), BF16),
    pltpu.VMEM((4, 96, 384), BF16),
    pltpu.VMEM((4, 96, 1024), BF16),
    pltpu.VMEM((4, 96, 1024), F32),
    pltpu.VMEM((4, 96, 1024), BF16),
    pltpu.VMEM((96, 1024), F32),
    pltpu.VMEM((4, 96, 1024), BF16),
    pltpu.VMEM((4, 96, 1024), BF16),
    pltpu.VMEM((384, 1024), BF16),
    pltpu.VMEM((384, 1024), BF16),
    pltpu.VMEM((384, 1024), F32),
    pltpu.VMEM((384, 1024), BF16),
    pltpu.VMEM((4, 8, 384), F32),
    pltpu.VMEM((4, 8, 384), F32),
    pltpu.SemaphoreType.DMA((6,)),
    pltpu.SemaphoreType.DMA((2, 4)),
    pltpu.SemaphoreType.DMA((2, 4)),
    pltpu.SemaphoreType.DMA((2, 4)),
    pltpu.SemaphoreType.DMA((2, 4)),
]
N_TRAINER = len(TRAINER_SCRATCH)
for _width in (1024, 1024, 384, 384):
    TRAINER_SCRATCH += Scatter.scratch(16, _width, BF16)


def columns(n):
    return pl.ds(pl.multiple_of(n * 256, 256), 256)


def step_kernel(
    velocity, viscosity, selection, w_in_far, w_up_far, w_down_far, w_out_far,
    velocity_next, pressure, out_up, out_down, out_small, lines, fold, *refs
):
    here = place()
    g, i, k = here
    n_stencil = len(Stencil.scratch)
    step = Stencil(here, velocity_next, pressure, refs[:n_stencil])
    refs = refs[n_stencil:]
    (
        w_in, w_up, w_down, w_out, targets, in_all, err_all, lifted_b, slope, active, own_mixed,
        down_send, down_recv, back_b, back_raised, lift_sum, lift_b, tail_send, tail_recv,
        near_sems, in_sems, down_sems, err_sems, tail_sems,
    ) = refs[:N_TRAINER]
    refs = refs[N_TRAINER:]
    up, down, grad_in, grad_out = (
        Scatter(here, refs[n * N_SCATTER : (n + 1) * N_SCATTER], BF16, x_first)
        for n, x_first in enumerate((True, False, False, True))
    )
    sent = []

    def peer(d):
        return (g, i, lax.rem(k + d, 4))

    def start(copies):
        for copy in copies:
            copy.start()
        sent.extend(copies)
        return copies

    met = stencil_targets(here) + trainer_targets(here)
    greet(met)
    near = [
        pltpu.make_async_copy(src, dst, near_sems.at[n])
        for n, (src, dst) in enumerate(
            (
                (velocity, step.fields.at[0:3]),
                (viscosity, step.fields.at[3]),
                (w_in_far, w_in),
                (w_up_far, w_up),
                (w_down_far, w_down),
                (w_out_far, w_out),
            )
        )
    ]
    for copy in near:
        copy.start()
    make_fold(fold)
    for copy in near[:2]:
        copy.wait()
    pick_patches(step.fields, selection, lines, fold, in_all.at[k])
    step.prepare()
    greeted(met)
    in_copies = start(
        [push(in_all.at[k], in_all.at[k], in_sems, d, peer(d)) for d in (2, 1, 3)]
    )
    step.send_one()
    for copy in near[2:]:
        copy.wait()

    def forward(owner):
        rows = in_all[owner]
        lifted = matmul(rows, w_in[...])
        lifted_b[owner] = lifted.astype(BF16)

        def raise_(n, carry):
            at = columns(n)
            raised = matmul(lifted_b[owner], w_up[:, at])
            sigmoid = jax.nn.sigmoid(raised)
            active[owner, :, at] = (raised * sigmoid).astype(BF16)
            slope[owner, :, at] = sigmoid * (1.0 + raised * (1.0 - sigmoid))
            return carry

        lax.fori_loop(0, 4, raise_, 0)
        return lifted

    own_mixed[...] = forward(k) + matmul(active[k], w_down[...])
    step.make_source()
    step.send_two()
    down_copies = []
    for copy, d in zip(in_copies[1:] + in_copies[:1], (3, 1, 2)):
        copy.wait_recv()
        owner = lax.rem(k + d, 4)
        forward(owner)
        down_send[d] = matmul(active[owner], w_down[...]).astype(BF16)
        down_copies += start([push(down_send.at[d], down_recv.at[d], down_sems, d, peer(d))])
    step.solve()
    pick_patches(velocity_next, selection, lines, fold, targets)

    for copy in down_copies:
        copy.wait_recv()
    mixed = own_mixed[...]
    for d in (1, 2, 3):
        mixed = mixed + down_recv[d].astype(F32)
    mixed_b = mixed.astype(BF16)
    predicted = matmul(mixed_b, w_out[...])
    scale = float(24576) ** (-0.5)
    err_all[k] = ((predicted - targets[...].astype(F32)) * scale).astype(BF16)
    err_copies = start(
        [push(err_all.at[k], err_all.at[k], err_sems, d, peer(d)) for d in (2, 1, 3)]
    )
    for n in range(8):
        block = matmul_tn(mixed_b[:, 128 * n : 128 * n + 128], err_all[k])
        grad_out.parts[n // 4, n % 4] = block.reshape(4, 2, 16, 384)
        grad_out.start_core(n)
    grad_out.wait_core()
    grad_out.first()
    for copy in err_copies:
        copy.wait_recv()
    errors = err_all[...].reshape(384, 384)

    def back(n, carry):
        at = columns(n)
        both = matmul_nt(errors, w_out[at, :])
        back_b[:, at] = both.astype(BF16)
        lift_sum[:, at] = both
        return carry

    lax.fori_loop(0, 4, back, 0)

    def grad_chunk(scatter, left, right, width):
        def chunk(n, carry):
            at = pl.ds(pl.multiple_of(n * 128, 128), 128)
            block = matmul_tn(left[:, at], right)
            scatter.parts[lax.div(n, 4), lax.rem(n, 4)] = block.reshape(4, 2, 16, width)
            scatter.start_core(n)
            return carry

        lax.fori_loop(0, 8, chunk, 0)

    grad_chunk(down, back_b, active[...].reshape(384, 1024), 1024)

    def back_up(n, carry):
        at = columns(n)
        steep = slope[:, :, at].reshape(384, 256)
        back_raised[:, at] = (matmul_nt(back_b[...], w_down[at, :]) * steep).astype(BF16)
        return carry

    lax.fori_loop(0, 4, back_up, 0)
    down.wait_core()
    down.first()
    own_row = iota((384, 256), 0) // 96 == k

    def back_lift(n, carry):
        at = columns(n)
        mine = jnp.where(own_row, lift_sum[:, at], 0.0)
        lift_b[:, at] = (mine + matmul_nt(back_raised[...], w_up[at, :])).astype(BF16)
        return carry

    lax.fori_loop(0, 4, back_lift, 0)
    lifted_rows = lifted_b.reshape(384, 1024)
    grad_chunk(up, lifted_rows, back_raised[...], 1024)
    grad_chunk(grad_in, lift_b, in_all[...].reshape(384, 384), 384)
    up.wait_core()
    up.first()
    grad_in.wait_core()
    grad_in.first()
    scatters = (grad_out, down, up, grad_in)
    for scatter in scatters:
        scatter.second()
    for scatter in scatters:
        scatter.third()
    last_in, last_out = grad_in.result(), grad_out.result()
    for j in range(4):
        tail_send[j, 0:4] = last_in[4 * j : 4 * j + 4]
        tail_send[j, 4:8] = last_out[4 * j : 4 * j + 4]
    tail_copies = start(
        [
            push(tail_send.at[lax.rem(k + d, 4)], tail_recv.at[d], tail_sems, d, peer(d))
            for d in (2, 1, 3)
        ]
    )
    out_down[...] = down.result()
    out_up[...] = up.result()
    for copy in tail_copies:
        copy.wait_recv()
    out_small[...] = tail_send[k] + tail_recv[1] + tail_recv[2] + tail_recv[3]
    for copy in sent:
        copy.wait_send()
    step.finish()
    for scatter in scatters:
        scatter.finish()


def on_device(velocity, viscosity, selection, w_in, w_up, w_down, w_out):
    shape = jax.ShapeDtypeStruct
    far, near = pl.BlockSpec(memory_space=pl.ANY), pl.BlockSpec(memory_space=pltpu.VMEM)
    velocity_next, pressure, grad_up, grad_down, small = pl.pallas_call(
        step_kernel,
        out_shape=[
            shape((3, 8, 32, 128), F32),
            shape((8, 32, 128), F32),
            shape((16, 1024), F32),
            shape((16, 1024), F32),
            shape((8, 384), F32),
        ],
        in_specs=[far, far, near, far, far, far, far],
        out_specs=[near] * 5,
        scratch_shapes=PATCH_SCRATCH + Stencil.scratch + TRAINER_SCRATCH,
        compiler_params=pltpu.CompilerParams(
            collective_id=0, has_side_effects=True, vmem_limit_bytes=56 * MIB
        ),
        name="step",
    )(velocity, viscosity, selection.reshape(1, 96), w_in, w_up, w_down, w_out)
    return (velocity_next, pressure, small[:4].T, grad_up, grad_down.T, small[4:])


def solution(mesh):
    placed = (
        P(None, "gx", "gy", "grp"),
        P("gx", "gy", "grp"),
        P("grp", "gx", "gy", None),
        P(),
        P(None, "gy"),
        P("gy", None),
        P(),
    )
    return jax.shard_map(
        on_device,
        mesh=mesh,
        in_specs=placed,
        out_specs=(
            P(None, "gx", "gy", "grp"),
            P("gx", "gy", "grp"),
            P(None, ("grp", "gx", "gy")),
            P(("grp", "gx"), "gy"),
            P("gy", ("grp", "gx")),
            P(("grp", "gx", "gy"), None),
        ),
        check_vma=False,
    )
```

```python
import jax
import jax.numpy as jnp
from jax import lax
from jax.experimental import pallas as pl
from jax.experimental.pallas import tpu as pltpu
from jax.sharding import PartitionSpec as P

F32 = jnp.float32
BF16 = jnp.bfloat16
MESH = pl.DeviceIdType.MESH
MIB = 1 << 20

FACES = [(1, 0), (-1, 0), (0, 1), (0, -1)]
DIAGONALS = [(1, 1), (1, -1), (-1, 1), (-1, -1)]
PLANE = FACES + DIAGONALS
CROSS_ONE = [(0, 0)] + FACES
CROSS_TWO = [(0, 0)] + PLANE
EDGE_ORDER = (1, 2, 0, 3)


def place():
    return lax.axis_index("grp"), lax.axis_index("gx"), lax.axis_index("gy")


def push(src, dst, sems, slot, target):
    return pltpu.make_async_remote_copy(
        src_ref=src,
        dst_ref=dst,
        send_sem=sems.at[0, slot],
        recv_sem=sems.at[1, slot],
        device_id=target,
        device_id_type=MESH,
    )


def greet(targets):
    barrier = pltpu.get_barrier_semaphore()
    for target in targets:
        pl.semaphore_signal(barrier, inc=1, device_id=target, device_id_type=MESH)


def greeted(targets):
    pl.semaphore_wait(pltpu.get_barrier_semaphore(), len(targets))


def matmul(a, b):
    return jnp.dot(a, b, preferred_element_type=F32)


def matmul_nt(a, b):
    return lax.dot_general(a, b, (((1,), (1,)), ((), ())), preferred_element_type=F32)


def matmul_tn(a, b):
    return lax.dot_general(a, b, (((0,), (0,)), ((), ())), preferred_element_type=F32)


def iota(shape, dim):
    return lax.broadcasted_iota(jnp.int32, shape, dim)


def offset(here, dx, dy, flip):
    g, i, k = here
    return (1 - g if flip else g, lax.rem(i + dx + 32, 32), lax.rem(k + dy + 4, 4))


def stencil_targets(here):
    return [offset(here, dx, dy, False) for dx, dy in PLANE] + [
        offset(here, dx, dy, True) for dx, dy in CROSS_TWO
    ]


def pack_edge(g, group):
    lane = iota((16, 128), 1) // 8
    packed = jnp.zeros((16, 128), F32)
    for part in range(16):
        moved = pltpu.roll(group(part), lax.rem(8 * part + 8 * (1 - g), 128), 1)
        packed = jnp.where(lane == part, moved, packed)
    return packed


def unpack_edge(g, packed, part):
    lane = iota((16, 128), 1)
    rows = pltpu.roll(packed, lax.rem(128 - 8 * part + 120 * g, 128), 1)
    return jnp.where((lane - 120 * g) >> 3 == 0, rows, 0.0)


def unpack_block(g, packed, dx, dy, deep, store):
    planes = range(8) if dx == 0 else (range(8 - deep, 8) if dx < 0 else range(deep))
    for x in planes:
        to = deep + x if dx == 0 else (x - (8 - deep) if dx < 0 else deep + 8 + x)
        if dy == 0:
            store(to, 8, unpack_edge(g, packed, 2 * x))
            store(to, 24, unpack_edge(g, packed, 2 * x + 1))
        elif dy < 0:
            store(to, 0, unpack_edge(g, packed, 2 * x + 1)[8:16])
        else:
            store(to, 40, unpack_edge(g, packed, 2 * x)[0:8])


def along_z(own, other):
    lane = iota(own.shape, 1)
    own_r, other_r = pltpu.roll(own, 127, 1), pltpu.roll(other, 127, 1)
    own_l, other_l = pltpu.roll(own, 1, 1), pltpu.roll(other, 1, 1)
    last, first = lane == 127, lane == 0
    right = (jnp.where(last, other_r, own_r), jnp.where(last, own_r, other_r))
    left = (jnp.where(first, other_l, own_l), jnp.where(first, own_l, other_l))
    return right, left


def own_slices(dx, dy, deep, rows):
    xs = slice(0, 8) if dx == 0 else (slice(8 - deep, 8) if dx > 0 else slice(0, deep))
    ys = slice(0, 32) if dy == 0 else (slice(32 - rows, 32) if dy > 0 else slice(0, rows))
    return xs, ys


class Stencil:
    scratch = [
        pltpu.VMEM((4, 8, 32, 128), F32),
        pltpu.VMEM((2, 4, 8, 2, 128), F32),
        pltpu.VMEM((2, 4, 8, 2, 128), F32),
        pltpu.VMEM((4, 4, 2, 2, 128), F32),
        pltpu.VMEM((4, 16, 128), F32),
        pltpu.VMEM((5, 4, 16, 128), F32),
        pltpu.VMEM((4, 2, 12, 48, 128), F32),
        pltpu.VMEM((3, 2, 12, 48, 128), F32),
        pltpu.VMEM((8, 32, 128), F32),
        pltpu.VMEM((16, 128), F32),
        pltpu.VMEM((9, 16, 128), F32),
        pltpu.VMEM((2, 20, 48, 128), F32),
        pltpu.VMEM((2, 20, 64, 128), F32),
        pltpu.VMEM((2, 20, 64, 128), F32),
        pltpu.SemaphoreType.DMA((2, 13)),
        pltpu.SemaphoreType.DMA((2, 17)),
    ]

    def __init__(self, here, velocity_next, pressure, refs):
        self.here = here
        self.velocity_next, self.pressure = velocity_next, pressure
        (
            self.fields, self.y_send, self.y_recv, self.d_recv, self.z_send, self.z_recv,
            self.wide, self.prov, self.source, self.sz_send, self.sz_recv, self.swide,
            self.p_a, self.p_b, self.sems_one, self.sems_two,
        ) = refs

    def prepare(self):
        g = self.here[0]
        self.y_send[0] = self.fields[:, :, 30:32, :]
        self.y_send[1] = self.fields[:, :, 0:2, :]
        for f in range(4):
            self.z_send[EDGE_ORDER.index(f)] = pack_edge(
                g, lambda part: self.fields[f, part // 2, 16 * (part % 2) : 16 * (part % 2) + 16, :]
            )

    def send_one(self):
        g = self.here[0]
        copies = []
        for dx, dy in PLANE:
            slot = len(copies)
            target = offset(self.here, dx, dy, False)
            xs, _ = own_slices(dx, dy, 2, 2)
            if dy == 0:
                x_to = 0 if dx > 0 else 10
                src = self.fields.at[:, xs]
                dst = self.wide.at[:, 0, x_to : x_to + 2, 8:40, :]
            elif dx == 0:
                edge = 0 if dy > 0 else 1
                src, dst = self.y_send.at[edge], self.y_recv.at[edge]
            else:
                edge = 0 if dy > 0 else 1
                src, dst = self.y_send.at[edge, :, xs], self.d_recv.at[slot - 4]
            copies.append(push(src, dst, self.sems_one, slot, target))
        for n, (dx, dy) in enumerate(CROSS_ONE):
            target = offset(self.here, dx, dy, True)
            some = slice(1, 3) if dx else (slice(0, 2) if dy else slice(0, 4))
            src, dst = self.z_send.at[some], self.z_recv.at[n, some]
            copies.append(push(src, dst, self.sems_one, len(copies), target))
        for copy in copies:
            copy.start()
        self.copies_one = copies

    def make_source(self):
        g, i, k = self.here
        wide = self.wide
        wide[:, 0, 2:10, 8:40, :] = self.fields[...]
        for copy in self.copies_one:
            copy.wait_recv()
        wide[:, 0, 2:10, 6:8, :] = self.y_recv[0]
        wide[:, 0, 2:10, 40:42, :] = self.y_recv[1]
        for n, (dx, dy) in enumerate(DIAGONALS):
            x_to, y_to = (0 if dx > 0 else 10), (6 if dy > 0 else 40)
            wide[:, 0, x_to : x_to + 2, y_to : y_to + 2, :] = self.d_recv[n]
        for n, (dx, dy) in enumerate(CROSS_ONE):
            for f in (0, 1, 2, 3) if n == 0 else ((0, 2) if dx else (1, 2)):

                def store(to, row, rows, f=f):
                    wide[f, 1, to, row : row + rows.shape[0], :] = rows

                unpack_block(g, self.z_recv[n, EDGE_ORDER.index(f)], -dx, -dy, 2, store)

        @pl.when(i == 0)
        def _():
            wide[:, :, 0:2] = jnp.zeros((4, 2, 2, 48, 128), F32)

        @pl.when(i == 31)
        def _():
            wide[:, :, 10:12] = jnp.zeros((4, 2, 2, 48, 128), F32)

        @pl.when(k == 0)
        def _():
            wide[:, :, :, 0:8, :] = jnp.zeros((4, 2, 12, 8, 128), F32)

        @pl.when(k == 3)
        def _():
            wide[:, :, :, 40:48, :] = jnp.zeros((4, 2, 12, 8, 128), F32)

        def advance(c, x, top, bottom, tiles):
            mid = [wide[c, t, x, top:bottom, :] for t in range(2)]
            right, left = along_z(*mid)
            for t in tiles:
                total = wide[c, t, x + 1, top:bottom, :] + wide[c, t, x - 1, top:bottom, :]
                total = total + wide[c, t, x, top + 1 : bottom + 1, :]
                total = total + wide[c, t, x, top - 1 : bottom - 1, :]
                total = total + right[t] + left[t]
                after = mid[t] + wide[3, t, x, top:bottom, :] * (total - 6.0 * mid[t])
                self.prov[c, t, x, top:bottom, :] = after

        def provisional(x, carry):
            advance(0, x, 8, 40, (0,))
            advance(1, x, 7, 41, (0,))
            advance(2, x, 8, 40, (0, 1))
            return carry

        advance(0, 1, 8, 40, (0,))
        advance(0, 10, 8, 40, (0,))
        lax.fori_loop(2, 10, provisional, 0)
        prov = self.prov

        def source(x, carry):
            right, left = along_z(prov[2, 0, x, 8:40, :], prov[2, 1, x, 8:40, :])
            slope = right[0] - left[0]
            slope = slope + prov[0, 0, x + 1, 8:40, :] - prov[0, 0, x - 1, 8:40, :]
            slope = slope + prov[1, 0, x, 9:41, :] - prov[1, 0, x, 7:39, :]
            self.source[x - 2] = 0.5 * slope
            return carry

        lax.fori_loop(2, 10, source, 0)
        self.sz_send[...] = pack_edge(
            g, lambda part: self.source[part // 2, 16 * (part % 2) : 16 * (part % 2) + 16, :]
        )

    def send_two(self):
        g = self.here[0]
        copies = []
        for dx, dy in PLANE:
            target = offset(self.here, dx, dy, False)
            xs, ys = own_slices(dx, dy, 6, 8)
            x_to = 6 if dx == 0 else (0 if dx > 0 else 14)
            y_to = 8 if dy == 0 else (0 if dy > 0 else 40)
            dst = self.swide.at[
                0, x_to : x_to + xs.stop - xs.start, y_to : y_to + ys.stop - ys.start, :
            ]
            copies.append(push(self.source.at[xs, ys, :], dst, self.sems_two, len(copies), target))
        for n, (dx, dy) in enumerate(CROSS_TWO):
            target = offset(self.here, dx, dy, True)
            copies.append(push(self.sz_send, self.sz_recv.at[n], self.sems_two, len(copies), target))
        for copy in copies:
            copy.start()
        self.copies_two = copies

    def solve(self):
        g, i, k = self.here
        swide = self.swide
        swide[0, 6:14, 8:40, :] = self.source[...]
        for copy in self.copies_two:
            copy.wait_recv()
        for n, (dx, dy) in enumerate(CROSS_TWO):

            def store(to, row, rows):
                swide[1, to, row : row + rows.shape[0], :] = rows

            unpack_block(g, self.sz_recv[n], -dx, -dy, 6, store)
        row, lane = iota((48, 128), 0), iota((48, 128), 1)
        outside = ((k == 0) & (row < 8)) | ((k == 3) & (row >= 40))
        sixth = jnp.where(outside, 0.0, 1.0 / 6.0).astype(F32)
        sixths = (sixth, jnp.where((lane - 120 * g) >> 3 == 0, sixth, 0.0))

        def inside(x):
            out = ((i == 0) & (x < 6)) | ((i == 31) & (x >= 14))
            scale = jnp.where(out, 0.0, 1.0).astype(F32)
            return [one * scale for one in sixths]

        def first(x, carry):
            scale = inside(x)
            for t in range(2):
                self.p_a[t, x, 8:56, :] = -swide[t, x] * scale[t]
            return carry

        lax.fori_loop(0, 20, first, 0)
        old, new = self.p_a, self.p_b
        for sweep in range(1, 6):

            def relax(x, carry, old=old, new=new):
                scale = inside(x)
                right, left = along_z(old[0, x, 8:56, :], old[1, x, 8:56, :])
                for t in range(2):
                    total = old[t, x + 1, 8:56, :] + old[t, x - 1, 8:56, :]
                    total = total + old[t, x, 9:57, :] + old[t, x, 7:55, :]
                    total = total + right[t] + left[t]
                    new[t, x, 8:56, :] = (total - swide[t, x]) * scale[t]
                return carry

            lax.fori_loop(sweep, 20 - sweep, relax, 0)
            old, new = new, old
        p, prov = old, self.prov

        def project(x, carry):
            at = x + 6
            right, left = along_z(p[0, at, 16:48, :], p[1, at, 16:48, :])
            slope_z = right[0] - left[0]
            slope_x = p[0, at + 1, 16:48, :] - p[0, at - 1, 16:48, :]
            slope_y = p[0, at, 17:49, :] - p[0, at, 15:47, :]
            for c, slope in enumerate((slope_x, slope_y, slope_z)):
                self.velocity_next[c, x] = prov[c, 0, x + 2, 8:40, :] - 0.5 * slope
            self.pressure[x] = p[0, at, 16:48, :]
            return carry

        lax.fori_loop(0, 8, project, 0)

    def finish(self):
        for copy in self.copies_one + self.copies_two:
            copy.wait_send()


PATCH_SCRATCH = [pltpu.VMEM((16, 6144), F32), pltpu.VMEM((2048, 128), BF16)]


def make_fold(fold):
    row, col = iota((2048, 128), 0), iota((2048, 128), 1)
    hit = (row // 128 == col // 8) & (row % 8 == col % 8)
    fold[...] = hit.astype(F32).astype(BF16)


def pick_patches(field, selection, lines, fold, out):
    for c in range(3):
        for x in range(8):
            for py in range(4):
                combo = (c * 4 + x % 4) * 4 + py
                row = 8 * (x // 4)
                lines[row : row + 8, 128 * combo : 128 * combo + 128] = field[
                    c, x, pl.ds(py, 8, stride=4), :
                ]
    chosen = jnp.broadcast_to(selection[...], (16, 96))
    line = (chosen >> 4 == iota((16, 96), 0)).astype(F32).astype(BF16)
    cell = (chosen & 15 == iota((16, 96), 0)).astype(F32).astype(BF16)
    spread = ((iota((16, 2048), 1) & 127) >> 3 == iota((16, 2048), 0)).astype(F32).astype(BF16)
    here = matmul_tn(cell, spread)
    for part in range(3):
        source = lines[:, 2048 * part : 2048 * part + 2048].astype(BF16)
        rows = (matmul_tn(line, source) * here).astype(BF16)
        out[:, 128 * part : 128 * part + 128] = matmul(rows, fold[...]).astype(BF16)


def trainer_targets(here):
    g, i, k = here
    x, y, c = lax.div(i, 8), lax.rem(lax.div(i, 2), 4), lax.rem(i, 2)
    out = [(g, i, lax.rem(k + d, 4)) for d in (1, 2, 3)]
    out += [(g, lax.rem(x + d, 4) * 8 + y * 2 + c, k) for d in (1, 2, 3)]
    out += [(g, x * 8 + lax.rem(y + d, 4) * 2 + c, k) for d in (1, 2, 3)]
    return out + [(g, x * 8 + y * 2 + 1 - c, k), (1 - g, i, k)]


class Scatter:
    @staticmethod
    def scratch(rows, width, wire):
        return [
            pltpu.VMEM((2, 4, 4, 2, rows, width), F32),
            pltpu.VMEM((2, 4, 4, rows, width), F32),
            pltpu.VMEM((2, 4, 4, rows, width), wire),
            pltpu.VMEM((2, 4, 4, rows, width), wire),
            pltpu.VMEM((2, 4, rows, width), F32),
            pltpu.VMEM((2, 4, rows, width), F32),
            pltpu.VMEM((2, rows, width), F32),
            pltpu.VMEM((rows, width), F32),
            pltpu.SemaphoreType.DMA((2, 8)),
            pltpu.SemaphoreType.DMA((2, 8)),
            pltpu.SemaphoreType.DMA((2, 8)),
            pltpu.SemaphoreType.DMA((2, 1)),
        ]

    def __init__(self, here, refs, wire):
        g, i, k = here
        self.here, self.wire = here, wire
        self.x, self.y, self.c = lax.div(i, 8), lax.rem(lax.div(i, 2), 4), lax.rem(i, 2)
        (
            self.parts, self.core_recv, self.one_send, self.one_recv, self.one_sum,
            self.two_recv, self.two_sum, self.three_recv,
            self.core_sems, self.one_sems, self.two_sems, self.three_sems,
        ) = refs
        self.one, self.two = ([], []), ([], [])

    def along(self, on_x, d):
        g, i, k = self.here
        x, y = self.x, self.y
        if on_x:
            x = lax.rem(x + d, 4)
        else:
            y = lax.rem(y + d, 4)
        return (g, x * 8 + y * 2 + self.c, k)

    def core_copy(self, chunk):
        g, i, k = self.here
        half, x = lax.div(chunk, 4), lax.rem(chunk, 4)
        return push(
            self.parts.at[half, x, :, 1 - self.c],
            self.core_recv.at[half, x],
            self.core_sems,
            chunk,
            (g, self.x * 8 + self.y * 2 + 1 - self.c, k),
        )

    def start_core(self, chunk):
        self.core_copy(jnp.int32(chunk)).start()

    def first(self, half):
        for chunk in range(4 * half, 4 * half + 4):
            self.core_copy(jnp.int32(chunk)).wait_recv()
        mine = self.y if half else self.x
        for d in (2, 1, 3, 0):
            to = lax.rem(mine + d, 4)
            if half:
                total = self.parts[half, :, to, self.c] + self.core_recv[half, :, to]
            else:
                total = self.parts[half, to, :, self.c] + self.core_recv[half, to]
            if d == 0:
                self.one_sum[half] = total
            else:
                self.one_send[half, d] = total.astype(self.wire)
                copy = push(
                    self.one_send.at[half, d], self.one_recv.at[half, d], self.one_sems,
                    4 * half + d, self.along(not half, d),
                )
                copy.start()
                self.one[half].append(copy)

    def second(self, half):
        for copy in self.one[half]:
            copy.wait_recv()
        total = self.one_sum[half]
        for d in (1, 2, 3):
            total = total + self.one_recv[half, d].astype(F32)
        self.one_sum[half] = total
        mine = self.x if half else self.y
        for d in (2, 1, 3):
            copy = push(
                self.one_sum.at[half, lax.rem(mine + d, 4)], self.two_recv.at[half, d],
                self.two_sems, 4 * half + d, self.along(half, d),
            )
            copy.start()
            self.two[half].append(copy)

    def third(self):
        g, i, k = self.here
        for half in (0, 1):
            mine = self.x if half else self.y
            for copy in self.two[half]:
                copy.wait_recv()
            total = self.one_sum[half, mine]
            for d in (1, 2, 3):
                total = total + self.two_recv[half, d]
            self.two_sum[half] = total
        self.three = push(
            self.two_sum.at[1 - g], self.three_recv, self.three_sems, 0, (1 - g, i, k)
        )
        self.three.start()

    def result(self):
        self.three.wait_recv()
        return self.two_sum[self.here[0]] + self.three_recv[...]

    def finish(self):
        for chunk in range(8):
            self.core_copy(jnp.int32(chunk)).wait_send()
        for copy in self.one[0] + self.one[1] + self.two[0] + self.two[1] + [self.three]:
            copy.wait_send()


N_SCATTER = 12
TRAINER_SCRATCH = [
    pltpu.VMEM((384, 1024), BF16),
    pltpu.VMEM((1024, 1024), BF16),
    pltpu.VMEM((1024, 1024), BF16),
    pltpu.VMEM((1024, 384), BF16),
    pltpu.VMEM((96, 384), BF16),
    pltpu.VMEM((4, 96, 384), BF16),
    pltpu.VMEM((4, 96, 384), BF16),
    pltpu.VMEM((4, 96, 1024), BF16),
    pltpu.VMEM((4, 96, 1024), F32),
    pltpu.VMEM((4, 96, 1024), BF16),
    pltpu.VMEM((4, 96, 1024), BF16),
    pltpu.VMEM((96, 384), F32),
    pltpu.VMEM((4, 96, 384), BF16),
    pltpu.VMEM((4, 96, 384), BF16),
    pltpu.VMEM((384, 1024), BF16),
    pltpu.VMEM((384, 1024), BF16),
    pltpu.VMEM((384, 1024), F32),
    pltpu.VMEM((384, 1024), BF16),
    pltpu.VMEM((4, 8, 384), F32),
    pltpu.VMEM((4, 8, 384), F32),
    pltpu.SemaphoreType.DMA((6,)),
    pltpu.SemaphoreType.DMA((2, 4)),
    pltpu.SemaphoreType.DMA((2, 4)),
    pltpu.SemaphoreType.DMA((2, 4)),
    pltpu.SemaphoreType.DMA((2, 4)),
]
N_TRAINER = len(TRAINER_SCRATCH)
for _width in (1024, 1024, 384, 384):
    TRAINER_SCRATCH += Scatter.scratch(16, _width, BF16)


def columns(n):
    return pl.ds(pl.multiple_of(n * 256, 256), 256)


def step_kernel(
    velocity, viscosity, selection, w_in_far, w_up_far, w_down_far, w_out_far,
    velocity_next, pressure, out_up, out_down, out_small, lines, fold, *refs
):
    here = place()
    g, i, k = here
    n_stencil = len(Stencil.scratch)
    step = Stencil(here, velocity_next, pressure, refs[:n_stencil])
    refs = refs[n_stencil:]
    (
        w_in, w_up, w_down, w_out, targets, in_all, err_all, lifted_b, slope, active, mixed,
        own_predicted, down_send, down_recv, back_b, back_raised, lift_sum, lift_b, tail_send, tail_recv,
        near_sems, in_sems, down_sems, err_sems, tail_sems,
    ) = refs[:N_TRAINER]
    refs = refs[N_TRAINER:]
    up, down, grad_in, grad_out = (
        Scatter(here, refs[n * N_SCATTER : (n + 1) * N_SCATTER], BF16) for n in range(4)
    )
    sent = []

    def peer(d):
        return (g, i, lax.rem(k + d, 4))

    def start(copies):
        for copy in copies:
            copy.start()
        sent.extend(copies)
        return copies

    met = stencil_targets(here) + trainer_targets(here)
    greet(met)
    near = [
        pltpu.make_async_copy(src, dst, near_sems.at[n])
        for n, (src, dst) in enumerate(
            (
                (velocity, step.fields.at[0:3]),
                (viscosity, step.fields.at[3]),
                (w_in_far, w_in),
                (w_up_far, w_up),
                (w_down_far, w_down),
                (w_out_far, w_out),
            )
        )
    ]
    for copy in near:
        copy.start()
    make_fold(fold)
    for copy in near[:2]:
        copy.wait()
    pick_patches(step.fields, selection, lines, fold, in_all.at[k])
    step.prepare()
    greeted(met)
    in_copies = start(
        [push(in_all.at[k], in_all.at[k], in_sems, d, peer(d)) for d in (2, 1, 3)]
    )
    step.send_one()
    for copy in near[2:]:
        copy.wait()

    def forward(owner, own):
        rows = in_all[owner]
        lifted = matmul(rows, w_in[...])
        lifted_b[owner] = lifted.astype(BF16)

        def raise_(n, carry):
            at = columns(n)
            raised = matmul(lifted_b[owner], w_up[:, at])
            sigmoid = jax.nn.sigmoid(raised)
            active[owner, :, at] = (raised * sigmoid).astype(BF16)
            slope[owner, :, at] = sigmoid * (1.0 + raised * (1.0 - sigmoid))
            return carry

        lax.fori_loop(0, 4, raise_, 0)
        part = matmul(active[owner], w_down[...])
        mixed[owner] = (lifted + part if own else part).astype(BF16)
        return matmul(mixed[owner], w_out[...])

    own_predicted[...] = forward(k, True)
    step.make_source()
    step.send_two()
    down_copies = []
    for copy, d in zip(in_copies[1:] + in_copies[:1], (3, 1, 2)):
        copy.wait_recv()
        down_send[d] = forward(lax.rem(k + d, 4), False).astype(BF16)
        down_copies += start([push(down_send.at[d], down_recv.at[d], down_sems, d, peer(d))])
    step.solve()
    pick_patches(velocity_next, selection, lines, fold, targets)

    for copy in down_copies:
        copy.wait_recv()
    predicted = own_predicted[...]
    for d in (1, 2, 3):
        predicted = predicted + down_recv[d].astype(F32)
    scale = float(24576) ** (-0.5)
    err_all[k] = ((predicted - targets[...].astype(F32)) * scale).astype(BF16)
    err_copies = start(
        [push(err_all.at[k], err_all.at[k], err_sems, d, peer(d)) for d in (2, 1, 3)]
    )
    for copy in err_copies:
        copy.wait_recv()
    errors = err_all[...].reshape(384, 384)

    def grad_chunk(scatter, half, left, right, width):
        def chunk(n, carry):
            at = pl.ds(pl.multiple_of(n * 128, 128), 128)
            block = matmul_tn(left[:, at], right)
            scatter.parts[half, n - 4 * half] = block.reshape(4, 2, 16, width)
            scatter.start_core(n)
            return carry

        lax.fori_loop(4 * half, 4 * half + 4, chunk, 0)

    def back(n, carry):
        at = columns(n)
        both = matmul_nt(errors, w_out[at, :])
        back_b[:, at] = both.astype(BF16)
        lift_sum[:, at] = both
        return carry

    lax.fori_loop(0, 4, back, 0)

    def back_up(n, carry):
        at = columns(n)
        steep = slope[:, :, at].reshape(384, 256)
        back_raised[:, at] = (matmul_nt(back_b[...], w_down[at, :]) * steep).astype(BF16)
        return carry

    lax.fori_loop(0, 4, back_up, 0)
    lifted_rows = lifted_b.reshape(384, 1024)
    mixed_rows = mixed.reshape(384, 1024)
    raised_rows = back_raised[...]
    grad_chunk(up, 0, lifted_rows, raised_rows, 1024)
    grad_chunk(up, 1, lifted_rows, raised_rows, 1024)
    up.first(0)
    grad_chunk(grad_out, 0, mixed_rows, errors, 384)
    grad_chunk(grad_out, 1, mixed_rows, errors, 384)
    up.first(1)
    own_row = iota((384, 256), 0) // 96 == k

    def back_lift(n, carry):
        at = columns(n)
        mine = jnp.where(own_row, lift_sum[:, at], 0.0)
        lift_b[:, at] = (mine + matmul_nt(raised_rows, w_up[at, :])).astype(BF16)
        return carry

    lax.fori_loop(0, 4, back_lift, 0)
    grad_out.first(0)
    grad_out.first(1)
    rows_in = in_all[...].reshape(384, 384)
    grad_chunk(grad_in, 0, lift_b, rows_in, 384)
    grad_chunk(grad_in, 1, lift_b, rows_in, 384)
    active_rows = active[...].reshape(384, 1024)
    grad_chunk(down, 0, back_b, active_rows, 1024)
    grad_in.first(0)
    grad_in.first(1)
    grad_chunk(down, 1, back_b, active_rows, 1024)
    down.first(0)
    down.first(1)
    scatters = (up, grad_out, grad_in, down)
    for scatter in scatters:
        scatter.second(0)
        scatter.second(1)
    for scatter in scatters:
        scatter.third()
    last_in, last_out = grad_in.result(), grad_out.result()
    for j in range(4):
        tail_send[j, 0:4] = last_in[4 * j : 4 * j + 4]
        tail_send[j, 4:8] = last_out[4 * j : 4 * j + 4]
    tail_copies = start(
        [
            push(tail_send.at[lax.rem(k + d, 4)], tail_recv.at[d], tail_sems, d, peer(d))
            for d in (2, 1, 3)
        ]
    )
    out_down[...] = down.result()
    out_up[...] = up.result()
    for copy in tail_copies:
        copy.wait_recv()
    out_small[...] = tail_send[k] + tail_recv[1] + tail_recv[2] + tail_recv[3]
    for copy in sent:
        copy.wait_send()
    step.finish()
    for scatter in scatters:
        scatter.finish()


def emit_kernel(
    near_next, near_pressure, near_up, near_down, near_small,
    velocity_next, pressure, grad_up, grad_down, first, second,
):
    velocity_next[...] = near_next[...]
    pressure[...] = near_pressure[...]
    grad_up[...] = near_up[...]
    grad_down[...] = near_down[...]
    first[...] = near_small[0:4]
    second[...] = near_small[4:8]


def on_device(velocity, viscosity, selection, w_in, w_up, w_down, w_out):
    shape = jax.ShapeDtypeStruct
    far, near = pl.BlockSpec(memory_space=pl.ANY), pl.BlockSpec(memory_space=pltpu.VMEM)
    velocity_next, pressure, grad_up, grad_down, small = pl.pallas_call(
        step_kernel,
        out_shape=[
            shape((3, 8, 32, 128), F32),
            shape((8, 32, 128), F32),
            shape((16, 1024), F32),
            shape((16, 1024), F32),
            shape((8, 384), F32),
        ],
        in_specs=[far, far, near, far, far, far, far],
        out_specs=[near] * 5,
        scratch_shapes=PATCH_SCRATCH + Stencil.scratch + TRAINER_SCRATCH,
        compiler_params=pltpu.CompilerParams(
            collective_id=0, has_side_effects=True, vmem_limit_bytes=56 * MIB
        ),
        name="step",
    )(velocity, viscosity, selection.reshape(1, 96), w_in, w_up, w_down, w_out)
    velocity_next, pressure, grad_up, grad_down, first, second = pl.pallas_call(
        emit_kernel,
        out_shape=[
            shape((3, 8, 32, 128), F32),
            shape((8, 32, 128), F32),
            shape((16, 1024), F32),
            shape((16, 1024), F32),
            shape((4, 384), F32),
            shape((4, 384), F32),
        ],
        in_specs=[near] * 5,
        out_specs=[near] * 6,
        compiler_params=pltpu.CompilerParams(vmem_limit_bytes=60 * MIB),
        name="emit",
    )(velocity_next, pressure, grad_up, grad_down, small)
    return (velocity_next, pressure, first.T, grad_up, grad_down.T, second)


def solution(mesh):
    placed = (
        P(None, "gx", "gy", "grp"),
        P("gx", "gy", "grp"),
        P("grp", "gx", "gy", None),
        P(),
        P(None, "gy"),
        P("gy", None),
        P(),
    )
    return jax.shard_map(
        on_device,
        mesh=mesh,
        in_specs=placed,
        out_specs=(
            P(None, "gx", "gy", "grp"),
            P("gx", "gy", "grp"),
            P(None, ("grp", "gx", "gy")),
            P(("grp", "gx"), "gy"),
            P("gy", ("grp", "gx")),
            P(("grp", "gx", "gy"), None),
        ),
        check_vma=False,
    )
```

```python
import jax
import jax.numpy as jnp
from jax import lax
from jax.experimental import pallas as pl
from jax.experimental.pallas import tpu as pltpu
from jax.sharding import PartitionSpec as P

F32 = jnp.float32
BF16 = jnp.bfloat16
MESH = pl.DeviceIdType.MESH
MIB = 1 << 20

FACES = [(1, 0), (-1, 0), (0, 1), (0, -1)]
DIAGONALS = [(1, 1), (1, -1), (-1, 1), (-1, -1)]
PLANE = FACES + DIAGONALS
CROSS_ONE = [(0, 0)] + FACES
CROSS_TWO = [(0, 0)] + PLANE
EDGE_ORDER = (1, 2, 0, 3)


def place():
    return lax.axis_index("grp"), lax.axis_index("gx"), lax.axis_index("gy")


def push(src, dst, sems, slot, target):
    return pltpu.make_async_remote_copy(
        src_ref=src,
        dst_ref=dst,
        send_sem=sems.at[0, slot],
        recv_sem=sems.at[1, slot],
        device_id=target,
        device_id_type=MESH,
    )


def greet(targets):
    barrier = pltpu.get_barrier_semaphore()
    for target in targets:
        pl.semaphore_signal(barrier, inc=1, device_id=target, device_id_type=MESH)


def greeted(targets):
    pl.semaphore_wait(pltpu.get_barrier_semaphore(), len(targets))


def matmul(a, b):
    return jnp.dot(a, b, preferred_element_type=F32)


def matmul_nt(a, b):
    return lax.dot_general(a, b, (((1,), (1,)), ((), ())), preferred_element_type=F32)


def matmul_tn(a, b):
    return lax.dot_general(a, b, (((0,), (0,)), ((), ())), preferred_element_type=F32)


def iota(shape, dim):
    return lax.broadcasted_iota(jnp.int32, shape, dim)


def offset(here, dx, dy, flip):
    g, i, k = here
    return (1 - g if flip else g, lax.rem(i + dx + 32, 32), lax.rem(k + dy + 4, 4))


def stencil_targets(here):
    return [offset(here, dx, dy, False) for dx, dy in PLANE] + [
        offset(here, dx, dy, True) for dx, dy in CROSS_TWO
    ]


def pack_edge(g, group):
    lane = iota((16, 128), 1) // 8
    packed = jnp.zeros((16, 128), F32)
    for part in range(16):
        moved = pltpu.roll(group(part), lax.rem(8 * part + 8 * (1 - g), 128), 1)
        packed = jnp.where(lane == part, moved, packed)
    return packed


def unpack_edge(g, packed, part):
    lane = iota((16, 128), 1)
    rows = pltpu.roll(packed, lax.rem(128 - 8 * part + 120 * g, 128), 1)
    return jnp.where((lane - 120 * g) >> 3 == 0, rows, 0.0)


def unpack_block(g, packed, dx, dy, deep, store):
    planes = range(8) if dx == 0 else (range(8 - deep, 8) if dx < 0 else range(deep))
    for x in planes:
        to = deep + x if dx == 0 else (x - (8 - deep) if dx < 0 else deep + 8 + x)
        if dy == 0:
            store(to, 8, unpack_edge(g, packed, 2 * x))
            store(to, 24, unpack_edge(g, packed, 2 * x + 1))
        elif dy < 0:
            store(to, 0, unpack_edge(g, packed, 2 * x + 1)[8:16])
        else:
            store(to, 40, unpack_edge(g, packed, 2 * x)[0:8])


def along_z(own, other):
    lane = iota(own.shape, 1)
    own_r, other_r = pltpu.roll(own, 127, 1), pltpu.roll(other, 127, 1)
    own_l, other_l = pltpu.roll(own, 1, 1), pltpu.roll(other, 1, 1)
    last, first = lane == 127, lane == 0
    right = (jnp.where(last, other_r, own_r), jnp.where(last, own_r, other_r))
    left = (jnp.where(first, other_l, own_l), jnp.where(first, own_l, other_l))
    return right, left


def own_slices(dx, dy, deep, rows):
    xs = slice(0, 8) if dx == 0 else (slice(8 - deep, 8) if dx > 0 else slice(0, deep))
    ys = slice(0, 32) if dy == 0 else (slice(32 - rows, 32) if dy > 0 else slice(0, rows))
    return xs, ys


class Stencil:
    scratch = [
        pltpu.VMEM((4, 8, 32, 128), F32),
        pltpu.VMEM((2, 4, 8, 2, 128), F32),
        pltpu.VMEM((2, 4, 8, 2, 128), F32),
        pltpu.VMEM((4, 4, 2, 2, 128), F32),
        pltpu.VMEM((4, 16, 128), F32),
        pltpu.VMEM((5, 4, 16, 128), F32),
        pltpu.VMEM((4, 2, 12, 48, 128), F32),
        pltpu.VMEM((3, 2, 12, 48, 128), F32),
        pltpu.VMEM((8, 32, 128), F32),
        pltpu.VMEM((16, 128), F32),
        pltpu.VMEM((9, 16, 128), F32),
        pltpu.VMEM((2, 20, 48, 128), F32),
        pltpu.VMEM((2, 20, 64, 128), F32),
        pltpu.VMEM((2, 20, 64, 128), F32),
        pltpu.SemaphoreType.DMA((2, 13)),
        pltpu.SemaphoreType.DMA((2, 17)),
    ]

    def __init__(self, here, velocity_next, pressure, refs):
        self.here = here
        self.velocity_next, self.pressure = velocity_next, pressure
        (
            self.fields, self.y_send, self.y_recv, self.d_recv, self.z_send, self.z_recv,
            self.wide, self.prov, self.source, self.sz_send, self.sz_recv, self.swide,
            self.p_a, self.p_b, self.sems_one, self.sems_two,
        ) = refs

    def prepare(self):
        g = self.here[0]
        self.y_send[0] = self.fields[:, :, 30:32, :]
        self.y_send[1] = self.fields[:, :, 0:2, :]
        for f in range(4):
            self.z_send[EDGE_ORDER.index(f)] = pack_edge(
                g, lambda part: self.fields[f, part // 2, 16 * (part % 2) : 16 * (part % 2) + 16, :]
            )

    def send_one(self):
        g = self.here[0]
        copies = []
        for dx, dy in PLANE:
            slot = len(copies)
            target = offset(self.here, dx, dy, False)
            xs, _ = own_slices(dx, dy, 2, 2)
            if dy == 0:
                x_to = 0 if dx > 0 else 10
                src = self.fields.at[:, xs]
                dst = self.wide.at[:, 0, x_to : x_to + 2, 8:40, :]
            elif dx == 0:
                edge = 0 if dy > 0 else 1
                src, dst = self.y_send.at[edge], self.y_recv.at[edge]
            else:
                edge = 0 if dy > 0 else 1
                src, dst = self.y_send.at[edge, :, xs], self.d_recv.at[slot - 4]
            copies.append(push(src, dst, self.sems_one, slot, target))
        for n, (dx, dy) in enumerate(CROSS_ONE):
            target = offset(self.here, dx, dy, True)
            some = slice(1, 3) if dx else (slice(0, 2) if dy else slice(0, 4))
            src, dst = self.z_send.at[some], self.z_recv.at[n, some]
            copies.append(push(src, dst, self.sems_one, len(copies), target))
        for copy in copies:
            copy.start()
        self.copies_one = copies

    def make_source(self):
        g, i, k = self.here
        wide = self.wide
        wide[:, 0, 2:10, 8:40, :] = self.fields[...]
        for copy in self.copies_one:
            copy.wait_recv()
        wide[:, 0, 2:10, 6:8, :] = self.y_recv[0]
        wide[:, 0, 2:10, 40:42, :] = self.y_recv[1]
        for n, (dx, dy) in enumerate(DIAGONALS):
            x_to, y_to = (0 if dx > 0 else 10), (6 if dy > 0 else 40)
            wide[:, 0, x_to : x_to + 2, y_to : y_to + 2, :] = self.d_recv[n]
        for n, (dx, dy) in enumerate(CROSS_ONE):
            for f in (0, 1, 2, 3) if n == 0 else ((0, 2) if dx else (1, 2)):

                def store(to, row, rows, f=f):
                    wide[f, 1, to, row : row + rows.shape[0], :] = rows

                unpack_block(g, self.z_recv[n, EDGE_ORDER.index(f)], -dx, -dy, 2, store)

        @pl.when(i == 0)
        def _():
            wide[:, :, 0:2] = jnp.zeros((4, 2, 2, 48, 128), F32)

        @pl.when(i == 31)
        def _():
            wide[:, :, 10:12] = jnp.zeros((4, 2, 2, 48, 128), F32)

        @pl.when(k == 0)
        def _():
            wide[:, :, :, 0:8, :] = jnp.zeros((4, 2, 12, 8, 128), F32)

        @pl.when(k == 3)
        def _():
            wide[:, :, :, 40:48, :] = jnp.zeros((4, 2, 12, 8, 128), F32)

        def advance(c, x, top, bottom, tiles):
            mid = [wide[c, t, x, top:bottom, :] for t in range(2)]
            right, left = along_z(*mid)
            for t in tiles:
                total = wide[c, t, x + 1, top:bottom, :] + wide[c, t, x - 1, top:bottom, :]
                total = total + wide[c, t, x, top + 1 : bottom + 1, :]
                total = total + wide[c, t, x, top - 1 : bottom - 1, :]
                total = total + right[t] + left[t]
                after = mid[t] + wide[3, t, x, top:bottom, :] * (total - 6.0 * mid[t])
                self.prov[c, t, x, top:bottom, :] = after

        def provisional(x, carry):
            advance(0, x, 8, 40, (0,))
            advance(1, x, 7, 41, (0,))
            advance(2, x, 8, 40, (0, 1))
            return carry

        advance(0, 1, 8, 40, (0,))
        advance(0, 10, 8, 40, (0,))
        lax.fori_loop(2, 10, provisional, 0)
        prov = self.prov

        def source(x, carry):
            right, left = along_z(prov[2, 0, x, 8:40, :], prov[2, 1, x, 8:40, :])
            slope = right[0] - left[0]
            slope = slope + prov[0, 0, x + 1, 8:40, :] - prov[0, 0, x - 1, 8:40, :]
            slope = slope + prov[1, 0, x, 9:41, :] - prov[1, 0, x, 7:39, :]
            self.source[x - 2] = 0.5 * slope
            return carry

        lax.fori_loop(2, 10, source, 0)
        self.sz_send[...] = pack_edge(
            g, lambda part: self.source[part // 2, 16 * (part % 2) : 16 * (part % 2) + 16, :]
        )

    def send_two(self):
        g = self.here[0]
        copies = []
        for dx, dy in PLANE:
            target = offset(self.here, dx, dy, False)
            xs, ys = own_slices(dx, dy, 6, 8)
            x_to = 6 if dx == 0 else (0 if dx > 0 else 14)
            y_to = 8 if dy == 0 else (0 if dy > 0 else 40)
            dst = self.swide.at[
                0, x_to : x_to + xs.stop - xs.start, y_to : y_to + ys.stop - ys.start, :
            ]
            copies.append(push(self.source.at[xs, ys, :], dst, self.sems_two, len(copies), target))
        for n, (dx, dy) in enumerate(CROSS_TWO):
            target = offset(self.here, dx, dy, True)
            copies.append(push(self.sz_send, self.sz_recv.at[n], self.sems_two, len(copies), target))
        for copy in copies:
            copy.start()
        self.copies_two = copies

    def solve(self):
        g, i, k = self.here
        swide = self.swide
        swide[0, 6:14, 8:40, :] = self.source[...]
        for copy in self.copies_two:
            copy.wait_recv()
        for n, (dx, dy) in enumerate(CROSS_TWO):

            def store(to, row, rows):
                swide[1, to, row : row + rows.shape[0], :] = rows

            unpack_block(g, self.sz_recv[n], -dx, -dy, 6, store)
        row, lane = iota((48, 128), 0), iota((48, 128), 1)
        outside = ((k == 0) & (row < 8)) | ((k == 3) & (row >= 40))
        sixth = jnp.where(outside, 0.0, 1.0 / 6.0).astype(F32)
        sixths = (sixth, jnp.where((lane - 120 * g) >> 3 == 0, sixth, 0.0))

        def inside(x):
            out = ((i == 0) & (x < 6)) | ((i == 31) & (x >= 14))
            scale = jnp.where(out, 0.0, 1.0).astype(F32)
            return [one * scale for one in sixths]

        def first(x, carry):
            scale = inside(x)
            for t in range(2):
                self.p_a[t, x, 8:56, :] = -swide[t, x] * scale[t]
            return carry

        lax.fori_loop(0, 20, first, 0)
        old, new = self.p_a, self.p_b
        for sweep in range(1, 6):

            def relax(x, carry, old=old, new=new):
                scale = inside(x)
                right, left = along_z(old[0, x, 8:56, :], old[1, x, 8:56, :])
                for t in range(2):
                    total = old[t, x + 1, 8:56, :] + old[t, x - 1, 8:56, :]
                    total = total + old[t, x, 9:57, :] + old[t, x, 7:55, :]
                    total = total + right[t] + left[t]
                    new[t, x, 8:56, :] = (total - swide[t, x]) * scale[t]
                return carry

            lax.fori_loop(sweep, 20 - sweep, relax, 0)
            old, new = new, old
        p, prov = old, self.prov

        def project(x, carry):
            at = x + 6
            right, left = along_z(p[0, at, 16:48, :], p[1, at, 16:48, :])
            slope_z = right[0] - left[0]
            slope_x = p[0, at + 1, 16:48, :] - p[0, at - 1, 16:48, :]
            slope_y = p[0, at, 17:49, :] - p[0, at, 15:47, :]
            for c, slope in enumerate((slope_x, slope_y, slope_z)):
                self.velocity_next[c, x] = prov[c, 0, x + 2, 8:40, :] - 0.5 * slope
            self.pressure[x] = p[0, at, 16:48, :]
            return carry

        lax.fori_loop(0, 8, project, 0)

    def finish(self):
        for copy in self.copies_one + self.copies_two:
            copy.wait_send()


PATCH_SCRATCH = [pltpu.VMEM((16, 6144), F32), pltpu.VMEM((2048, 128), BF16)]


def make_fold(fold):
    row, col = iota((2048, 128), 0), iota((2048, 128), 1)
    hit = (row // 128 == col // 8) & (row % 8 == col % 8)
    fold[...] = hit.astype(F32).astype(BF16)


def pick_patches(field, selection, lines, fold, out):
    for c in range(3):
        for x in range(8):
            for py in range(4):
                combo = (c * 4 + x % 4) * 4 + py
                row = 8 * (x // 4)
                lines[row : row + 8, 128 * combo : 128 * combo + 128] = field[
                    c, x, pl.ds(py, 8, stride=4), :
                ]
    chosen = jnp.broadcast_to(selection[...], (16, 96))
    line = (chosen >> 4 == iota((16, 96), 0)).astype(F32).astype(BF16)
    cell = (chosen & 15 == iota((16, 96), 0)).astype(F32).astype(BF16)
    spread = ((iota((16, 2048), 1) & 127) >> 3 == iota((16, 2048), 0)).astype(F32).astype(BF16)
    here = matmul_tn(cell, spread)
    for part in range(3):
        source = lines[:, 2048 * part : 2048 * part + 2048].astype(BF16)
        rows = (matmul_tn(line, source) * here).astype(BF16)
        out[:, 128 * part : 128 * part + 128] = matmul(rows, fold[...]).astype(BF16)


def trainer_targets(here):
    g, i, k = here
    x, y, c = lax.div(i, 8), lax.rem(lax.div(i, 2), 4), lax.rem(i, 2)
    out = [(g, i, lax.rem(k + d, 4)) for d in (1, 2, 3)]
    out += [(g, lax.rem(x + d, 4) * 8 + y * 2 + c, k) for d in (1, 2, 3)]
    out += [(g, x * 8 + lax.rem(y + d, 4) * 2 + c, k) for d in (1, 2, 3)]
    out += [(g, lax.rem(x + d, 4) * 8 + y * 2 + 1 - c, k) for d in (1, 2, 3)]
    out += [(g, x * 8 + lax.rem(y + d, 4) * 2 + 1 - c, k) for d in (1, 2, 3)]
    return out + [(g, x * 8 + y * 2 + 1 - c, k), (1 - g, i, k)]


class Scatter:
    @staticmethod
    def scratch(rows, width, wire):
        return [
            pltpu.VMEM((2, 4, 4, 2, rows, width), F32),
            pltpu.VMEM((2, 4, 4, rows, width), F32),
            pltpu.VMEM((2, 4, 4, rows, width), wire),
            pltpu.VMEM((2, 4, 4, rows, width), wire),
            pltpu.VMEM((2, 4, rows, width), F32),
            pltpu.VMEM((2, 4, rows, width), wire),
            pltpu.VMEM((2, 4, rows, width), wire),
            pltpu.VMEM((2, rows, width), F32),
            pltpu.VMEM((rows, width), F32),
            pltpu.SemaphoreType.DMA((2, 8)),
            pltpu.SemaphoreType.DMA((2, 8)),
            pltpu.SemaphoreType.DMA((2, 8)),
            pltpu.SemaphoreType.DMA((2, 1)),
        ]

    def __init__(self, here, refs, wire):
        g, i, k = here
        self.here, self.wire = here, wire
        self.x, self.y, self.c = lax.div(i, 8), lax.rem(lax.div(i, 2), 4), lax.rem(i, 2)
        (
            self.parts, self.core_recv, self.one_send, self.one_recv, self.one_sum,
            self.two_send, self.two_recv, self.two_sum, self.three_recv,
            self.core_sems, self.one_sems, self.two_sems, self.three_sems,
        ) = refs
        self.one, self.two = ([], []), ([], [])

    def along(self, on_x, d):
        g, i, k = self.here
        x, y = self.x, self.y
        if on_x:
            x = lax.rem(x + d, 4)
        else:
            y = lax.rem(y + d, 4)
        return (g, x * 8 + y * 2 + self.c, k)

    def core_copy(self, chunk):
        g, i, k = self.here
        half, x = lax.div(chunk, 4), lax.rem(chunk, 4)
        return push(
            self.parts.at[half, x, :, 1 - self.c],
            self.core_recv.at[half, x],
            self.core_sems,
            chunk,
            (g, self.x * 8 + self.y * 2 + 1 - self.c, k),
        )

    def start_core(self, chunk):
        self.core_copy(chunk).start()

    def first(self, half):
        for chunk in range(4 * half, 4 * half + 4):
            self.core_copy(jnp.int32(chunk)).wait_recv()
        mine = self.y if half else self.x
        for d in (2, 1, 3, 0):
            to = lax.rem(mine + d, 4)
            if half:
                total = self.parts[half, :, to, self.c] + self.core_recv[half, :, to]
            else:
                total = self.parts[half, to, :, self.c] + self.core_recv[half, to]
            if d == 0:
                self.one_sum[half] = total
            else:
                self.one_send[half, d] = total.astype(self.wire)
                copy = push(
                    self.one_send.at[half, d], self.one_recv.at[half, d], self.one_sems,
                    4 * half + d, self.along(not half, d),
                )
                copy.start()
                self.one[half].append(copy)

    def second(self, half):
        for copy in self.one[half]:
            copy.wait_recv()
        total = self.one_sum[half]
        for d in (1, 2, 3):
            total = total + self.one_recv[half, d].astype(F32)
        self.one_sum[half] = total
        self.two_send[half] = total.astype(self.wire)
        mine = self.x if half else self.y
        for d in (2, 1, 3):
            copy = push(
                self.two_send.at[half, lax.rem(mine + d, 4)], self.two_recv.at[half, d],
                self.two_sems, 4 * half + d, self.along(half, d),
            )
            copy.start()
            self.two[half].append(copy)

    def third(self):
        g, i, k = self.here
        for half in (0, 1):
            mine = self.x if half else self.y
            for copy in self.two[half]:
                copy.wait_recv()
            total = self.one_sum[half, mine]
            for d in (1, 2, 3):
                total = total + self.two_recv[half, d].astype(F32)
            self.two_sum[half] = total
        self.three = push(
            self.two_sum.at[1 - g], self.three_recv, self.three_sems, 0, (1 - g, i, k)
        )
        self.three.start()

    def result(self):
        self.three.wait_recv()
        return self.two_sum[self.here[0]] + self.three_recv[...]

    def finish(self):
        for chunk in range(8):
            self.core_copy(jnp.int32(chunk)).wait_send()
        for copy in self.one[0] + self.one[1] + self.two[0] + self.two[1] + [self.three]:
            copy.wait_send()


class Product:
    scratch = [
        pltpu.VMEM((4, 2, 128, 384), F32),
        pltpu.VMEM((4, 128, 384), F32),
        pltpu.VMEM((4, 128, 384), BF16),
        pltpu.VMEM((4, 128, 384), BF16),
        pltpu.VMEM((128, 384), F32),
        pltpu.VMEM((2, 4, 4, 2, 16, 128), F32),
        pltpu.VMEM((4, 2, 4, 2, 16, 128), BF16),
        pltpu.VMEM((4, 2, 4, 2, 16, 128), BF16),
        pltpu.VMEM((2, 4, 2, 16, 128), F32),
        pltpu.VMEM((4, 2, 16, 128), F32),
        pltpu.VMEM((4, 2, 16, 128), F32),
        pltpu.VMEM((4, 2, 16, 128), F32),
        pltpu.SemaphoreType.DMA((2, 4)),
        pltpu.SemaphoreType.DMA((2, 4)),
        pltpu.SemaphoreType.DMA((2, 4)),
        pltpu.SemaphoreType.DMA((2, 1)),
        pltpu.SemaphoreType.DMA((2, 8)),
    ]

    def __init__(self, here, refs, on_x):
        g, i, k = here
        self.here, self.on_x = here, on_x
        self.x, self.y, self.c = lax.div(i, 8), lax.rem(lax.div(i, 2), 4), lax.rem(i, 2)
        self.mine, self.other = (self.x, self.y) if on_x else (self.y, self.x)
        (
            self.parts, self.core_recv, self.one_send, self.one_recv, self.one_sum, self.wide,
            self.two_send, self.two_recv, self.two_sum, self.three_recv, self.three_sum,
            self.four_recv, self.core_sems, self.one_sems, self.two_sems, self.three_sems,
            self.four_sems,
        ) = refs
        self.copies = []

    def target(self, first, second, core):
        g, i, k = self.here
        first, second = lax.rem(self.mine + first, 4), lax.rem(self.other + second, 4)
        x, y = (first, second) if self.on_x else (second, first)
        return (g, x * 8 + y * 2 + lax.rem(self.c + core, 2), k)

    def core_copy(self, chunk):
        return push(
            self.parts.at[chunk, 1 - self.c], self.core_recv.at[chunk], self.core_sems, chunk,
            self.target(0, 0, 1),
        )

    def start(self, copy):
        copy.start()
        self.copies.append(copy)
        return copy

    def fill(self, left, right):
        def chunk(n, carry):
            at = pl.ds(pl.multiple_of(n * 256, 256), 256)
            self.parts[n] = matmul_tn(left[:, at], right).reshape(2, 128, 384)
            self.core_copy(n).start()
            return carry

        lax.fori_loop(0, 4, chunk, 0)

    def first(self):
        for chunk in range(4):
            self.core_copy(jnp.int32(chunk)).wait_recv()
        self.one = []
        for d in (2, 1, 3, 0):
            to = lax.rem(self.mine + d, 4)
            total = self.parts[to, self.c] + self.core_recv[to]
            if d == 0:
                self.one_sum[...] = total
            else:
                self.one_send[d] = total.astype(BF16)
                copy = push(
                    self.one_send.at[d], self.one_recv.at[d], self.one_sems, d,
                    self.target(d, 0, 0),
                )
                self.one.append(self.start(copy))

    def own_rows(self, at):
        return self.wide[:, :, at] if self.on_x else self.wide[:, at]

    def second(self, weights):
        for copy in self.one:
            copy.wait_recv()
        total = self.one_sum[...]
        for d in (1, 2, 3):
            total = total + self.one_recv[d].astype(F32)
        high = total.astype(BF16)
        low = (total - high.astype(F32)).astype(BF16)
        product = matmul_nt(weights, high) + matmul_nt(weights, low)
        self.wide[...] = product.reshape(2, 4, 4, 2, 16, 128)
        self.two = []
        for d in (2, 1, 3):
            self.two_send[d] = self.own_rows(lax.rem(self.other + d, 4)).astype(BF16)
            copy = push(
                self.two_send.at[d], self.two_recv.at[d], self.two_sems, d, self.target(0, d, 0)
            )
            self.two.append(self.start(copy))

    def third(self):
        g, i, k = self.here
        for copy in self.two:
            copy.wait_recv()
        total = self.own_rows(self.other)
        for d in (1, 2, 3):
            total = total + self.two_recv[d].astype(F32)
        self.two_sum[...] = total
        self.three = self.start(
            push(self.two_sum.at[1 - g], self.three_recv, self.three_sems, 0, (1 - g, i, k))
        )

    def fourth(self):
        self.three.wait_recv()
        self.three_sum[...] = self.two_sum[self.here[0]] + self.three_recv[...]
        self.four = []
        for d, core in ((2, 0), (2, 1), (1, 0), (1, 1), (3, 0), (3, 1), (0, 1)):
            src = self.three_sum.at[lax.rem(self.mine + d, 4), lax.rem(self.c + core, 2)]
            copy = push(
                src, self.four_recv.at[self.mine, self.c], self.four_sems, 2 * d + core,
                self.target(d, 0, core),
            )
            self.four.append(self.start(copy))
        self.four_recv[self.mine, self.c] = self.three_sum[self.mine, self.c]

    def result(self, out):
        for copy in self.four:
            copy.wait_recv()
        for first in range(4):
            for core in range(2):
                at = 128 * (2 * first + core)
                out[:, at : at + 128] = self.four_recv[first, core]

    def finish(self):
        for chunk in range(4):
            self.core_copy(jnp.int32(chunk)).wait_send()
        for copy in self.copies:
            copy.wait_send()


N_SCATTER = 13
TRAINER_SCRATCH = [
    pltpu.VMEM((384, 1024), BF16),
    pltpu.VMEM((1024, 1024), BF16),
    pltpu.VMEM((1024, 1024), BF16),
    pltpu.VMEM((1024, 384), BF16),
    pltpu.VMEM((96, 384), BF16),
    pltpu.VMEM((4, 96, 384), BF16),
    pltpu.VMEM((4, 96, 384), BF16),
    pltpu.VMEM((96, 1024), BF16),
    pltpu.VMEM((4, 96, 1024), F32),
    pltpu.VMEM((4, 96, 1024), BF16),
    pltpu.VMEM((4, 96, 1024), BF16),
    pltpu.VMEM((96, 384), F32),
    pltpu.VMEM((4, 96, 384), BF16),
    pltpu.VMEM((4, 96, 384), BF16),
    pltpu.VMEM((4, 96, 1024), BF16),
    pltpu.VMEM((4, 96, 1024), BF16),
    pltpu.VMEM((96, 1024), BF16),
    pltpu.VMEM((96, 1024), F32),
    pltpu.VMEM((1024, 384), BF16),
    pltpu.VMEM((4, 8, 384), F32),
    pltpu.VMEM((4, 8, 384), F32),
    pltpu.SemaphoreType.DMA((6,)),
    pltpu.SemaphoreType.DMA((2, 4)),
    pltpu.SemaphoreType.DMA((2, 4)),
    pltpu.SemaphoreType.DMA((2, 4)),
    pltpu.SemaphoreType.DMA((2, 4)),
]
N_TRAINER = len(TRAINER_SCRATCH)
TRAINER_SCRATCH += Scatter.scratch(16, 384, BF16) * 2 + Product.scratch * 2


def columns(n):
    return pl.ds(pl.multiple_of(n * 256, 256), 256)


def step_kernel(
    velocity, viscosity, selection, w_in_far, w_up_far, w_down_far, w_out_far,
    velocity_next, pressure, out_up, out_down, out_small, lines, fold, *refs
):
    here = place()
    g, i, k = here
    n_stencil = len(Stencil.scratch)
    step = Stencil(here, velocity_next, pressure, refs[:n_stencil])
    refs = refs[n_stencil:]
    (
        w_in, w_up, w_down, w_out, targets, in_all, err_all, lifted_b, slope, active, mixed,
        own_predicted, down_send, down_recv, back_raised, lift_b, back_b, own_back, w_in_t, tail_send, tail_recv,
        near_sems, in_sems, down_sems, err_sems, tail_sems,
    ) = refs[:N_TRAINER]
    refs = refs[N_TRAINER:]
    grad_in, grad_out = (
        Scatter(here, refs[n * N_SCATTER : (n + 1) * N_SCATTER], BF16) for n in range(2)
    )
    refs = refs[2 * N_SCATTER :]
    up, down = (
        Product(here, refs[: len(Product.scratch)], True),
        Product(here, refs[len(Product.scratch) :], False),
    )
    sent = []

    def peer(d):
        return (g, i, lax.rem(k + d, 4))

    def start(copies):
        for copy in copies:
            copy.start()
        sent.extend(copies)
        return copies

    met = stencil_targets(here) + trainer_targets(here)
    greet(met)
    near = [
        pltpu.make_async_copy(src, dst, near_sems.at[n])
        for n, (src, dst) in enumerate(
            (
                (velocity, step.fields.at[0:3]),
                (viscosity, step.fields.at[3]),
                (w_in_far, w_in),
                (w_up_far, w_up),
                (w_down_far, w_down),
                (w_out_far, w_out),
            )
        )
    ]
    for copy in near:
        copy.start()
    make_fold(fold)
    for copy in near[:2]:
        copy.wait()
    pick_patches(step.fields, selection, lines, fold, in_all.at[k])
    step.prepare()
    greeted(met)
    step.send_one()
    in_copies = start(
        [push(in_all.at[k], in_all.at[k], in_sems, d, peer(d)) for d in (2, 1, 3)]
    )
    for copy in near[2:]:
        copy.wait()

    def forward(owner, own):
        rows = in_all[owner]
        lifted = matmul(rows, w_in[...])
        lifted_b[...] = lifted.astype(BF16)

        def raise_(n, carry):
            at = columns(n)
            raised = matmul(lifted_b[...], w_up[:, at])
            sigmoid = jax.nn.sigmoid(raised)
            active[owner, :, at] = (raised * sigmoid).astype(BF16)
            slope[owner, :, at] = sigmoid * (1.0 + raised * (1.0 - sigmoid))
            return carry

        lax.fori_loop(0, 4, raise_, 0)
        part = matmul(active[owner], w_down[...])
        mixed[owner] = (lifted + part if own else part).astype(BF16)
        return matmul(mixed[owner], w_out[...])

    own_predicted[...] = forward(k, True)
    w_in_t[...] = w_in[...].T
    step.make_source()
    step.send_two()
    down_copies = []
    for copy, d in zip(in_copies[1:] + in_copies[:1], (3, 1, 2)):
        copy.wait_recv()
        down_send[d] = forward(lax.rem(k + d, 4), False).astype(BF16)
        down_copies += start([push(down_send.at[d], down_recv.at[d], down_sems, d, peer(d))])
    step.solve()
    pick_patches(velocity_next, selection, lines, fold, targets)

    for copy in down_copies:
        copy.wait_recv()
    predicted = own_predicted[...]
    for d in (1, 2, 3):
        predicted = predicted + down_recv[d].astype(F32)
    scale = float(24576) ** (-0.5)
    err_all[k] = ((predicted - targets[...].astype(F32)) * scale).astype(BF16)
    err_copies = start(
        [push(err_all.at[k], err_all.at[k], err_sems, d, peer(d)) for d in (2, 1, 3)]
    )
    def backward(owner, own):
        errors = err_all[owner]

        def back(n, carry):
            at = columns(n)
            both = matmul_nt(errors, w_out[at, :])
            back_b[:, at] = both.astype(BF16)
            if own:
                own_back[:, at] = both
            return carry

        lax.fori_loop(0, 4, back, 0)

        def back_up(n, carry):
            at = columns(n)
            steep = matmul_nt(back_b[...], w_down[at, :])
            back_raised[owner, :, at] = (steep * slope[owner, :, at]).astype(BF16)
            return carry

        lax.fori_loop(0, 4, back_up, 0)

    def lift(owner, own):
        part = matmul_nt(back_raised[owner], w_up[...])
        lift_b[owner] = (part + own_back[...] if own else part).astype(BF16)

    backward(k, True)
    lift(k, True)
    for copy, d in zip(err_copies[1:], (3, 1)):
        copy.wait_recv()
        owner = lax.rem(k + d, 4)
        backward(owner, False)
        lift(owner, False)
    err_copies[0].wait_recv()
    owner = lax.rem(k + 2, 4)
    backward(owner, False)
    rows_in = in_all[...].reshape(384, 384)
    errors = err_all[...].reshape(384, 384)
    up.fill(back_raised.reshape(384, 1024), rows_in)
    down.fill(active.reshape(384, 1024), errors)

    def grad_chunk(scatter, left, right):
        def chunk(n, carry):
            at = pl.ds(pl.multiple_of(n * 256, 256), 256)
            block = matmul_tn(left[:, at], right).reshape(2, 4, 2, 16, 384)
            for part in range(2):
                scatter.parts[lax.div(n, 2), lax.rem(n, 2) * 2 + part] = block[part]
                scatter.start_core(n * 2 + part)
            return carry

        lax.fori_loop(0, 4, chunk, 0)

    lift(owner, False)
    up.first()
    grad_chunk(grad_in, lift_b.reshape(384, 1024), rows_in)
    down.first()
    grad_chunk(grad_out, mixed.reshape(384, 1024), errors)
    scatters = (grad_in, grad_out)
    for scatter in scatters:
        scatter.first(0)
        scatter.first(1)
    up.second(w_in_t[...])
    down.second(w_out[...])
    for scatter in scatters:
        scatter.second(0)
        scatter.second(1)
    up.third()
    down.third()
    for scatter in scatters:
        scatter.third()
    up.fourth()
    down.fourth()
    last_in, last_out = grad_in.result(), grad_out.result()
    for j in range(4):
        tail_send[j, 0:4] = last_in[4 * j : 4 * j + 4]
        tail_send[j, 4:8] = last_out[4 * j : 4 * j + 4]
    tail_copies = start(
        [
            push(tail_send.at[lax.rem(k + d, 4)], tail_recv.at[d], tail_sems, d, peer(d))
            for d in (2, 1, 3)
        ]
    )
    up.result(out_up)
    down.result(out_down)
    for copy in tail_copies:
        copy.wait_recv()
    out_small[...] = tail_send[k] + tail_recv[1] + tail_recv[2] + tail_recv[3]
    for copy in sent:
        copy.wait_send()
    step.finish()
    for scatter in scatters + (up, down):
        scatter.finish()


def emit_kernel(
    near_next, near_pressure, near_up, near_down, near_small,
    velocity_next, pressure, grad_up, grad_down, first, second,
):
    velocity_next[...] = near_next[...]
    pressure[...] = near_pressure[...]
    grad_up[...] = near_up[...]
    grad_down[...] = near_down[...]
    first[...] = near_small[0:4]
    second[...] = near_small[4:8]


def on_device(velocity, viscosity, selection, w_in, w_up, w_down, w_out):
    shape = jax.ShapeDtypeStruct
    far, near = pl.BlockSpec(memory_space=pl.ANY), pl.BlockSpec(memory_space=pltpu.VMEM)
    velocity_next, pressure, grad_up, grad_down, small = pl.pallas_call(
        step_kernel,
        out_shape=[
            shape((3, 8, 32, 128), F32),
            shape((8, 32, 128), F32),
            shape((16, 1024), F32),
            shape((16, 1024), F32),
            shape((8, 384), F32),
        ],
        in_specs=[far, far, near, far, far, far, far],
        out_specs=[near] * 5,
        scratch_shapes=PATCH_SCRATCH + Stencil.scratch + TRAINER_SCRATCH,
        compiler_params=pltpu.CompilerParams(
            collective_id=0, has_side_effects=True, vmem_limit_bytes=56 * MIB
        ),
        name="step",
    )(velocity, viscosity, selection.reshape(1, 96), w_in, w_up, w_down, w_out)
    velocity_next, pressure, grad_up, grad_down, first, second = pl.pallas_call(
        emit_kernel,
        out_shape=[
            shape((3, 8, 32, 128), F32),
            shape((8, 32, 128), F32),
            shape((16, 1024), F32),
            shape((16, 1024), F32),
            shape((4, 384), F32),
            shape((4, 384), F32),
        ],
        in_specs=[near] * 5,
        out_specs=[near] * 6,
        compiler_params=pltpu.CompilerParams(vmem_limit_bytes=60 * MIB),
        name="emit",
    )(velocity_next, pressure, grad_up, grad_down, small)
    return (velocity_next, pressure, first.T, grad_up, grad_down.T, second)


def solution(mesh):
    placed = (
        P(None, "gx", "gy", "grp"),
        P("gx", "gy", "grp"),
        P("grp", "gx", "gy", None),
        P(),
        P(None, "gy"),
        P("gy", None),
        P(),
    )
    return jax.shard_map(
        on_device,
        mesh=mesh,
        in_specs=placed,
        out_specs=(
            P(None, "gx", "gy", "grp"),
            P("gx", "gy", "grp"),
            P(None, ("grp", "gx", "gy")),
            P(("grp", "gx"), "gy"),
            P("gy", ("grp", "gx")),
            P(("grp", "gx", "gy"), None),
        ),
        check_vma=False,
    )
```

```python
import jax
import jax.numpy as jnp
from jax import lax
from jax.experimental import pallas as pl
from jax.experimental.pallas import tpu as pltpu
from jax.sharding import PartitionSpec as P

F32 = jnp.float32
BF16 = jnp.bfloat16
MESH = pl.DeviceIdType.MESH
MIB = 1 << 20

FACES = [(1, 0), (-1, 0), (0, 1), (0, -1)]
DIAGONALS = [(1, 1), (1, -1), (-1, 1), (-1, -1)]
PLANE = FACES + DIAGONALS
CROSS_ONE = [(0, 0)] + FACES
CROSS_TWO = [(0, 0)] + PLANE
EDGE_ORDER = (1, 2, 0, 3)


def place():
    return lax.axis_index("grp"), lax.axis_index("gx"), lax.axis_index("gy")


def push(src, dst, sems, slot, target):
    return pltpu.make_async_remote_copy(
        src_ref=src,
        dst_ref=dst,
        send_sem=sems.at[0, slot],
        recv_sem=sems.at[1, slot],
        device_id=target,
        device_id_type=MESH,
    )


def greet(targets):
    barrier = pltpu.get_barrier_semaphore()
    for target in targets:
        pl.semaphore_signal(barrier, inc=1, device_id=target, device_id_type=MESH)


def greeted(targets):
    pl.semaphore_wait(pltpu.get_barrier_semaphore(), len(targets))


def matmul(a, b):
    return jnp.dot(a, b, preferred_element_type=F32)


def matmul_nt(a, b):
    return lax.dot_general(a, b, (((1,), (1,)), ((), ())), preferred_element_type=F32)


def matmul_tn(a, b):
    return lax.dot_general(a, b, (((0,), (0,)), ((), ())), preferred_element_type=F32)


def iota(shape, dim):
    return lax.broadcasted_iota(jnp.int32, shape, dim)


def offset(here, dx, dy, flip):
    g, i, k = here
    return (1 - g if flip else g, lax.rem(i + dx + 32, 32), lax.rem(k + dy + 4, 4))


def stencil_targets(here):
    return [offset(here, dx, dy, False) for dx, dy in PLANE] + [
        offset(here, dx, dy, True) for dx, dy in CROSS_TWO
    ]


def pack_edge(g, group):
    lane = iota((16, 128), 1) // 8
    packed = jnp.zeros((16, 128), F32)
    for part in range(16):
        moved = pltpu.roll(group(part), lax.rem(8 * part + 8 * (1 - g), 128), 1)
        packed = jnp.where(lane == part, moved, packed)
    return packed


def unpack_edge(g, packed, part):
    lane = iota((16, 128), 1)
    rows = pltpu.roll(packed, lax.rem(128 - 8 * part + 120 * g, 128), 1)
    return jnp.where((lane - 120 * g) >> 3 == 0, rows, 0.0)


def unpack_block(g, packed, dx, dy, deep, store):
    planes = range(8) if dx == 0 else (range(8 - deep, 8) if dx < 0 else range(deep))
    for x in planes:
        to = deep + x if dx == 0 else (x - (8 - deep) if dx < 0 else deep + 8 + x)
        if dy == 0:
            store(to, 8, unpack_edge(g, packed, 2 * x))
            store(to, 24, unpack_edge(g, packed, 2 * x + 1))
        elif dy < 0:
            store(to, 0, unpack_edge(g, packed, 2 * x + 1)[8:16])
        else:
            store(to, 40, unpack_edge(g, packed, 2 * x)[0:8])


def along_z(own, other):
    lane = iota(own.shape, 1)
    own_r, other_r = pltpu.roll(own, 127, 1), pltpu.roll(other, 127, 1)
    own_l, other_l = pltpu.roll(own, 1, 1), pltpu.roll(other, 1, 1)
    last, first = lane == 127, lane == 0
    right = (jnp.where(last, other_r, own_r), jnp.where(last, own_r, other_r))
    left = (jnp.where(first, other_l, own_l), jnp.where(first, own_l, other_l))
    return right, left


def own_slices(dx, dy, deep, rows):
    xs = slice(0, 8) if dx == 0 else (slice(8 - deep, 8) if dx > 0 else slice(0, deep))
    ys = slice(0, 32) if dy == 0 else (slice(32 - rows, 32) if dy > 0 else slice(0, rows))
    return xs, ys


class Stencil:
    scratch = [
        pltpu.VMEM((4, 8, 32, 128), F32),
        pltpu.VMEM((2, 4, 8, 2, 128), F32),
        pltpu.VMEM((2, 4, 8, 2, 128), F32),
        pltpu.VMEM((4, 4, 2, 2, 128), F32),
        pltpu.VMEM((4, 16, 128), F32),
        pltpu.VMEM((5, 4, 16, 128), F32),
        pltpu.VMEM((4, 2, 12, 48, 128), F32),
        pltpu.VMEM((3, 2, 12, 48, 128), F32),
        pltpu.VMEM((8, 32, 128), F32),
        pltpu.VMEM((16, 128), F32),
        pltpu.VMEM((9, 16, 128), F32),
        pltpu.VMEM((2, 20, 48, 128), F32),
        pltpu.VMEM((2, 20, 64, 128), F32),
        pltpu.VMEM((2, 20, 64, 128), F32),
        pltpu.SemaphoreType.DMA((2, 13)),
        pltpu.SemaphoreType.DMA((2, 17)),
    ]

    def __init__(self, here, velocity_next, pressure, refs):
        self.here = here
        self.velocity_next, self.pressure = velocity_next, pressure
        (
            self.fields, self.y_send, self.y_recv, self.d_recv, self.z_send, self.z_recv,
            self.wide, self.prov, self.source, self.sz_send, self.sz_recv, self.swide,
            self.p_a, self.p_b, self.sems_one, self.sems_two,
        ) = refs

    def prepare(self):
        g = self.here[0]
        self.y_send[0] = self.fields[:, :, 30:32, :]
        self.y_send[1] = self.fields[:, :, 0:2, :]
        for f in range(4):
            self.z_send[EDGE_ORDER.index(f)] = pack_edge(
                g, lambda part: self.fields[f, part // 2, 16 * (part % 2) : 16 * (part % 2) + 16, :]
            )

    def send_one(self):
        g = self.here[0]
        copies = []
        for dx, dy in PLANE:
            slot = len(copies)
            target = offset(self.here, dx, dy, False)
            xs, _ = own_slices(dx, dy, 2, 2)
            if dy == 0:
                x_to = 0 if dx > 0 else 10
                src = self.fields.at[:, xs]
                dst = self.wide.at[:, 0, x_to : x_to + 2, 8:40, :]
            elif dx == 0:
                edge = 0 if dy > 0 else 1
                src, dst = self.y_send.at[edge], self.y_recv.at[edge]
            else:
                edge = 0 if dy > 0 else 1
                src, dst = self.y_send.at[edge, :, xs], self.d_recv.at[slot - 4]
            copies.append(push(src, dst, self.sems_one, slot, target))
        for n, (dx, dy) in enumerate(CROSS_ONE):
            target = offset(self.here, dx, dy, True)
            some = slice(1, 3) if dx else (slice(0, 2) if dy else slice(0, 4))
            src, dst = self.z_send.at[some], self.z_recv.at[n, some]
            copies.append(push(src, dst, self.sems_one, len(copies), target))
        for copy in copies:
            copy.start()
        self.copies_one = copies

    def make_source(self):
        g, i, k = self.here
        wide = self.wide
        wide[:, 0, 2:10, 8:40, :] = self.fields[...]
        for copy in self.copies_one:
            copy.wait_recv()
        wide[:, 0, 2:10, 6:8, :] = self.y_recv[0]
        wide[:, 0, 2:10, 40:42, :] = self.y_recv[1]
        for n, (dx, dy) in enumerate(DIAGONALS):
            x_to, y_to = (0 if dx > 0 else 10), (6 if dy > 0 else 40)
            wide[:, 0, x_to : x_to + 2, y_to : y_to + 2, :] = self.d_recv[n]
        for n, (dx, dy) in enumerate(CROSS_ONE):
            for f in (0, 1, 2, 3) if n == 0 else ((0, 2) if dx else (1, 2)):

                def store(to, row, rows, f=f):
                    wide[f, 1, to, row : row + rows.shape[0], :] = rows

                unpack_block(g, self.z_recv[n, EDGE_ORDER.index(f)], -dx, -dy, 2, store)

        @pl.when(i == 0)
        def _():
            wide[:, :, 0:2] = jnp.zeros((4, 2, 2, 48, 128), F32)

        @pl.when(i == 31)
        def _():
            wide[:, :, 10:12] = jnp.zeros((4, 2, 2, 48, 128), F32)

        @pl.when(k == 0)
        def _():
            wide[:, :, :, 0:8, :] = jnp.zeros((4, 2, 12, 8, 128), F32)

        @pl.when(k == 3)
        def _():
            wide[:, :, :, 40:48, :] = jnp.zeros((4, 2, 12, 8, 128), F32)

        def advance(c, x, top, bottom, tiles):
            mid = [wide[c, t, x, top:bottom, :] for t in range(2)]
            right, left = along_z(*mid)
            for t in tiles:
                total = wide[c, t, x + 1, top:bottom, :] + wide[c, t, x - 1, top:bottom, :]
                total = total + wide[c, t, x, top + 1 : bottom + 1, :]
                total = total + wide[c, t, x, top - 1 : bottom - 1, :]
                total = total + right[t] + left[t]
                after = mid[t] + wide[3, t, x, top:bottom, :] * (total - 6.0 * mid[t])
                self.prov[c, t, x, top:bottom, :] = after

        def provisional(x, carry):
            advance(0, x, 8, 40, (0,))
            advance(1, x, 7, 41, (0,))
            advance(2, x, 8, 40, (0, 1))
            return carry

        advance(0, 1, 8, 40, (0,))
        advance(0, 10, 8, 40, (0,))
        lax.fori_loop(2, 10, provisional, 0)
        prov = self.prov

        def source(x, carry):
            right, left = along_z(prov[2, 0, x, 8:40, :], prov[2, 1, x, 8:40, :])
            slope = right[0] - left[0]
            slope = slope + prov[0, 0, x + 1, 8:40, :] - prov[0, 0, x - 1, 8:40, :]
            slope = slope + prov[1, 0, x, 9:41, :] - prov[1, 0, x, 7:39, :]
            self.source[x - 2] = 0.5 * slope
            return carry

        lax.fori_loop(2, 10, source, 0)
        self.sz_send[...] = pack_edge(
            g, lambda part: self.source[part // 2, 16 * (part % 2) : 16 * (part % 2) + 16, :]
        )

    def send_two(self):
        g = self.here[0]
        copies = []
        for dx, dy in PLANE:
            target = offset(self.here, dx, dy, False)
            xs, ys = own_slices(dx, dy, 6, 8)
            x_to = 6 if dx == 0 else (0 if dx > 0 else 14)
            y_to = 8 if dy == 0 else (0 if dy > 0 else 40)
            dst = self.swide.at[
                0, x_to : x_to + xs.stop - xs.start, y_to : y_to + ys.stop - ys.start, :
            ]
            copies.append(push(self.source.at[xs, ys, :], dst, self.sems_two, len(copies), target))
        for n, (dx, dy) in enumerate(CROSS_TWO):
            target = offset(self.here, dx, dy, True)
            copies.append(push(self.sz_send, self.sz_recv.at[n], self.sems_two, len(copies), target))
        for copy in copies:
            copy.start()
        self.copies_two = copies

    def solve(self):
        g, i, k = self.here
        swide = self.swide
        swide[0, 6:14, 8:40, :] = self.source[...]
        for copy in self.copies_two:
            copy.wait_recv()
        for n, (dx, dy) in enumerate(CROSS_TWO):

            def store(to, row, rows):
                swide[1, to, row : row + rows.shape[0], :] = rows

            unpack_block(g, self.sz_recv[n], -dx, -dy, 6, store)
        row, lane = iota((48, 128), 0), iota((48, 128), 1)
        outside = ((k == 0) & (row < 8)) | ((k == 3) & (row >= 40))
        sixth = jnp.where(outside, 0.0, 1.0 / 6.0).astype(F32)
        sixths = (sixth, jnp.where((lane - 120 * g) >> 3 == 0, sixth, 0.0))

        def inside(x):
            out = ((i == 0) & (x < 6)) | ((i == 31) & (x >= 14))
            scale = jnp.where(out, 0.0, 1.0).astype(F32)
            return [one * scale for one in sixths]

        def first(x, carry):
            scale = inside(x)
            for t in range(2):
                self.p_a[t, x, 8:56, :] = -swide[t, x] * scale[t]
            return carry

        lax.fori_loop(0, 20, first, 0)
        old, new = self.p_a, self.p_b
        for sweep in range(1, 6):

            def relax(x, carry, old=old, new=new):
                scale = inside(x)
                right, left = along_z(old[0, x, 8:56, :], old[1, x, 8:56, :])
                for t in range(2):
                    total = old[t, x + 1, 8:56, :] + old[t, x - 1, 8:56, :]
                    total = total + old[t, x, 9:57, :] + old[t, x, 7:55, :]
                    total = total + right[t] + left[t]
                    new[t, x, 8:56, :] = (total - swide[t, x]) * scale[t]
                return carry

            lax.fori_loop(sweep, 20 - sweep, relax, 0)
            old, new = new, old
        p, prov = old, self.prov

        def project(x, carry):
            at = x + 6
            right, left = along_z(p[0, at, 16:48, :], p[1, at, 16:48, :])
            slope_z = right[0] - left[0]
            slope_x = p[0, at + 1, 16:48, :] - p[0, at - 1, 16:48, :]
            slope_y = p[0, at, 17:49, :] - p[0, at, 15:47, :]
            for c, slope in enumerate((slope_x, slope_y, slope_z)):
                self.velocity_next[c, x] = prov[c, 0, x + 2, 8:40, :] - 0.5 * slope
            self.pressure[x] = p[0, at, 16:48, :]
            return carry

        lax.fori_loop(0, 8, project, 0)

    def finish(self):
        for copy in self.copies_one + self.copies_two:
            copy.wait_send()


PATCH_SCRATCH = [pltpu.VMEM((16, 6144), F32), pltpu.VMEM((2048, 128), BF16)]


def make_fold(fold):
    row, col = iota((2048, 128), 0), iota((2048, 128), 1)
    hit = (row // 128 == col // 8) & (row % 8 == col % 8)
    fold[...] = hit.astype(F32).astype(BF16)


def pick_patches(field, selection, lines, fold, out):
    for c in range(3):
        for x in range(8):
            for py in range(4):
                combo = (c * 4 + x % 4) * 4 + py
                row = 8 * (x // 4)
                lines[row : row + 8, 128 * combo : 128 * combo + 128] = field[
                    c, x, pl.ds(py, 8, stride=4), :
                ]
    chosen = jnp.broadcast_to(selection[...], (16, 96))
    line = (chosen >> 4 == iota((16, 96), 0)).astype(F32).astype(BF16)
    cell = (chosen & 15 == iota((16, 96), 0)).astype(F32).astype(BF16)
    spread = ((iota((16, 2048), 1) & 127) >> 3 == iota((16, 2048), 0)).astype(F32).astype(BF16)
    here = matmul_tn(cell, spread)
    for part in range(3):
        source = lines[:, 2048 * part : 2048 * part + 2048].astype(BF16)
        rows = (matmul_tn(line, source) * here).astype(BF16)
        out[:, 128 * part : 128 * part + 128] = matmul(rows, fold[...]).astype(BF16)


def trainer_targets(here):
    g, i, k = here
    x, y, c = lax.div(i, 8), lax.rem(lax.div(i, 2), 4), lax.rem(i, 2)
    out = [(g, i, lax.rem(k + d, 4)) for d in (1, 2, 3)]
    out += [(g, lax.rem(x + d, 4) * 8 + y * 2 + c, k) for d in (1, 2, 3)]
    out += [(g, x * 8 + lax.rem(y + d, 4) * 2 + c, k) for d in (1, 2, 3)]
    out += [(g, lax.rem(x + d, 4) * 8 + y * 2 + 1 - c, k) for d in (1, 2, 3)]
    out += [(g, x * 8 + lax.rem(y + d, 4) * 2 + 1 - c, k) for d in (1, 2, 3)]
    return out + [(g, x * 8 + y * 2 + 1 - c, k), (1 - g, i, k)]


class Scatter:
    @staticmethod
    def scratch(rows, width, wire):
        return [
            pltpu.VMEM((2, 4, 4, 2, rows, width), F32),
            pltpu.VMEM((2, 4, 4, rows, width), F32),
            pltpu.VMEM((2, 4, 4, rows, width), wire),
            pltpu.VMEM((2, 4, 4, rows, width), wire),
            pltpu.VMEM((2, 4, rows, width), F32),
            pltpu.VMEM((2, 4, rows, width), wire),
            pltpu.VMEM((2, 4, rows, width), wire),
            pltpu.VMEM((2, rows, width), F32),
            pltpu.VMEM((rows, width), F32),
            pltpu.SemaphoreType.DMA((2, 8)),
            pltpu.SemaphoreType.DMA((2, 8)),
            pltpu.SemaphoreType.DMA((2, 8)),
            pltpu.SemaphoreType.DMA((2, 1)),
        ]

    def __init__(self, here, refs, wire):
        g, i, k = here
        self.here, self.wire = here, wire
        self.x, self.y, self.c = lax.div(i, 8), lax.rem(lax.div(i, 2), 4), lax.rem(i, 2)
        (
            self.parts, self.core_recv, self.one_send, self.one_recv, self.one_sum,
            self.two_send, self.two_recv, self.two_sum, self.three_recv,
            self.core_sems, self.one_sems, self.two_sems, self.three_sems,
        ) = refs
        self.one, self.two = ([], []), ([], [])

    def along(self, on_x, d):
        g, i, k = self.here
        x, y = self.x, self.y
        if on_x:
            x = lax.rem(x + d, 4)
        else:
            y = lax.rem(y + d, 4)
        return (g, x * 8 + y * 2 + self.c, k)

    def core_copy(self, chunk):
        g, i, k = self.here
        half, x = lax.div(chunk, 4), lax.rem(chunk, 4)
        return push(
            self.parts.at[half, x, :, 1 - self.c],
            self.core_recv.at[half, x],
            self.core_sems,
            chunk,
            (g, self.x * 8 + self.y * 2 + 1 - self.c, k),
        )

    def start_core(self, chunk):
        self.core_copy(chunk).start()

    def first(self, half):
        for chunk in range(4 * half, 4 * half + 4):
            self.core_copy(jnp.int32(chunk)).wait_recv()
        mine = self.y if half else self.x
        for d in (2, 1, 3, 0):
            to = lax.rem(mine + d, 4)
            if half:
                total = self.parts[half, :, to, self.c] + self.core_recv[half, :, to]
            else:
                total = self.parts[half, to, :, self.c] + self.core_recv[half, to]
            if d == 0:
                self.one_sum[half] = total
            else:
                self.one_send[half, d] = total.astype(self.wire)
                copy = push(
                    self.one_send.at[half, d], self.one_recv.at[half, d], self.one_sems,
                    4 * half + d, self.along(not half, d),
                )
                copy.start()
                self.one[half].append(copy)

    def second(self, half):
        for copy in self.one[half]:
            copy.wait_recv()
        total = self.one_sum[half]
        for d in (1, 2, 3):
            total = total + self.one_recv[half, d].astype(F32)
        self.one_sum[half] = total
        self.two_send[half] = total.astype(self.wire)
        mine = self.x if half else self.y
        for d in (2, 1, 3):
            copy = push(
                self.two_send.at[half, lax.rem(mine + d, 4)], self.two_recv.at[half, d],
                self.two_sems, 4 * half + d, self.along(half, d),
            )
            copy.start()
            self.two[half].append(copy)

    def third(self):
        g, i, k = self.here
        for half in (0, 1):
            mine = self.x if half else self.y
            for copy in self.two[half]:
                copy.wait_recv()
            total = self.one_sum[half, mine]
            for d in (1, 2, 3):
                total = total + self.two_recv[half, d].astype(F32)
            self.two_sum[half] = total
        self.three = push(
            self.two_sum.at[1 - g], self.three_recv, self.three_sems, 0, (1 - g, i, k)
        )
        self.three.start()

    def result(self):
        self.three.wait_recv()
        return self.two_sum[self.here[0]] + self.three_recv[...]

    def finish(self):
        for chunk in range(8):
            self.core_copy(jnp.int32(chunk)).wait_send()
        for copy in self.one[0] + self.one[1] + self.two[0] + self.two[1] + [self.three]:
            copy.wait_send()


class Product:
    scratch = [
        pltpu.VMEM((4, 2, 128, 384), F32),
        pltpu.VMEM((4, 128, 384), F32),
        pltpu.VMEM((4, 128, 384), BF16),
        pltpu.VMEM((4, 128, 384), BF16),
        pltpu.VMEM((128, 384), F32),
        pltpu.VMEM((2, 4, 4, 2, 16, 128), F32),
        pltpu.VMEM((4, 2, 4, 2, 16, 128), BF16),
        pltpu.VMEM((4, 2, 4, 2, 16, 128), BF16),
        pltpu.VMEM((2, 4, 2, 16, 128), F32),
        pltpu.VMEM((4, 2, 16, 128), F32),
        pltpu.VMEM((4, 2, 16, 128), F32),
        pltpu.VMEM((4, 2, 16, 128), F32),
        pltpu.SemaphoreType.DMA((2, 4)),
        pltpu.SemaphoreType.DMA((2, 4)),
        pltpu.SemaphoreType.DMA((2, 4)),
        pltpu.SemaphoreType.DMA((2, 1)),
        pltpu.SemaphoreType.DMA((2, 8)),
    ]

    def __init__(self, here, refs, on_x):
        g, i, k = here
        self.here, self.on_x = here, on_x
        self.x, self.y, self.c = lax.div(i, 8), lax.rem(lax.div(i, 2), 4), lax.rem(i, 2)
        self.mine, self.other = (self.x, self.y) if on_x else (self.y, self.x)
        (
            self.parts, self.core_recv, self.one_send, self.one_recv, self.one_sum, self.wide,
            self.two_send, self.two_recv, self.two_sum, self.three_recv, self.three_sum,
            self.four_recv, self.core_sems, self.one_sems, self.two_sems, self.three_sems,
            self.four_sems,
        ) = refs
        self.copies = []

    def target(self, first, second, core):
        g, i, k = self.here
        first, second = lax.rem(self.mine + first, 4), lax.rem(self.other + second, 4)
        x, y = (first, second) if self.on_x else (second, first)
        return (g, x * 8 + y * 2 + lax.rem(self.c + core, 2), k)

    def core_copy(self, chunk):
        return push(
            self.parts.at[chunk, 1 - self.c], self.core_recv.at[chunk], self.core_sems, chunk,
            self.target(0, 0, 1),
        )

    def start(self, copy):
        copy.start()
        self.copies.append(copy)
        return copy

    def fill(self, left, right):
        def chunk(n, carry):
            at = pl.ds(pl.multiple_of(n * 256, 256), 256)
            self.parts[n] = matmul_tn(left[:, at], right).reshape(2, 128, 384)
            self.core_copy(n).start()
            return carry

        lax.fori_loop(0, 4, chunk, 0)

    def first(self):
        for chunk in range(4):
            self.core_copy(jnp.int32(chunk)).wait_recv()
        self.one = []
        for d in (2, 1, 3, 0):
            to = lax.rem(self.mine + d, 4)
            total = self.parts[to, self.c] + self.core_recv[to]
            if d == 0:
                self.one_sum[...] = total
            else:
                self.one_send[d] = total.astype(BF16)
                copy = push(
                    self.one_send.at[d], self.one_recv.at[d], self.one_sems, d,
                    self.target(d, 0, 0),
                )
                self.one.append(self.start(copy))

    def own_rows(self, at):
        return self.wide[:, :, at] if self.on_x else self.wide[:, at]

    def second(self, weights):
        for copy in self.one:
            copy.wait_recv()
        total = self.one_sum[...]
        for d in (1, 2, 3):
            total = total + self.one_recv[d].astype(F32)
        high = total.astype(BF16)
        low = (total - high.astype(F32)).astype(BF16)
        product = matmul_nt(weights, high) + matmul_nt(weights, low)
        self.wide[...] = product.reshape(2, 4, 4, 2, 16, 128)
        self.two = []
        for d in (2, 1, 3):
            self.two_send[d] = self.own_rows(lax.rem(self.other + d, 4)).astype(BF16)
            copy = push(
                self.two_send.at[d], self.two_recv.at[d], self.two_sems, d, self.target(0, d, 0)
            )
            self.two.append(self.start(copy))

    def third(self):
        g, i, k = self.here
        for copy in self.two:
            copy.wait_recv()
        total = self.own_rows(self.other)
        for d in (1, 2, 3):
            total = total + self.two_recv[d].astype(F32)
        self.two_sum[...] = total
        self.three = self.start(
            push(self.two_sum.at[1 - g], self.three_recv, self.three_sems, 0, (1 - g, i, k))
        )

    def fourth(self):
        self.three.wait_recv()
        self.three_sum[...] = self.two_sum[self.here[0]] + self.three_recv[...]
        self.four = []
        for d, core in ((2, 0), (2, 1), (1, 0), (1, 1), (3, 0), (3, 1), (0, 1)):
            src = self.three_sum.at[lax.rem(self.mine + d, 4), lax.rem(self.c + core, 2)]
            copy = push(
                src, self.four_recv.at[self.mine, self.c], self.four_sems, 2 * d + core,
                self.target(d, 0, core),
            )
            self.four.append(self.start(copy))
        self.four_recv[self.mine, self.c] = self.three_sum[self.mine, self.c]

    def result(self, out):
        for copy in self.four:
            copy.wait_recv()
        for first in range(4):
            for core in range(2):
                at = 128 * (2 * first + core)
                out[:, at : at + 128] = self.four_recv[first, core]

    def finish(self):
        for chunk in range(4):
            self.core_copy(jnp.int32(chunk)).wait_send()
        for copy in self.copies:
            copy.wait_send()


N_SCATTER = 13
TRAINER_SCRATCH = [
    pltpu.VMEM((384, 1024), BF16),
    pltpu.VMEM((1024, 1024), BF16),
    pltpu.VMEM((1024, 1024), BF16),
    pltpu.VMEM((1024, 384), BF16),
    pltpu.VMEM((96, 384), BF16),
    pltpu.VMEM((4, 96, 384), BF16),
    pltpu.VMEM((4, 96, 384), BF16),
    pltpu.VMEM((288, 1024), BF16),
    pltpu.VMEM((96, 1024), F32),
    pltpu.VMEM((384, 1024), F32),
    pltpu.VMEM((384, 1024), BF16),
    pltpu.VMEM((384, 1024), BF16),
    pltpu.VMEM((96, 384), F32),
    pltpu.VMEM((4, 96, 384), BF16),
    pltpu.VMEM((4, 96, 384), BF16),
    pltpu.VMEM((384, 1024), BF16),
    pltpu.VMEM((384, 1024), BF16),
    pltpu.VMEM((384, 1024), BF16),
    pltpu.VMEM((96, 1024), F32),
    pltpu.VMEM((1024, 384), BF16),
    pltpu.VMEM((4, 8, 384), F32),
    pltpu.VMEM((4, 8, 384), F32),
    pltpu.SemaphoreType.DMA((6,)),
    pltpu.SemaphoreType.DMA((2, 4)),
    pltpu.SemaphoreType.DMA((2, 4)),
    pltpu.SemaphoreType.DMA((2, 4)),
    pltpu.SemaphoreType.DMA((2, 4)),
]
N_TRAINER = len(TRAINER_SCRATCH)
TRAINER_SCRATCH += Scatter.scratch(16, 384, BF16) * 2 + Product.scratch * 2


def columns(n):
    return pl.ds(pl.multiple_of(n * 256, 256), 256)


def step_kernel(
    velocity, viscosity, selection, w_in_far, w_up_far, w_down_far, w_out_far,
    velocity_next, pressure, out_up, out_down, out_small, lines, fold, *refs
):
    here = place()
    g, i, k = here
    n_stencil = len(Stencil.scratch)
    step = Stencil(here, velocity_next, pressure, refs[:n_stencil])
    refs = refs[n_stencil:]
    (
        w_in, w_up, w_down, w_out, targets, in_all, err_all, lifted_b, own_lift, slope, active, mixed,
        own_predicted, down_send, down_recv, back_raised, lift_b, back_b, own_back, w_in_t, tail_send, tail_recv,
        near_sems, in_sems, down_sems, err_sems, tail_sems,
    ) = refs[:N_TRAINER]
    refs = refs[N_TRAINER:]
    grad_in, grad_out = (
        Scatter(here, refs[n * N_SCATTER : (n + 1) * N_SCATTER], BF16) for n in range(2)
    )
    refs = refs[2 * N_SCATTER :]
    up, down = (
        Product(here, refs[: len(Product.scratch)], True),
        Product(here, refs[len(Product.scratch) :], False),
    )
    sent = []

    def peer(d):
        return (g, i, lax.rem(k + d, 4))

    def start(copies):
        for copy in copies:
            copy.start()
        sent.extend(copies)
        return copies

    met = stencil_targets(here) + trainer_targets(here)
    greet(met)
    near = [
        pltpu.make_async_copy(src, dst, near_sems.at[n])
        for n, (src, dst) in enumerate(
            (
                (velocity, step.fields.at[0:3]),
                (viscosity, step.fields.at[3]),
                (w_in_far, w_in),
                (w_up_far, w_up),
                (w_down_far, w_down),
                (w_out_far, w_out),
            )
        )
    ]
    for copy in near:
        copy.start()
    make_fold(fold)
    for copy in near[:2]:
        copy.wait()
    pick_patches(step.fields, selection, lines, fold, in_all.at[0])
    step.prepare()
    greeted(met)
    step.send_one()
    in_copies = start(
        [push(in_all.at[0], in_all.at[4 - d], in_sems, d, peer(d)) for d in (2, 1, 3)]
    )
    for copy in near[2:]:
        copy.wait()

    def forward(first, count):
        rows = in_all[first : first + count].reshape(96 * count, 384)
        at_rows = slice(96 * first, 96 * (first + count))

        def lift_in(n, carry):
            at = columns(n)
            lifted = matmul(rows, w_in[:, at])
            lifted_b[0 : 96 * count, at] = lifted.astype(BF16)
            if first == 0:
                own_lift[:, at] = lifted
            return carry

        def raise_(n, carry):
            at = columns(n)
            raised = matmul(lifted_b[0 : 96 * count, :], w_up[:, at])
            sigmoid = jax.nn.sigmoid(raised)
            active[at_rows, at] = (raised * sigmoid).astype(BF16)
            slope[at_rows, at] = sigmoid * (1.0 + raised * (1.0 - sigmoid))
            return carry

        def lower(n, carry):
            at = columns(n)
            part = matmul(active[at_rows, :], w_down[:, at])
            if first == 0:
                part = part + own_lift[:, at]
            mixed[at_rows, at] = part.astype(BF16)
            return carry

        for body in (lift_in, raise_, lower):
            lax.fori_loop(0, 4, body, 0)
        return matmul(mixed[at_rows, :], w_out[...])

    own_predicted[...] = forward(0, 1)
    w_in_t[...] = w_in[...].T
    step.make_source()
    step.send_two()
    for copy in in_copies:
        copy.wait_recv()
    parts = forward(1, 3).astype(BF16)
    down_copies = []
    for d in (2, 1, 3):
        down_send[d] = parts[96 * (d - 1) : 96 * d]
        down_copies += start([push(down_send.at[d], down_recv.at[d], down_sems, d, peer(d))])
    step.solve()
    pick_patches(velocity_next, selection, lines, fold, targets)

    for copy in down_copies:
        copy.wait_recv()
    predicted = own_predicted[...]
    for d in (1, 2, 3):
        predicted = predicted + down_recv[d].astype(F32)
    scale = float(24576) ** (-0.5)
    err_all[0] = ((predicted - targets[...].astype(F32)) * scale).astype(BF16)
    err_copies = start(
        [push(err_all.at[0], err_all.at[4 - d], err_sems, d, peer(d)) for d in (2, 1, 3)]
    )
    for copy in err_copies:
        copy.wait_recv()
    rows_in = in_all[...].reshape(384, 384)
    errors = err_all[...].reshape(384, 384)

    def back(n, carry):
        at = columns(n)
        both = matmul_nt(errors, w_out[at, :])
        back_b[:, at] = both.astype(BF16)
        own_back[:, at] = both[0:96]
        return carry

    def back_up(n, carry):
        at = columns(n)
        steep = matmul_nt(back_b[...], w_down[at, :])
        back_raised[:, at] = (steep * slope[:, at]).astype(BF16)
        return carry

    def back_lift(n, carry):
        at = columns(n)
        part = matmul_nt(back_raised[...], w_up[at, :])
        lift_b[0:96, at] = (part[0:96] + own_back[:, at]).astype(BF16)
        lift_b[96:384, at] = part[96:384].astype(BF16)
        return carry

    lax.fori_loop(0, 4, back, 0)
    lax.fori_loop(0, 4, back_up, 0)
    up.fill(back_raised, rows_in)
    down.fill(active, errors)

    def grad_chunk(scatter, left, right):
        def chunk(n, carry):
            at = pl.ds(pl.multiple_of(n * 256, 256), 256)
            block = matmul_tn(left[:, at], right).reshape(2, 4, 2, 16, 384)
            for part in range(2):
                scatter.parts[lax.div(n, 2), lax.rem(n, 2) * 2 + part] = block[part]
                scatter.start_core(n * 2 + part)
            return carry

        lax.fori_loop(0, 4, chunk, 0)

    up.first()
    lax.fori_loop(0, 4, back_lift, 0)
    grad_chunk(grad_in, lift_b, rows_in)
    down.first()
    grad_chunk(grad_out, mixed, errors)
    scatters = (grad_in, grad_out)
    for scatter in scatters:
        scatter.first(0)
        scatter.first(1)
    up.second(w_in_t[...])
    down.second(w_out[...])
    for scatter in scatters:
        scatter.second(0)
        scatter.second(1)
    up.third()
    down.third()
    for scatter in scatters:
        scatter.third()
    up.fourth()
    down.fourth()
    last_in, last_out = grad_in.result(), grad_out.result()
    for j in range(4):
        tail_send[j, 0:4] = last_in[4 * j : 4 * j + 4]
        tail_send[j, 4:8] = last_out[4 * j : 4 * j + 4]
    tail_copies = start(
        [
            push(tail_send.at[lax.rem(k + d, 4)], tail_recv.at[d], tail_sems, d, peer(d))
            for d in (2, 1, 3)
        ]
    )
    up.result(out_up)
    down.result(out_down)
    for copy in tail_copies:
        copy.wait_recv()
    out_small[...] = tail_send[k] + tail_recv[1] + tail_recv[2] + tail_recv[3]
    for copy in sent:
        copy.wait_send()
    step.finish()
    for scatter in scatters + (up, down):
        scatter.finish()


def emit_kernel(
    near_next, near_pressure, near_up, near_down, near_small,
    velocity_next, pressure, grad_up, grad_down, first, second,
):
    velocity_next[...] = near_next[...]
    pressure[...] = near_pressure[...]
    grad_up[...] = near_up[...]
    grad_down[...] = near_down[...]
    first[...] = near_small[0:4]
    second[...] = near_small[4:8]


def on_device(velocity, viscosity, selection, w_in, w_up, w_down, w_out):
    shape = jax.ShapeDtypeStruct
    far, near = pl.BlockSpec(memory_space=pl.ANY), pl.BlockSpec(memory_space=pltpu.VMEM)
    velocity_next, pressure, grad_up, grad_down, small = pl.pallas_call(
        step_kernel,
        out_shape=[
            shape((3, 8, 32, 128), F32),
            shape((8, 32, 128), F32),
            shape((16, 1024), F32),
            shape((16, 1024), F32),
            shape((8, 384), F32),
        ],
        in_specs=[far, far, near, far, far, far, far],
        out_specs=[near] * 5,
        scratch_shapes=PATCH_SCRATCH + Stencil.scratch + TRAINER_SCRATCH,
        compiler_params=pltpu.CompilerParams(
            collective_id=0, has_side_effects=True, vmem_limit_bytes=56 * MIB
        ),
        name="step",
    )(velocity, viscosity, selection.reshape(1, 96), w_in, w_up, w_down, w_out)
    velocity_next, pressure, grad_up, grad_down, first, second = pl.pallas_call(
        emit_kernel,
        out_shape=[
            shape((3, 8, 32, 128), F32),
            shape((8, 32, 128), F32),
            shape((16, 1024), F32),
            shape((16, 1024), F32),
            shape((4, 384), F32),
            shape((4, 384), F32),
        ],
        in_specs=[near] * 5,
        out_specs=[near] * 6,
        compiler_params=pltpu.CompilerParams(vmem_limit_bytes=60 * MIB),
        name="emit",
    )(velocity_next, pressure, grad_up, grad_down, small)
    return (velocity_next, pressure, first.T, grad_up, grad_down.T, second)


def solution(mesh):
    placed = (
        P(None, "gx", "gy", "grp"),
        P("gx", "gy", "grp"),
        P("grp", "gx", "gy", None),
        P(),
        P(None, "gy"),
        P("gy", None),
        P(),
    )
    return jax.shard_map(
        on_device,
        mesh=mesh,
        in_specs=placed,
        out_specs=(
            P(None, "gx", "gy", "grp"),
            P("gx", "gy", "grp"),
            P(None, ("grp", "gx", "gy")),
            P(("grp", "gx"), "gy"),
            P("gy", ("grp", "gx")),
            P(("grp", "gx", "gy"), None),
        ),
        check_vma=False,
    )
```

```python
import jax
import jax.numpy as jnp
from jax import lax
from jax.experimental import pallas as pl
from jax.experimental.pallas import tpu as pltpu
from jax.sharding import PartitionSpec as P

F32 = jnp.float32
BF16 = jnp.bfloat16
MESH = pl.DeviceIdType.MESH
MIB = 1 << 20

FACES = [(1, 0), (-1, 0), (0, 1), (0, -1)]
DIAGONALS = [(1, 1), (1, -1), (-1, 1), (-1, -1)]
PLANE = FACES + DIAGONALS
CROSS_ONE = [(0, 0)] + FACES
CROSS_TWO = [(0, 0)] + PLANE
EDGE_ORDER = (1, 2, 0, 3)


def place():
    return lax.axis_index("grp"), lax.axis_index("gx"), lax.axis_index("gy")


def push(src, dst, sems, slot, target):
    return pltpu.make_async_remote_copy(
        src_ref=src,
        dst_ref=dst,
        send_sem=sems.at[0, slot],
        recv_sem=sems.at[1, slot],
        device_id=target,
        device_id_type=MESH,
    )


def greet(targets):
    barrier = pltpu.get_barrier_semaphore()
    for target in targets:
        pl.semaphore_signal(barrier, inc=1, device_id=target, device_id_type=MESH)


def greeted(targets):
    pl.semaphore_wait(pltpu.get_barrier_semaphore(), len(targets))


def matmul(a, b):
    return jnp.dot(a, b, preferred_element_type=F32)


def matmul_nt(a, b):
    return lax.dot_general(a, b, (((1,), (1,)), ((), ())), preferred_element_type=F32)


def matmul_tn(a, b):
    return lax.dot_general(a, b, (((0,), (0,)), ((), ())), preferred_element_type=F32)


def iota(shape, dim):
    return lax.broadcasted_iota(jnp.int32, shape, dim)


def offset(here, dx, dy, flip):
    g, i, k = here
    return (1 - g if flip else g, lax.rem(i + dx + 32, 32), lax.rem(k + dy + 4, 4))


def stencil_targets(here):
    return [offset(here, dx, dy, False) for dx, dy in PLANE] + [
        offset(here, dx, dy, True) for dx, dy in CROSS_TWO
    ]


def pack_edge(g, group):
    lane = iota((16, 128), 1) // 8
    packed = jnp.zeros((16, 128), F32)
    for part in range(16):
        moved = pltpu.roll(group(part), lax.rem(8 * part + 8 * (1 - g), 128), 1)
        packed = jnp.where(lane == part, moved, packed)
    return packed


def unpack_edge(g, packed, part):
    lane = iota((16, 128), 1)
    rows = pltpu.roll(packed, lax.rem(128 - 8 * part + 120 * g, 128), 1)
    return jnp.where((lane - 120 * g) >> 3 == 0, rows, 0.0)


def unpack_block(g, packed, dx, dy, deep, store):
    planes = range(8) if dx == 0 else (range(8 - deep, 8) if dx < 0 else range(deep))
    for x in planes:
        to = deep + x if dx == 0 else (x - (8 - deep) if dx < 0 else deep + 8 + x)
        if dy == 0:
            store(to, 8, unpack_edge(g, packed, 2 * x))
            store(to, 24, unpack_edge(g, packed, 2 * x + 1))
        elif dy < 0:
            store(to, 0, unpack_edge(g, packed, 2 * x + 1)[8:16])
        else:
            store(to, 40, unpack_edge(g, packed, 2 * x)[0:8])


def along_z(own, other):
    lane = iota(own.shape, 1)
    own_r, other_r = pltpu.roll(own, 127, 1), pltpu.roll(other, 127, 1)
    own_l, other_l = pltpu.roll(own, 1, 1), pltpu.roll(other, 1, 1)
    last, first = lane == 127, lane == 0
    right = (jnp.where(last, other_r, own_r), jnp.where(last, own_r, other_r))
    left = (jnp.where(first, other_l, own_l), jnp.where(first, own_l, other_l))
    return right, left


def own_slices(dx, dy, deep, rows):
    xs = slice(0, 8) if dx == 0 else (slice(8 - deep, 8) if dx > 0 else slice(0, deep))
    ys = slice(0, 32) if dy == 0 else (slice(32 - rows, 32) if dy > 0 else slice(0, rows))
    return xs, ys


class Stencil:
    scratch = [
        pltpu.VMEM((4, 8, 32, 128), F32),
        pltpu.VMEM((2, 4, 8, 2, 128), F32),
        pltpu.VMEM((2, 4, 8, 2, 128), F32),
        pltpu.VMEM((4, 4, 2, 2, 128), F32),
        pltpu.VMEM((4, 16, 128), F32),
        pltpu.VMEM((5, 4, 16, 128), F32),
        pltpu.VMEM((4, 2, 12, 48, 128), F32),
        pltpu.VMEM((3, 2, 12, 48, 128), F32),
        pltpu.VMEM((8, 32, 128), F32),
        pltpu.VMEM((16, 128), F32),
        pltpu.VMEM((9, 16, 128), F32),
        pltpu.VMEM((2, 20, 48, 128), F32),
        pltpu.VMEM((2, 20, 64, 128), F32),
        pltpu.VMEM((2, 20, 64, 128), F32),
        pltpu.SemaphoreType.DMA((2, 13)),
        pltpu.SemaphoreType.DMA((2, 17)),
    ]

    def __init__(self, here, velocity_next, pressure, refs):
        self.here = here
        self.velocity_next, self.pressure = velocity_next, pressure
        (
            self.fields, self.y_send, self.y_recv, self.d_recv, self.z_send, self.z_recv,
            self.wide, self.prov, self.source, self.sz_send, self.sz_recv, self.swide,
            self.p_a, self.p_b, self.sems_one, self.sems_two,
        ) = refs

    def prepare(self):
        g = self.here[0]
        self.y_send[0] = self.fields[:, :, 30:32, :]
        self.y_send[1] = self.fields[:, :, 0:2, :]
        for f in range(4):
            self.z_send[EDGE_ORDER.index(f)] = pack_edge(
                g, lambda part: self.fields[f, part // 2, 16 * (part % 2) : 16 * (part % 2) + 16, :]
            )

    def send_one(self):
        g = self.here[0]
        copies = []
        for dx, dy in PLANE:
            slot = len(copies)
            target = offset(self.here, dx, dy, False)
            xs, _ = own_slices(dx, dy, 2, 2)
            if dy == 0:
                x_to = 0 if dx > 0 else 10
                src = self.fields.at[:, xs]
                dst = self.wide.at[:, 0, x_to : x_to + 2, 8:40, :]
            elif dx == 0:
                edge = 0 if dy > 0 else 1
                src, dst = self.y_send.at[edge], self.y_recv.at[edge]
            else:
                edge = 0 if dy > 0 else 1
                src, dst = self.y_send.at[edge, :, xs], self.d_recv.at[slot - 4]
            copies.append(push(src, dst, self.sems_one, slot, target))
        for n, (dx, dy) in enumerate(CROSS_ONE):
            target = offset(self.here, dx, dy, True)
            some = slice(1, 3) if dx else (slice(0, 2) if dy else slice(0, 4))
            src, dst = self.z_send.at[some], self.z_recv.at[n, some]
            copies.append(push(src, dst, self.sems_one, len(copies), target))
        for copy in copies:
            copy.start()
        self.copies_one = copies

    def make_source(self):
        g, i, k = self.here
        wide = self.wide
        wide[:, 0, 2:10, 8:40, :] = self.fields[...]
        for copy in self.copies_one:
            copy.wait_recv()
        wide[:, 0, 2:10, 6:8, :] = self.y_recv[0]
        wide[:, 0, 2:10, 40:42, :] = self.y_recv[1]
        for n, (dx, dy) in enumerate(DIAGONALS):
            x_to, y_to = (0 if dx > 0 else 10), (6 if dy > 0 else 40)
            wide[:, 0, x_to : x_to + 2, y_to : y_to + 2, :] = self.d_recv[n]
        for n, (dx, dy) in enumerate(CROSS_ONE):
            for f in (0, 1, 2, 3) if n == 0 else ((0, 2) if dx else (1, 2)):

                def store(to, row, rows, f=f):
                    wide[f, 1, to, row : row + rows.shape[0], :] = rows

                unpack_block(g, self.z_recv[n, EDGE_ORDER.index(f)], -dx, -dy, 2, store)

        @pl.when(i == 0)
        def _():
            wide[:, :, 0:2] = jnp.zeros((4, 2, 2, 48, 128), F32)

        @pl.when(i == 31)
        def _():
            wide[:, :, 10:12] = jnp.zeros((4, 2, 2, 48, 128), F32)

        @pl.when(k == 0)
        def _():
            wide[:, :, :, 0:8, :] = jnp.zeros((4, 2, 12, 8, 128), F32)

        @pl.when(k == 3)
        def _():
            wide[:, :, :, 40:48, :] = jnp.zeros((4, 2, 12, 8, 128), F32)

        def advance(c, x, top, bottom, tiles):
            mid = [wide[c, t, x, top:bottom, :] for t in range(2)]
            right, left = along_z(*mid)
            for t in tiles:
                total = wide[c, t, x + 1, top:bottom, :] + wide[c, t, x - 1, top:bottom, :]
                total = total + wide[c, t, x, top + 1 : bottom + 1, :]
                total = total + wide[c, t, x, top - 1 : bottom - 1, :]
                total = total + right[t] + left[t]
                after = mid[t] + wide[3, t, x, top:bottom, :] * (total - 6.0 * mid[t])
                self.prov[c, t, x, top:bottom, :] = after

        def provisional(x, carry):
            advance(0, x, 8, 40, (0,))
            advance(1, x, 7, 41, (0,))
            advance(2, x, 8, 40, (0, 1))
            return carry

        advance(0, 1, 8, 40, (0,))
        advance(0, 10, 8, 40, (0,))
        lax.fori_loop(2, 10, provisional, 0)
        prov = self.prov

        def source(x, carry):
            right, left = along_z(prov[2, 0, x, 8:40, :], prov[2, 1, x, 8:40, :])
            slope = right[0] - left[0]
            slope = slope + prov[0, 0, x + 1, 8:40, :] - prov[0, 0, x - 1, 8:40, :]
            slope = slope + prov[1, 0, x, 9:41, :] - prov[1, 0, x, 7:39, :]
            self.source[x - 2] = 0.5 * slope
            return carry

        lax.fori_loop(2, 10, source, 0)
        self.sz_send[...] = pack_edge(
            g, lambda part: self.source[part // 2, 16 * (part % 2) : 16 * (part % 2) + 16, :]
        )

    def send_two(self):
        g = self.here[0]
        copies = []
        for dx, dy in PLANE:
            target = offset(self.here, dx, dy, False)
            xs, ys = own_slices(dx, dy, 6, 8)
            x_to = 6 if dx == 0 else (0 if dx > 0 else 14)
            y_to = 8 if dy == 0 else (0 if dy > 0 else 40)
            dst = self.swide.at[
                0, x_to : x_to + xs.stop - xs.start, y_to : y_to + ys.stop - ys.start, :
            ]
            copies.append(push(self.source.at[xs, ys, :], dst, self.sems_two, len(copies), target))
        for n, (dx, dy) in enumerate(CROSS_TWO):
            target = offset(self.here, dx, dy, True)
            copies.append(push(self.sz_send, self.sz_recv.at[n], self.sems_two, len(copies), target))
        for copy in copies:
            copy.start()
        self.copies_two = copies

    def solve(self):
        g, i, k = self.here
        swide = self.swide
        swide[0, 6:14, 8:40, :] = self.source[...]
        for copy in self.copies_two:
            copy.wait_recv()
        for n, (dx, dy) in enumerate(CROSS_TWO):

            def store(to, row, rows):
                swide[1, to, row : row + rows.shape[0], :] = rows

            unpack_block(g, self.sz_recv[n], -dx, -dy, 6, store)
        row, lane = iota((48, 128), 0), iota((48, 128), 1)
        outside = ((k == 0) & (row < 8)) | ((k == 3) & (row >= 40))
        sixth = jnp.where(outside, 0.0, 1.0 / 6.0).astype(F32)
        sixths = (sixth, jnp.where((lane - 120 * g) >> 3 == 0, sixth, 0.0))

        def inside(x):
            out = ((i == 0) & (x < 6)) | ((i == 31) & (x >= 14))
            scale = jnp.where(out, 0.0, 1.0).astype(F32)
            return [one * scale for one in sixths]

        def first(x, carry):
            scale = inside(x)
            for t in range(2):
                self.p_a[t, x, 8:56, :] = -swide[t, x] * scale[t]
            return carry

        lax.fori_loop(0, 20, first, 0)
        old, new = self.p_a, self.p_b
        for sweep in range(1, 6):

            def relax(x, carry, old=old, new=new):
                scale = inside(x)
                right, left = along_z(old[0, x, 8:56, :], old[1, x, 8:56, :])
                for t in range(2):
                    total = old[t, x + 1, 8:56, :] + old[t, x - 1, 8:56, :]
                    total = total + old[t, x, 9:57, :] + old[t, x, 7:55, :]
                    total = total + right[t] + left[t]
                    new[t, x, 8:56, :] = (total - swide[t, x]) * scale[t]
                return carry

            def pair(n, carry, relax=relax, sweep=sweep):
                relax(sweep + 2 * n, carry)
                return relax(sweep + 2 * n + 1, carry)

            lax.fori_loop(0, 10 - sweep, pair, 0)
            old, new = new, old
        p, prov = old, self.prov

        def project(x, carry):
            at = x + 6
            right, left = along_z(p[0, at, 16:48, :], p[1, at, 16:48, :])
            slope_z = right[0] - left[0]
            slope_x = p[0, at + 1, 16:48, :] - p[0, at - 1, 16:48, :]
            slope_y = p[0, at, 17:49, :] - p[0, at, 15:47, :]
            for c, slope in enumerate((slope_x, slope_y, slope_z)):
                self.velocity_next[c, x] = prov[c, 0, x + 2, 8:40, :] - 0.5 * slope
            self.pressure[x] = p[0, at, 16:48, :]
            return carry

        lax.fori_loop(0, 8, project, 0)

    def finish(self):
        for copy in self.copies_one + self.copies_two:
            copy.wait_send()


PATCH_SCRATCH = [pltpu.VMEM((16, 6144), F32), pltpu.VMEM((2048, 128), BF16)]


def make_fold(fold):
    row, col = iota((2048, 128), 0), iota((2048, 128), 1)
    hit = (row // 128 == col // 8) & (row % 8 == col % 8)
    fold[...] = hit.astype(F32).astype(BF16)


def pick_patches(field, selection, lines, fold, out):
    for c in range(3):
        for x in range(8):
            for py in range(4):
                combo = (c * 4 + x % 4) * 4 + py
                row = 8 * (x // 4)
                lines[row : row + 8, 128 * combo : 128 * combo + 128] = field[
                    c, x, pl.ds(py, 8, stride=4), :
                ]
    chosen = jnp.broadcast_to(selection[...], (16, 96))
    line = (chosen >> 4 == iota((16, 96), 0)).astype(F32).astype(BF16)
    cell = (chosen & 15 == iota((16, 96), 0)).astype(F32).astype(BF16)
    spread = ((iota((16, 2048), 1) & 127) >> 3 == iota((16, 2048), 0)).astype(F32).astype(BF16)
    here = matmul_tn(cell, spread)
    for part in range(3):
        source = lines[:, 2048 * part : 2048 * part + 2048].astype(BF16)
        rows = (matmul_tn(line, source) * here).astype(BF16)
        out[:, 128 * part : 128 * part + 128] = matmul(rows, fold[...]).astype(BF16)


def trainer_targets(here):
    g, i, k = here
    x, y, c = lax.div(i, 8), lax.rem(lax.div(i, 2), 4), lax.rem(i, 2)
    out = [(g, i, lax.rem(k + d, 4)) for d in (1, 2, 3)]
    out += [(g, lax.rem(x + d, 4) * 8 + y * 2 + c, k) for d in (1, 2, 3)]
    out += [(g, x * 8 + lax.rem(y + d, 4) * 2 + c, k) for d in (1, 2, 3)]
    out += [(g, lax.rem(x + d, 4) * 8 + y * 2 + 1 - c, k) for d in (1, 2, 3)]
    out += [(g, x * 8 + lax.rem(y + d, 4) * 2 + 1 - c, k) for d in (1, 2, 3)]
    return out + [(g, x * 8 + y * 2 + 1 - c, k), (1 - g, i, k)]


class Scatter:
    @staticmethod
    def scratch(rows, width, wire):
        return [
            pltpu.VMEM((2, 4, 4, 2, rows, width), F32),
            pltpu.VMEM((2, 4, 4, rows, width), F32),
            pltpu.VMEM((2, 4, 4, rows, width), wire),
            pltpu.VMEM((2, 4, 4, rows, width), wire),
            pltpu.VMEM((2, 4, rows, width), F32),
            pltpu.VMEM((2, 4, rows, width), wire),
            pltpu.VMEM((2, 4, rows, width), wire),
            pltpu.VMEM((2, rows, width), F32),
            pltpu.VMEM((rows, width), F32),
            pltpu.SemaphoreType.DMA((2, 8)),
            pltpu.SemaphoreType.DMA((2, 8)),
            pltpu.SemaphoreType.DMA((2, 8)),
            pltpu.SemaphoreType.DMA((2, 1)),
        ]

    def __init__(self, here, refs, wire):
        g, i, k = here
        self.here, self.wire = here, wire
        self.x, self.y, self.c = lax.div(i, 8), lax.rem(lax.div(i, 2), 4), lax.rem(i, 2)
        (
            self.parts, self.core_recv, self.one_send, self.one_recv, self.one_sum,
            self.two_send, self.two_recv, self.two_sum, self.three_recv,
            self.core_sems, self.one_sems, self.two_sems, self.three_sems,
        ) = refs
        self.one, self.two = ([], []), ([], [])

    def along(self, on_x, d):
        g, i, k = self.here
        x, y = self.x, self.y
        if on_x:
            x = lax.rem(x + d, 4)
        else:
            y = lax.rem(y + d, 4)
        return (g, x * 8 + y * 2 + self.c, k)

    def core_copy(self, chunk):
        g, i, k = self.here
        half, x = lax.div(chunk, 4), lax.rem(chunk, 4)
        return push(
            self.parts.at[half, x, :, 1 - self.c],
            self.core_recv.at[half, x],
            self.core_sems,
            chunk,
            (g, self.x * 8 + self.y * 2 + 1 - self.c, k),
        )

    def start_core(self, chunk):
        self.core_copy(chunk).start()

    def first(self, half):
        for chunk in range(4 * half, 4 * half + 4):
            self.core_copy(jnp.int32(chunk)).wait_recv()
        mine = self.y if half else self.x
        for d in (2, 1, 3, 0):
            to = lax.rem(mine + d, 4)
            if half:
                total = self.parts[half, :, to, self.c] + self.core_recv[half, :, to]
            else:
                total = self.parts[half, to, :, self.c] + self.core_recv[half, to]
            if d == 0:
                self.one_sum[half] = total
            else:
                self.one_send[half, d] = total.astype(self.wire)
                copy = push(
                    self.one_send.at[half, d], self.one_recv.at[half, d], self.one_sems,
                    4 * half + d, self.along(not half, d),
                )
                copy.start()
                self.one[half].append(copy)

    def second(self, half):
        for copy in self.one[half]:
            copy.wait_recv()
        total = self.one_sum[half]
        for d in (1, 2, 3):
            total = total + self.one_recv[half, d].astype(F32)
        self.one_sum[half] = total
        self.two_send[half] = total.astype(self.wire)
        mine = self.x if half else self.y
        for d in (2, 1, 3):
            copy = push(
                self.two_send.at[half, lax.rem(mine + d, 4)], self.two_recv.at[half, d],
                self.two_sems, 4 * half + d, self.along(half, d),
            )
            copy.start()
            self.two[half].append(copy)

    def third(self):
        g, i, k = self.here
        for half in (0, 1):
            mine = self.x if half else self.y
            for copy in self.two[half]:
                copy.wait_recv()
            total = self.one_sum[half, mine]
            for d in (1, 2, 3):
                total = total + self.two_recv[half, d].astype(F32)
            self.two_sum[half] = total
        self.three = push(
            self.two_sum.at[1 - g], self.three_recv, self.three_sems, 0, (1 - g, i, k)
        )
        self.three.start()

    def result(self):
        self.three.wait_recv()
        return self.two_sum[self.here[0]] + self.three_recv[...]

    def finish(self):
        for chunk in range(8):
            self.core_copy(jnp.int32(chunk)).wait_send()
        for copy in self.one[0] + self.one[1] + self.two[0] + self.two[1] + [self.three]:
            copy.wait_send()


class Product:
    scratch = [
        pltpu.VMEM((4, 2, 128, 384), F32),
        pltpu.VMEM((4, 128, 384), F32),
        pltpu.VMEM((4, 128, 384), BF16),
        pltpu.VMEM((4, 128, 384), BF16),
        pltpu.VMEM((128, 384), F32),
        pltpu.VMEM((2, 4, 4, 2, 16, 128), F32),
        pltpu.VMEM((4, 2, 4, 2, 16, 128), BF16),
        pltpu.VMEM((4, 2, 4, 2, 16, 128), BF16),
        pltpu.VMEM((2, 4, 2, 16, 128), F32),
        pltpu.VMEM((4, 2, 16, 128), F32),
        pltpu.VMEM((4, 2, 16, 128), F32),
        pltpu.VMEM((4, 2, 16, 128), F32),
        pltpu.SemaphoreType.DMA((2, 4)),
        pltpu.SemaphoreType.DMA((2, 4)),
        pltpu.SemaphoreType.DMA((2, 4)),
        pltpu.SemaphoreType.DMA((2, 1)),
        pltpu.SemaphoreType.DMA((2, 8)),
    ]

    def __init__(self, here, refs, on_x):
        g, i, k = here
        self.here, self.on_x = here, on_x
        self.x, self.y, self.c = lax.div(i, 8), lax.rem(lax.div(i, 2), 4), lax.rem(i, 2)
        self.mine, self.other = (self.x, self.y) if on_x else (self.y, self.x)
        (
            self.parts, self.core_recv, self.one_send, self.one_recv, self.one_sum, self.wide,
            self.two_send, self.two_recv, self.two_sum, self.three_recv, self.three_sum,
            self.four_recv, self.core_sems, self.one_sems, self.two_sems, self.three_sems,
            self.four_sems,
        ) = refs
        self.copies = []

    def target(self, first, second, core):
        g, i, k = self.here
        first, second = lax.rem(self.mine + first, 4), lax.rem(self.other + second, 4)
        x, y = (first, second) if self.on_x else (second, first)
        return (g, x * 8 + y * 2 + lax.rem(self.c + core, 2), k)

    def core_copy(self, chunk):
        return push(
            self.parts.at[chunk, 1 - self.c], self.core_recv.at[chunk], self.core_sems, chunk,
            self.target(0, 0, 1),
        )

    def start(self, copy):
        copy.start()
        self.copies.append(copy)
        return copy

    def fill(self, left, right):
        def chunk(n, carry):
            at = pl.ds(pl.multiple_of(n * 256, 256), 256)
            self.parts[n] = matmul_tn(left[:, at], right).reshape(2, 128, 384)
            self.core_copy(n).start()
            return carry

        lax.fori_loop(0, 4, chunk, 0)

    def first(self):
        for chunk in range(4):
            self.core_copy(jnp.int32(chunk)).wait_recv()
        self.one = []
        for d in (2, 1, 3, 0):
            to = lax.rem(self.mine + d, 4)
            total = self.parts[to, self.c] + self.core_recv[to]
            if d == 0:
                self.one_sum[...] = total
            else:
                self.one_send[d] = total.astype(BF16)
                copy = push(
                    self.one_send.at[d], self.one_recv.at[d], self.one_sems, d,
                    self.target(d, 0, 0),
                )
                self.one.append(self.start(copy))

    def own_rows(self, at):
        return self.wide[:, :, at] if self.on_x else self.wide[:, at]

    def second(self, weights):
        for copy in self.one:
            copy.wait_recv()
        total = self.one_sum[...]
        for d in (1, 2, 3):
            total = total + self.one_recv[d].astype(F32)
        high = total.astype(BF16)
        low = (total - high.astype(F32)).astype(BF16)
        product = matmul_nt(weights, high) + matmul_nt(weights, low)
        self.wide[...] = product.reshape(2, 4, 4, 2, 16, 128)
        self.two = []
        for d in (2, 1, 3):
            self.two_send[d] = self.own_rows(lax.rem(self.other + d, 4)).astype(BF16)
            copy = push(
                self.two_send.at[d], self.two_recv.at[d], self.two_sems, d, self.target(0, d, 0)
            )
            self.two.append(self.start(copy))

    def third(self):
        g, i, k = self.here
        for copy in self.two:
            copy.wait_recv()
        total = self.own_rows(self.other)
        for d in (1, 2, 3):
            total = total + self.two_recv[d].astype(F32)
        self.two_sum[...] = total
        self.three = self.start(
            push(self.two_sum.at[1 - g], self.three_recv, self.three_sems, 0, (1 - g, i, k))
        )

    def fourth(self):
        self.three.wait_recv()
        self.three_sum[...] = self.two_sum[self.here[0]] + self.three_recv[...]
        self.four = []
        for d, core in ((2, 0), (2, 1), (1, 0), (1, 1), (3, 0), (3, 1), (0, 1)):
            src = self.three_sum.at[lax.rem(self.mine + d, 4), lax.rem(self.c + core, 2)]
            copy = push(
                src, self.four_recv.at[self.mine, self.c], self.four_sems, 2 * d + core,
                self.target(d, 0, core),
            )
            self.four.append(self.start(copy))
        self.four_recv[self.mine, self.c] = self.three_sum[self.mine, self.c]

    def result(self, out):
        for copy in self.four:
            copy.wait_recv()
        for first in range(4):
            for core in range(2):
                at = 128 * (2 * first + core)
                out[:, at : at + 128] = self.four_recv[first, core]

    def finish(self):
        for chunk in range(4):
            self.core_copy(jnp.int32(chunk)).wait_send()
        for copy in self.copies:
            copy.wait_send()


N_SCATTER = 13
TRAINER_SCRATCH = [
    pltpu.VMEM((384, 1024), BF16),
    pltpu.VMEM((1024, 1024), BF16),
    pltpu.VMEM((1024, 1024), BF16),
    pltpu.VMEM((1024, 384), BF16),
    pltpu.VMEM((96, 384), BF16),
    pltpu.VMEM((4, 96, 384), BF16),
    pltpu.VMEM((4, 96, 384), BF16),
    pltpu.VMEM((288, 1024), BF16),
    pltpu.VMEM((96, 1024), F32),
    pltpu.VMEM((384, 1024), F32),
    pltpu.VMEM((384, 1024), BF16),
    pltpu.VMEM((384, 1024), BF16),
    pltpu.VMEM((96, 384), F32),
    pltpu.VMEM((4, 96, 384), BF16),
    pltpu.VMEM((4, 96, 384), BF16),
    pltpu.VMEM((384, 1024), BF16),
    pltpu.VMEM((384, 1024), BF16),
    pltpu.VMEM((384, 1024), BF16),
    pltpu.VMEM((96, 1024), F32),
    pltpu.VMEM((1024, 384), BF16),
    pltpu.VMEM((4, 8, 384), F32),
    pltpu.VMEM((4, 8, 384), F32),
    pltpu.SemaphoreType.DMA((6,)),
    pltpu.SemaphoreType.DMA((2, 4)),
    pltpu.SemaphoreType.DMA((2, 4)),
    pltpu.SemaphoreType.DMA((2, 4)),
    pltpu.SemaphoreType.DMA((2, 4)),
]
N_TRAINER = len(TRAINER_SCRATCH)
TRAINER_SCRATCH += Scatter.scratch(16, 384, BF16) * 2 + Product.scratch * 2


def columns(n):
    return pl.ds(pl.multiple_of(n * 256, 256), 256)


def step_kernel(
    velocity, viscosity, selection, w_in_far, w_up_far, w_down_far, w_out_far,
    velocity_next, pressure, out_up, out_down, out_small, lines, fold, *refs
):
    here = place()
    g, i, k = here
    n_stencil = len(Stencil.scratch)
    step = Stencil(here, velocity_next, pressure, refs[:n_stencil])
    refs = refs[n_stencil:]
    (
        w_in, w_up, w_down, w_out, targets, in_all, err_all, lifted_b, own_lift, slope, active, mixed,
        own_predicted, down_send, down_recv, back_raised, lift_b, back_b, own_back, w_in_t, tail_send, tail_recv,
        near_sems, in_sems, down_sems, err_sems, tail_sems,
    ) = refs[:N_TRAINER]
    refs = refs[N_TRAINER:]
    grad_in, grad_out = (
        Scatter(here, refs[n * N_SCATTER : (n + 1) * N_SCATTER], BF16) for n in range(2)
    )
    refs = refs[2 * N_SCATTER :]
    up, down = (
        Product(here, refs[: len(Product.scratch)], True),
        Product(here, refs[len(Product.scratch) :], False),
    )
    sent = []

    def peer(d):
        return (g, i, lax.rem(k + d, 4))

    def start(copies):
        for copy in copies:
            copy.start()
        sent.extend(copies)
        return copies

    met = stencil_targets(here) + trainer_targets(here)
    greet(met)
    near = [
        pltpu.make_async_copy(src, dst, near_sems.at[n])
        for n, (src, dst) in enumerate(
            (
                (velocity, step.fields.at[0:3]),
                (viscosity, step.fields.at[3]),
                (w_in_far, w_in),
                (w_up_far, w_up),
                (w_down_far, w_down),
                (w_out_far, w_out),
            )
        )
    ]
    for copy in near:
        copy.start()
    make_fold(fold)
    for copy in near[:2]:
        copy.wait()
    pick_patches(step.fields, selection, lines, fold, in_all.at[0])
    step.prepare()
    greeted(met)
    step.send_one()
    in_copies = start(
        [push(in_all.at[0], in_all.at[4 - d], in_sems, d, peer(d)) for d in (2, 1, 3)]
    )
    for copy in near[2:]:
        copy.wait()

    def forward(first, count):
        rows = in_all[first : first + count].reshape(96 * count, 384)
        at_rows = slice(96 * first, 96 * (first + count))

        def lift_in(n, carry):
            at = columns(n)
            lifted = matmul(rows, w_in[:, at])
            lifted_b[0 : 96 * count, at] = lifted.astype(BF16)
            if first == 0:
                own_lift[:, at] = lifted
            return carry

        def raise_(n, carry):
            at = columns(n)
            raised = matmul(lifted_b[0 : 96 * count, :], w_up[:, at])
            sigmoid = jax.nn.sigmoid(raised)
            active[at_rows, at] = (raised * sigmoid).astype(BF16)
            slope[at_rows, at] = sigmoid * (1.0 + raised * (1.0 - sigmoid))
            return carry

        def lower(n, carry):
            at = columns(n)
            part = matmul(active[at_rows, :], w_down[:, at])
            if first == 0:
                part = part + own_lift[:, at]
            mixed[at_rows, at] = part.astype(BF16)
            return carry

        lax.fori_loop(0, 4, lift_in, 0)
        for body in (raise_, lower):
            lax.fori_loop(0, 4, body, 0, unroll=True)
        return matmul(mixed[at_rows, :], w_out[...])

    own_predicted[...] = forward(0, 1)
    w_in_t[...] = w_in[...].T
    step.make_source()
    step.send_two()
    for copy in in_copies:
        copy.wait_recv()
    parts = forward(1, 3).astype(BF16)
    down_copies = []
    for d in (2, 1, 3):
        down_send[d] = parts[96 * (d - 1) : 96 * d]
        down_copies += start([push(down_send.at[d], down_recv.at[d], down_sems, d, peer(d))])
    step.solve()
    pick_patches(velocity_next, selection, lines, fold, targets)

    for copy in down_copies:
        copy.wait_recv()
    predicted = own_predicted[...]
    for d in (1, 2, 3):
        predicted = predicted + down_recv[d].astype(F32)
    scale = float(24576) ** (-0.5)
    err_all[0] = ((predicted - targets[...].astype(F32)) * scale).astype(BF16)
    err_copies = start(
        [push(err_all.at[0], err_all.at[4 - d], err_sems, d, peer(d)) for d in (2, 1, 3)]
    )
    for copy in err_copies:
        copy.wait_recv()
    rows_in = in_all[...].reshape(384, 384)
    errors = err_all[...].reshape(384, 384)

    def back(n, carry):
        at = columns(n)
        both = matmul_nt(errors, w_out[at, :])
        back_b[:, at] = both.astype(BF16)
        own_back[:, at] = both[0:96]
        return carry

    def back_up(n, carry):
        at = columns(n)
        steep = matmul_nt(back_b[...], w_down[at, :])
        back_raised[:, at] = (steep * slope[:, at]).astype(BF16)
        return carry

    def back_lift(n, carry):
        at = columns(n)
        part = matmul_nt(back_raised[...], w_up[at, :])
        lift_b[0:96, at] = (part[0:96] + own_back[:, at]).astype(BF16)
        lift_b[96:384, at] = part[96:384].astype(BF16)
        return carry

    lax.fori_loop(0, 4, back, 0)
    lax.fori_loop(0, 4, back_up, 0, unroll=True)
    up.fill(back_raised, rows_in)
    down.fill(active, errors)

    def grad_chunk(scatter, left, right):
        def chunk(n, carry):
            at = pl.ds(pl.multiple_of(n * 256, 256), 256)
            block = matmul_tn(left[:, at], right).reshape(2, 4, 2, 16, 384)
            for part in range(2):
                scatter.parts[lax.div(n, 2), lax.rem(n, 2) * 2 + part] = block[part]
                scatter.start_core(n * 2 + part)
            return carry

        lax.fori_loop(0, 4, chunk, 0)

    up.first()
    lax.fori_loop(0, 4, back_lift, 0)
    grad_chunk(grad_in, lift_b, rows_in)
    down.first()
    grad_chunk(grad_out, mixed, errors)
    scatters = (grad_in, grad_out)
    for scatter in scatters:
        scatter.first(0)
        scatter.first(1)
    up.second(w_in_t[...])
    down.second(w_out[...])
    for scatter in scatters:
        scatter.second(0)
        scatter.second(1)
    up.third()
    down.third()
    for scatter in scatters:
        scatter.third()
    up.fourth()
    down.fourth()
    last_in, last_out = grad_in.result(), grad_out.result()
    for j in range(4):
        tail_send[j, 0:4] = last_in[4 * j : 4 * j + 4]
        tail_send[j, 4:8] = last_out[4 * j : 4 * j + 4]
    tail_copies = start(
        [
            push(tail_send.at[lax.rem(k + d, 4)], tail_recv.at[d], tail_sems, d, peer(d))
            for d in (2, 1, 3)
        ]
    )
    up.result(out_up)
    down.result(out_down)
    for copy in tail_copies:
        copy.wait_recv()
    out_small[...] = tail_send[k] + tail_recv[1] + tail_recv[2] + tail_recv[3]
    for copy in sent:
        copy.wait_send()
    step.finish()
    for scatter in scatters + (up, down):
        scatter.finish()


def emit_kernel(
    near_next, near_pressure, near_up, near_down, near_small,
    velocity_next, pressure, grad_up, grad_down, first, second,
):
    velocity_next[...] = near_next[...]
    pressure[...] = near_pressure[...]
    grad_up[...] = near_up[...]
    grad_down[...] = near_down[...]
    first[...] = near_small[0:4]
    second[...] = near_small[4:8]


def on_device(velocity, viscosity, selection, w_in, w_up, w_down, w_out):
    shape = jax.ShapeDtypeStruct
    far, near = pl.BlockSpec(memory_space=pl.ANY), pl.BlockSpec(memory_space=pltpu.VMEM)
    velocity_next, pressure, grad_up, grad_down, small = pl.pallas_call(
        step_kernel,
        out_shape=[
            shape((3, 8, 32, 128), F32),
            shape((8, 32, 128), F32),
            shape((16, 1024), F32),
            shape((16, 1024), F32),
            shape((8, 384), F32),
        ],
        in_specs=[far, far, near, far, far, far, far],
        out_specs=[near] * 5,
        scratch_shapes=PATCH_SCRATCH + Stencil.scratch + TRAINER_SCRATCH,
        compiler_params=pltpu.CompilerParams(
            collective_id=0, has_side_effects=True, vmem_limit_bytes=56 * MIB
        ),
        name="step",
    )(velocity, viscosity, selection.reshape(1, 96), w_in, w_up, w_down, w_out)
    velocity_next, pressure, grad_up, grad_down, first, second = pl.pallas_call(
        emit_kernel,
        out_shape=[
            shape((3, 8, 32, 128), F32),
            shape((8, 32, 128), F32),
            shape((16, 1024), F32),
            shape((16, 1024), F32),
            shape((4, 384), F32),
            shape((4, 384), F32),
        ],
        in_specs=[near] * 5,
        out_specs=[near] * 6,
        compiler_params=pltpu.CompilerParams(vmem_limit_bytes=60 * MIB),
        name="emit",
    )(velocity_next, pressure, grad_up, grad_down, small)
    return (velocity_next, pressure, first.T, grad_up, grad_down.T, second)


def solution(mesh):
    placed = (
        P(None, "gx", "gy", "grp"),
        P("gx", "gy", "grp"),
        P("grp", "gx", "gy", None),
        P(),
        P(None, "gy"),
        P("gy", None),
        P(),
    )
    return jax.shard_map(
        on_device,
        mesh=mesh,
        in_specs=placed,
        out_specs=(
            P(None, "gx", "gy", "grp"),
            P("gx", "gy", "grp"),
            P(None, ("grp", "gx", "gy")),
            P(("grp", "gx"), "gy"),
            P("gy", ("grp", "gx")),
            P(("grp", "gx", "gy"), None),
        ),
        check_vma=False,
    )
```
